32 devices in a mesh: groups: 2 (over x), delta: 4 (over y, core), tensor: 4 (over z).
Axes of the slice: x: 2, y: 2, z: 4, core: 2. Of those that a mesh axis runs over, the one named last changes fastest.
Arguments:
- tokens: bfloat16 [1024, 8192], P('groups', 'delta'), parts along dimension 0, may hold values from -6 to 6
- gate_weight: bfloat16 [8192, 16384], P('delta', 'tensor'), may hold values from -0.0625 to 0.0625
- up_weight: bfloat16 [8192, 16384], P('delta', 'tensor'), may hold values from -0.0625 to 0.0625
- down_weight: bfloat16 [16384, 8192], P('tensor', 'delta'), may hold values from -0.046875 to 0.046875
- gate_tiles: bfloat16 [16, 8, 256, 256], P('delta', 'tensor'), may hold values from -0.375 to 0.375
- up_tiles: bfloat16 [16, 8, 256, 256], P('delta', 'tensor'), may hold values from -0.375 to 0.375
- down_tiles: bfloat16 [16, 8, 256, 256], P('delta', 'tensor'), may hold values from -0.375 to 0.375
- gate_pattern: int32 [16, 8], P('delta', 'tensor'), may hold values from 0 to 511, as said below
- up_pattern: int32 [16, 8], P('delta', 'tensor'), may hold values from 0 to 511, as said below
- down_pattern: int32 [16, 8], P('delta', 'tensor'), may hold values from 0 to 511, as said below
- row_variant: int32 [1024], P('groups'), parts along dimension 0, may hold values from 0 to 15, as said below
- variant_slot: int32 [32], P('groups'), parts along dimension 0, may hold values from 0 to 15, as said below
Outputs:
- mixed: bfloat16 [1024, 8192], P(('groups', 'tensor'), 'delta'), parts along dimension 0
The draws below stay inside these ranges and needn't reach their ends.
There are 2 independent parts, one for each index of `groups`. The reference program is written for one: setup_inputs(seed, part) draws one part's arguments, and reference() takes and returns one part's arrays. A program takes and returns all parts, laid end to end along the dimension named above; an argument that names none is the same for every part. Nothing has to cross between parts.
Inputs may be any that keep to these rules, and one draw needn't show every extreme that they name: `row_variant`: owner k of the delta axis holds the slots k * 4 to k * 4 + 3. The rows whose slot lies with one owner number at most 128; exactly 128 for one owner, which one varies from draw to draw; the other owners' counts differ by at most one. `variant_slot`: A permutation: every slot holds exactly one variant. `gate_pattern`: within one slot and one tensor shard the 2 positions differ; position p stands for row block p // c and column block p % c of that shard's [8192, 4096] grid of tiles. `up_pattern`: as gate_pattern. `down_pattern`: within one slot and one tensor shard the 2 positions differ; position p stands for row block p // e and column block p % e of that shard's [4096, 8192] grid of tiles.
All inputs are finite; a program needn't handle non-finite values.
Results may differ from the reference program's by a relative error of at most 0.005.
Values may be sent and summed in bfloat16 or wider, within the bound.
No kernel may reach another device: no remote copies, remote signals or barrier semaphores. Data moves between devices by JAX's collectives and lax.ppermute only.
A program may use at most 192 MiB of HBM per device.

```python
import jax
import jax.numpy as jnp
from jax import lax

D = 8192
FF = 16384
TILE = 256
KT = 2
VPO = 4
ROWS = 512
CAP = 128
SLOTS = 16
TILES_ALL = 8
GRID = 512
N_DELTA = 4
N_TENSOR = 4


def split_rows(key):
    slot_order = jax.random.permutation(jax.random.fold_in(key, 11), SLOTS).astype(jnp.int32)
    hottest = jax.random.randint(jax.random.fold_in(key, 12), (), 0, SLOTS // VPO)
    row_index = jnp.arange(ROWS, dtype=jnp.int32)
    remain = (row_index - CAP) % (SLOTS // VPO - 1)
    others = remain + (remain >= hottest).astype(jnp.int32)
    owner_of = jnp.where(row_index < CAP, hottest, others)
    shuffle = jax.random.permutation(jax.random.fold_in(key, 13), ROWS)
    owner_of = owner_of[shuffle]
    within = jax.random.randint(jax.random.fold_in(key, 14), (ROWS,), 0, VPO)
    inverse = jnp.argsort(slot_order)
    variants = inverse[owner_of * VPO + within]
    return (slot_order, variants.astype(jnp.int32))


def pick_tiles(key):
    scores = jax.random.randint(key, (SLOTS * TILES_ALL // KT, GRID), 0, 1 << 20) * GRID + jnp.arange(GRID, dtype=jnp.int32)[None, :]
    ranked = jnp.argsort(scores, axis=1)[:, :KT]
    return ranked.reshape(SLOTS, TILES_ALL).astype(jnp.int32)


def draw_variant_slot(key, part):
    slot_order, variants = split_rows(key)
    return slot_order


def draw_row_variant(key, part):
    slot_order, variants = split_rows(key)
    return variants


def draw_gate_pattern(key, part):
    key = jax.random.fold_in(key, 3)
    return pick_tiles(key)


def draw_up_pattern(key, part):
    key = jax.random.fold_in(key, 5)
    return pick_tiles(key)


def draw_down_pattern(key, part):
    key = jax.random.fold_in(key, 7)
    return pick_tiles(key)


def level_of(stream_key, extent, shards, low, top_value):
    def one(axis_at, parts):
        heights = jax.random.uniform(jax.random.fold_in(jax.random.fold_in(stream_key, 6), axis_at), (parts,), jnp.float32, low / len(shards), top_value / len(shards))
        return jnp.repeat(jnp.exp(heights), extent[axis_at] // parts).reshape((-1,) + (1,) * (len(extent) - axis_at - 1))

    gain = one(*shards[0])
    for cut in shards[1:]:
        gain = gain * one(*cut)
    return gain


def normal_values(own_key, extent, spread, most, shards=(), kind=jnp.bfloat16):
    entries = spread * jax.random.normal(own_key, extent, jnp.float32)
    if shards:
        entries = entries * level_of(own_key, extent, shards, -0.22, 0.18)
    return jnp.clip(entries, -most, most).astype(kind)


def setup_inputs(seed: int = 0, part: int = 0) -> dict:
    arg_keys = jax.random.split(jax.random.key(seed), 13)
    part_keys = jax.random.split(jax.random.fold_in(arg_keys[12], part), 13)
    tokens = normal_values(part_keys[0], (ROWS, D), 1.0, 6.0, ((1, 4),))
    gate_weight = normal_values(arg_keys[1], (D, FF), D ** -0.5, 0.0625, ((0, 4), (1, 4)))
    up_weight = normal_values(arg_keys[2], (D, FF), D ** -0.5, 0.0625, ((0, 4), (1, 4)))
    down_weight = normal_values(arg_keys[3], (FF, D), FF ** -0.5, 0.046875, ((0, 4), (1, 4)))
    gate_tiles = normal_values(arg_keys[4], (SLOTS, TILES_ALL, TILE, TILE), TILE ** -0.5, 0.375, ((0, 4), (1, 4)))
    up_tiles = normal_values(arg_keys[5], (SLOTS, TILES_ALL, TILE, TILE), TILE ** -0.5, 0.375, ((0, 4), (1, 4)))
    down_tiles = normal_values(arg_keys[6], (SLOTS, TILES_ALL, TILE, TILE), TILE ** -0.5, 0.375, ((0, 4), (1, 4)))
    gate_pattern = draw_gate_pattern(jax.random.fold_in(arg_keys[12], 71), part)
    up_pattern = draw_up_pattern(jax.random.fold_in(arg_keys[12], 71), part)
    down_pattern = draw_down_pattern(jax.random.fold_in(arg_keys[12], 71), part)
    row_variant = draw_row_variant(jax.random.fold_in(jax.random.fold_in(arg_keys[12], part), 71), part)
    variant_slot = draw_variant_slot(jax.random.fold_in(jax.random.fold_in(arg_keys[12], part), 71), part)
    return dict(tokens=tokens, gate_weight=gate_weight, up_weight=up_weight, down_weight=down_weight, gate_tiles=gate_tiles, up_tiles=up_tiles, down_tiles=down_tiles, gate_pattern=gate_pattern, up_pattern=up_pattern, down_pattern=down_pattern, row_variant=row_variant, variant_slot=variant_slot)


def tile_delta(source, tile_set, pattern, row_slot, gate_like):
    column_tiles = FF // N_TENSOR // TILE
    width_tiles = D // TILE
    shard_of = (jnp.arange(TILES_ALL, dtype=jnp.int32) // KT)[None, :]
    if gate_like:
        in_global = pattern // column_tiles
        out_global = shard_of * column_tiles + pattern % column_tiles
        out_count = FF // TILE
    else:
        in_global = shard_of * column_tiles + pattern // width_tiles
        out_global = pattern % width_tiles
        out_count = width_tiles
    block_rows = ROWS // N_DELTA
    blocks = source.reshape(N_DELTA, block_rows, -1, TILE)
    slot_blocks = row_slot.reshape(N_DELTA, block_rows)
    targets = jnp.arange(out_count, dtype=jnp.int32)

    def one_block(block_item):
        rows_in, slots_in = block_item
        inward = in_global[slots_in]
        outward = out_global[slots_in]
        picked = jnp.take_along_axis(rows_in, inward[:, :, None], axis=1).astype(jnp.float32)
        chosen = tile_set[slots_in].astype(jnp.float32)
        products = jnp.einsum("bjk,bjkf->bjf", picked, chosen, precision=lax.Precision.HIGHEST)
        placing = (outward[:, :, None] == targets[None, None, :]).astype(jnp.float32)
        placed = jnp.einsum("bjf,bjg->bgf", products, placing, precision=lax.Precision.HIGHEST)
        return placed.reshape(block_rows, out_count * TILE)

    return lax.map(one_block, (blocks, slot_blocks)).reshape(ROWS, out_count * TILE)


def reference(tokens, gate_weight, up_weight, down_weight, gate_tiles, up_tiles, down_tiles, gate_pattern, up_pattern, down_pattern, row_variant, variant_slot):
    row_slot = variant_slot[row_variant]
    gate = jnp.dot(tokens, gate_weight, preferred_element_type=jnp.float32) + tile_delta(tokens, gate_tiles, gate_pattern, row_slot, True)
    upward = jnp.dot(tokens, up_weight, preferred_element_type=jnp.float32) + tile_delta(tokens, up_tiles, up_pattern, row_slot, True)
    hidden = (jax.nn.silu(gate) * upward).astype(jnp.bfloat16)
    mixed = jnp.dot(hidden, down_weight, preferred_element_type=jnp.float32) + tile_delta(hidden, down_tiles, down_pattern, row_slot, False)
    return mixed.astype(jnp.bfloat16)
```

```python
import functools

import jax
import jax.numpy as jnp
from jax import lax
from jax.experimental import pallas as pl
from jax.experimental.pallas import tpu as pltpu
from jax.sharding import PartitionSpec as P

CAP = 128
CHUNKS = (1, 1, 1, 1)
VMEM = 56 * 1024 * 1024
BF = jnp.bfloat16
F32 = jnp.float32


def cost(flops, moved):
    return pl.CostEstimate(flops=int(flops), bytes_accessed=int(moved), transcendentals=0)


def whole(shape):
    zeros = (0,) * len(shape)
    return pl.BlockSpec(shape, lambda *_: zeros)


def ranks(slot_lane, slot_sub, row_lane, row_sub, per_owner):
    same = (slot_sub // per_owner) == (slot_lane // per_owner)
    ahead = same & (row_sub < row_lane)
    return jnp.sum(ahead.astype(jnp.int32), axis=0, keepdims=True)


def pack_body(owners, per_owner, kinds, col_tiles, capacity, scal, x, sl, ss, rl, rs, out):
    tile = 256
    here = x.shape[1] // tile
    me = scal[0]
    pos = ranks(sl[...], ss[...], rl[...], rs[...], per_owner)
    rows = x.shape[0]
    place = lax.broadcasted_iota(jnp.int32, (capacity, rows), 0) == pos
    out[...] = jnp.zeros_like(out)

    def step(i, carry):
        at = i // per_owner
        local = i % per_owner
        owner = scal[1 + at]
        slot = owner * per_owner + local
        hot = jnp.where(place & (sl[...] == slot), 1.0, 0.0).astype(BF)
        top = pl.multiple_of(at * capacity, capacity)
        for j in range(kinds):
            block = scal[1 + owners + slot * kinds + j] // col_tiles

            @pl.when(block // here == me)
            def _():
                col = pl.multiple_of((block % here) * tile, tile)
                got = jnp.dot(hot, x[:, pl.ds(col, tile)], preferred_element_type=F32)
                view = (pl.ds(top, capacity), pl.ds(j * tile, tile))
                out[view] = out[view] + got.astype(BF)

        return carry

    lax.fori_loop(0, owners * per_owner, step, 0)


def pack(scal, xs, sl, ss, rl, rs, owners, per_owner, kinds, col_tiles):
    rows = xs.shape[0]
    width = kinds * 256
    return pl.pallas_call(
        functools.partial(pack_body, owners, per_owner, kinds, col_tiles, CAP),
        grid_spec=pltpu.PrefetchScalarGridSpec(
            num_scalar_prefetch=1,
            grid=(1,),
            in_specs=[whole(xs.shape), whole((1, rows)), whole((rows, 1)), whole((1, rows)), whole((rows, 1))],
            out_specs=whole((owners * CAP, width)),
        ),
        out_shape=jax.ShapeDtypeStruct((owners * CAP, width), BF),
        compiler_params=pltpu.CompilerParams(vmem_limit_bytes=VMEM),
        cost_estimate=cost(2e9, 4e6),
    )(scal, xs, sl, ss, rl, rs)


def product_body(owners, per_owner, per_slot, pieces, scal, x, gt, ut, sl, ss, rl, rs, out):
    tile = 256
    me = scal[0]
    capacity = x.shape[0]
    rows = sl.shape[1]
    pos = ranks(sl[...], ss[...], rl[...], rs[...], per_owner)
    place = lax.broadcasted_iota(jnp.int32, (capacity, rows), 0) == pos
    mine = place & ((sl[...] // per_owner) == me)
    slot = jnp.sum(jnp.where(mine, sl[...] % per_owner + 1, 0), axis=1, keepdims=True) - 1
    hot = jnp.where(mine, 1.0, 0.0).astype(BF)
    for kind, tiles in enumerate((gt, ut)):
        for j in range(per_slot):
            at = (kind * per_slot + j) * tile
            source = x[:, at : at + tile]
            total = jnp.zeros((capacity, tile), F32)
            for s in range(per_owner):
                picked = jnp.where(slot == s, source, jnp.zeros_like(source))
                total = total + jnp.dot(picked, tiles[s, j], preferred_element_type=F32)
            spread = lax.dot_general(
                hot, total.astype(BF), (((0,), (0,)), ((), ())), preferred_element_type=F32
            ).astype(BF)
            for home, offset, size, start in pieces:
                out[home, offset : offset + size, at : at + tile] = spread[start : start + size]


def product(scal, x, gt, ut, sl, ss, rl, rs, owners, per_owner, pieces):
    rows = sl.shape[1]
    per_slot = gt.shape[1]
    shape = (owners, rows // owners, x.shape[1])
    return pl.pallas_call(
        functools.partial(product_body, owners, per_owner, per_slot, pieces),
        grid_spec=pltpu.PrefetchScalarGridSpec(
            num_scalar_prefetch=1,
            grid=(1,),
            in_specs=[
                whole(x.shape),
                whole(gt.shape),
                whole(ut.shape),
                whole((1, rows)),
                whole((rows, 1)),
                whole((1, rows)),
                whole((rows, 1)),
            ],
            out_specs=whole(shape),
        ),
        out_shape=jax.ShapeDtypeStruct(shape, BF),
        compiler_params=pltpu.CompilerParams(vmem_limit_bytes=VMEM),
        cost_estimate=cost(1e9, 4e6),
    )(scal, x, gt, ut, sl, ss, rl, rs)


def gate_up_body(x, wg, wu, send, keep):
    half = send.shape[1]
    for i, w in enumerate((wg, wu)):
        total = jnp.dot(x[...], w[...], preferred_element_type=F32)
        send[i] = total[:half].astype(send.dtype)
        keep[i] = total[half:]


def gate_up(x, wg, wu):
    rows, depth = x.shape
    width = wg.shape[1]
    block = min(1024, width)
    outs = pl.BlockSpec((2, rows // 2, block), lambda i: (0, 0, i))
    weights = pl.BlockSpec((depth, block), lambda i: (0, i))
    return pl.pallas_call(
        gate_up_body,
        grid=(width // block,),
        in_specs=[whole(x.shape), weights, weights],
        out_specs=[outs, outs],
        out_shape=[jax.ShapeDtypeStruct((2, rows // 2, width), F32)] * 2,
        compiler_params=pltpu.CompilerParams(vmem_limit_bytes=VMEM),
        cost_estimate=cost(4 * rows * depth * width, 4 * depth * width),
    )(x, wg, wu)


def activate_body(per_slot, slots, col_tiles, first, scal, mine, got, delta, slot, out):
    tile = 256
    rows = out.shape[0]
    where = []
    for j in range(2 * per_slot):

        def look(s, held):
            return jnp.where(slot[...] == s, scal[first + s * 2 * per_slot + j] % col_tiles, held)

        where.append(lax.fori_loop(0, slots, look, jnp.zeros((rows, 1), jnp.int32)))
    for b in range(col_tiles):
        cols = slice(b * tile, (b + 1) * tile)
        sums = []
        for kind in range(2):
            total = mine[kind, :, cols] + got[kind, :, cols].astype(F32)
            for j in range(per_slot):
                k = kind * per_slot + j
                add = delta[:, k * tile : (k + 1) * tile].astype(F32)
                total = total + jnp.where(where[k] == b, add, 0.0)
            sums.append(total)
        gate, up = sums
        out[:, cols] = (gate / (1.0 + jnp.exp(-gate)) * up).astype(BF)


def activate(scal, mine, got, delta, slot, per_slot, slots, col_tiles, first):
    rows, width = mine.shape[1:]
    return pl.pallas_call(
        functools.partial(activate_body, per_slot, slots, col_tiles, first),
        grid_spec=pltpu.PrefetchScalarGridSpec(
            num_scalar_prefetch=1,
            grid=(1,),
            in_specs=[whole(mine.shape), whole(got.shape), whole(delta.shape), whole((rows, 1))],
            out_specs=whole((rows, width)),
        ),
        out_shape=jax.ShapeDtypeStruct((rows, width), BF),
        compiler_params=pltpu.CompilerParams(vmem_limit_bytes=VMEM),
        cost_estimate=cost(20 * rows * width, 14 * rows * width),
    )(scal, mine, got, delta, slot)


def down_body(width_tiles, here, count, scal, hid, w, tiles, slot, out):
    tile = 256
    me = scal[0]
    across = out.shape[1] // tile
    step = pl.program_id(0)
    out[...] = jnp.dot(hid[...], w[...], preferred_element_type=F32)

    def one(i, carry):
        place = scal[1 + count + i]
        block = place % width_tiles - me * here - step * across

        @pl.when((block >= 0) & (block < across))
        def _():
            source = hid[:, pl.ds(pl.multiple_of((place // width_tiles) * tile, tile), tile)]
            picked = jnp.where(slot[...] == scal[1 + i], source, jnp.zeros_like(source))
            add = jnp.dot(picked, tiles[i], preferred_element_type=F32)
            cols = pl.ds(pl.multiple_of(block * tile, tile), tile)
            out[:, cols] = out[:, cols] + add

        return carry

    lax.fori_loop(0, count, one, 0)


def down(scal, hid, w, tiles, slot, width_tiles):
    rows, depth = hid.shape
    width = w.shape[1]
    block = min(512, width)
    count = tiles.shape[0]
    return pl.pallas_call(
        functools.partial(down_body, width_tiles, width // 256, count),
        grid_spec=pltpu.PrefetchScalarGridSpec(
            num_scalar_prefetch=1,
            grid=(width // block,),
            in_specs=[
                whole(hid.shape),
                pl.BlockSpec((depth, block), lambda i, s: (0, i)),
                whole(tiles.shape),
                whole((rows, 1)),
            ],
            out_specs=pl.BlockSpec((rows, block), lambda i, s: (0, i)),
        ),
        out_shape=jax.ShapeDtypeStruct((rows, width), F32),
        compiler_params=pltpu.CompilerParams(vmem_limit_bytes=VMEM),
        cost_estimate=cost(2 * rows * depth * width, 2 * depth * width),
    )(scal, hid, w, tiles, slot)


def shards(
    tokens,
    gate_weight,
    up_weight,
    down_weight,
    gate_tiles,
    up_tiles,
    down_tiles,
    gate_pattern,
    up_pattern,
    down_pattern,
    row_variant,
    variant_slot,
):
    owners = lax.axis_size("delta")
    shift = lax.axis_size("tensor")
    groups = lax.axis_size("groups")
    me = lax.axis_index("delta")
    here_t = lax.axis_index("tensor")
    my_core, my_y = me % 2, me // 2
    ys = owners // 2
    per_owner, per_slot = gate_pattern.shape
    slots = owners * per_owner
    rows, shard_width = tokens.shape
    width = gate_weight.shape[1]
    col_tiles = width // 256
    width_tiles = shard_width * owners // 256
    unit = rows // sum(CHUNKS)
    sizes = [unit * c for c in CHUNKS]

    def core_swap(x):
        return lax.ppermute(x, "delta", [(i, i ^ 1) for i in range(owners)])

    def y_move(x, k):
        return lax.ppermute(x, "delta", [(i, (i + 2 * k) % owners) for i in range(owners)])

    order_y = [(my_y + k) % ys for k in range(1, ys)] + [my_y]
    homes = jnp.stack([y * 2 + c for c in (1 - my_core, my_core) for y in order_y]).astype(jnp.int32)

    def reduce_homes(x, axis):
        half = owners // 2
        kept = x[half:] + core_swap(x[:half])
        total = kept[ys - 1]
        for k in range(1, ys):
            total = total + y_move(kept[k - 1], k)
        return total

    row_ids = []
    offset = 0
    for size in sizes:
        each = size // (owners * shift)
        ids = (
            jnp.arange(shift, dtype=jnp.int32)[None, :, None] * (rows // shift)
            + offset
            + homes[:, None, None] * each
            + jnp.arange(each, dtype=jnp.int32)[None, None, :]
        )
        row_ids.append(ids.reshape(-1))
        offset += owners * each
    row_of = jnp.concatenate(row_ids)

    hit = row_variant[:, None] == jnp.arange(variant_slot.shape[0], dtype=jnp.int32)[None, :]
    slot_rows = jnp.sum(jnp.where(hit, variant_slot[None, :], 0), axis=1)
    slot_q = jnp.sum(
        jnp.where(row_of[:, None] == jnp.arange(rows, dtype=jnp.int32)[None, :], slot_rows[None, :], 0), axis=1
    )
    sl, ss = slot_q[None, :], slot_q[:, None]
    rl, rs = row_of[None, :], row_of[:, None]

    own = jnp.concatenate([gate_pattern, up_pattern, down_pattern], axis=1)
    seen = jnp.stack([own] + [lax.ppermute(own, "delta", [(i, (i - k) % owners) for i in range(owners)]) for k in range(1, owners)])
    back = (jnp.arange(owners, dtype=jnp.int32) - me) % owners
    by_owner = jnp.sum(
        jnp.where(
            (back[:, None] == jnp.arange(owners, dtype=jnp.int32)[None, :])[:, :, None, None], seen[None], 0
        ),
        axis=1,
    ).reshape(slots, 3 * per_slot)
    kinds = 2 * per_slot
    in_places = by_owner[:, :kinds].reshape(-1)
    scal = jnp.concatenate([me.astype(jnp.int32)[None], homes, in_places])

    if groups == 2 and per_owner % 2 == 0:
        part = per_owner // 2
        mine_g = lax.axis_index("groups")
        piece = lax.dynamic_slice_in_dim(down_tiles, mine_g * part, part, 0)
        gathered = jnp.stack([y_move(piece, -k) for k in range(1, ys)] + [piece])
        other = lax.ppermute(gathered, "groups", [(0, 1), (1, 0)])
        both = jnp.stack([gathered, other])
        starts = [mine_g * part, (1 - mine_g) * part]
    else:
        part = per_owner
        both = jnp.stack([y_move(down_tiles, -k) for k in range(1, ys)] + [down_tiles])[None]
        starts = [0]
    all_tiles = jnp.stack([core_swap(both), both]).reshape(-1, 256, 256)
    tile_slots = jnp.stack(
        [
            (y * 2 + c) * per_owner + start + s
            for c in (1 - my_core, my_core)
            for start in starts
            for y in order_y
            for s in range(part)
        ]
    ).astype(jnp.int32)
    picked = tile_slots[:, None] == jnp.arange(slots, dtype=jnp.int32)[None, :]
    places = jnp.sum(jnp.where(picked[:, :, None], by_owner[None, :, kinds:], 0), axis=1).reshape(-1)
    down_scal = jnp.concatenate([me.astype(jnp.int32)[None], jnp.repeat(tile_slots, per_slot), places])

    xs = jnp.take(tokens, row_of, axis=0)

    packed = pack(scal, xs, sl, ss, rl, rs, owners, per_owner, kinds, col_tiles)
    features = reduce_homes(packed.reshape(owners, CAP, -1), 0)
    pieces = []
    start, inner = 0, 0
    for size in sizes:
        each = size // owners
        for home in range(owners):
            pieces.append((home, inner, each, start + home * each))
        start += size
        inner += each
    spread = product(scal, features, gate_tiles, up_tiles, sl, ss, rl, rs, owners, per_owner, tuple(pieces))
    home_delta = reduce_homes(spread, 0)

    result = []
    start, inner = 0, 0
    for size in sizes:
        each = size // owners
        x = xs[start : start + size]
        send, keep = gate_up(x, gate_weight, up_weight)
        summed = keep + core_swap(send)
        mine = summed[:, (ys - 1) * each :]
        got = None
        for k in range(1, ys):
            moved = y_move(summed[:, (k - 1) * each : k * each].astype(BF), k)
            if got is None:
                got = moved
            else:
                mine = mine + moved.astype(F32)
        slot_home = ss[start + size - each : start + size]
        hid = activate(
            scal, mine, got, home_delta[inner : inner + each], slot_home, per_slot, slots, col_tiles, 1 + owners
        )
        chip = jnp.concatenate([y_move(hid, -k) for k in range(1, ys)] + [hid])
        full = jnp.concatenate([core_swap(chip), chip])
        out = down(down_scal, full, down_weight, all_tiles, ss[start : start + size], width_tiles)
        blocks = out.reshape(owners, shift, size // (owners * shift), shard_width).transpose(1, 0, 2, 3)
        total = lax.dynamic_index_in_dim(blocks, here_t, 0, keepdims=False)
        for k in range(1, shift):
            gone = lax.dynamic_index_in_dim(blocks, (here_t + k) % shift, 0, keepdims=False).astype(BF)
            total = total + lax.ppermute(
                gone, "tensor", [(i, (i + k) % shift) for i in range(shift)]
            ).astype(F32)
        result.append(total.astype(BF))
        start += size
        inner += each

    at = jnp.stack([((d // 2) - my_y - 1) % ys + ys * jnp.where(d % 2 == my_core, 1, 0) for d in range(owners)])
    placed = [jnp.take(r, at, axis=0).reshape(-1, shard_width) for r in result]
    return jnp.concatenate(placed, axis=0)


def solution(mesh):
    return jax.shard_map(
        shards,
        mesh=mesh,
        in_specs=(
            P("groups", "delta"),
            P("delta", "tensor"),
            P("delta", "tensor"),
            P("tensor", "delta"),
            P("delta", "tensor", None, None),
            P("delta", "tensor", None, None),
            P("delta", "tensor", None, None),
            P("delta", "tensor"),
            P("delta", "tensor"),
            P("delta", "tensor"),
            P("groups"),
            P("groups"),
        ),
        out_specs=P(("groups", "tensor"), "delta"),
        check_vma=False,
    )
```

```python
import functools

import jax
import jax.numpy as jnp
from jax import lax
from jax.experimental import pallas as pl
from jax.experimental.pallas import tpu as pltpu
from jax.sharding import PartitionSpec as P

CAP = 128
CHUNKS = (1, 2, 1)
VMEM = 56 * 1024 * 1024
BF = jnp.bfloat16
F32 = jnp.float32


def cost(flops, moved):
    return pl.CostEstimate(flops=int(flops), bytes_accessed=int(moved), transcendentals=0)


def whole(shape):
    zeros = (0,) * len(shape)
    return pl.BlockSpec(shape, lambda *_: zeros)


def pack_body(owners, per_owner, kinds, capacity, scal, x, sl, ss, table, out, code):
    tile = 256
    rows, held = x.shape
    here = held // tile
    owner_l = sl[...] // per_owner
    first = lax.broadcasted_iota(jnp.int32, (rows, rows), 0)
    second = lax.broadcasted_iota(jnp.int32, (rows, rows), 1)
    ahead = ((ss[...] // per_owner) == owner_l) & (first < second)
    pos = jnp.sum(jnp.where(ahead, 1, 0), axis=0, keepdims=True)
    code[...] = sl[...] * capacity + pos
    target = pos
    for o in range(owners):
        target = target + jnp.where(owner_l == o, scal[1 + o] * capacity, 0)
    hot = lax.broadcasted_iota(jnp.int32, (owners * capacity, rows), 0) == target
    hot = jnp.where(hot, 1.0, 0.0).astype(BF)
    lanes = lax.broadcasted_iota(jnp.int32, (rows, table.shape[0]), 1)
    slot_hot = jnp.where(ss[...] == lanes, 1.0, 0.0).astype(BF)
    block = jnp.dot(slot_hot, table[...], preferred_element_type=F32)
    block = block - (scal[0] * here).astype(F32)
    for j in range(kinds):
        at = block[:, j : j + 1]
        picked = jnp.zeros((rows, tile), BF)
        for b in range(here):
            picked = jnp.where(at == float(b), x[:, b * tile : (b + 1) * tile], picked)
        out[:, j * tile : (j + 1) * tile] = jnp.dot(hot, picked, preferred_element_type=F32).astype(BF)


def pack(scal, x, sl, ss, table, owners, per_owner, kinds):
    rows = x.shape[0]
    width = kinds * 256
    return pl.pallas_call(
        functools.partial(pack_body, owners, per_owner, kinds, CAP),
        grid_spec=pltpu.PrefetchScalarGridSpec(
            num_scalar_prefetch=1,
            grid=(1,),
            in_specs=[whole(x.shape), whole((1, rows)), whole((rows, 1)), whole(table.shape)],
            out_specs=[whole((owners * CAP, width)), whole((1, rows))],
        ),
        out_shape=[
            jax.ShapeDtypeStruct((owners * CAP, width), BF),
            jax.ShapeDtypeStruct((1, rows), jnp.int32),
        ],
        compiler_params=pltpu.CompilerParams(vmem_limit_bytes=VMEM),
        cost_estimate=cost(4e9, 4e6),
    )(scal, x, sl, ss, table)


def product_body(owners, per_owner, per_slot, pieces, scal, x, gt, ut, code, out):
    tile = 256
    capacity = x.shape[0]
    rows = code.shape[1]
    slot_l = code[...] // capacity
    place = lax.broadcasted_iota(jnp.int32, (capacity, rows), 0) == code[...] % capacity
    mine = place & (slot_l // per_owner == scal[0])
    slot = jnp.sum(jnp.where(mine, slot_l % per_owner + 1, 0), axis=1, keepdims=True) - 1
    hot = jnp.where(mine, 1.0, 0.0).astype(BF)
    for kind, tiles in enumerate((gt, ut)):
        for j in range(per_slot):
            at = (kind * per_slot + j) * tile
            source = x[:, at : at + tile]
            total = jnp.zeros((capacity, tile), F32)
            for s in range(per_owner):
                picked = jnp.where(slot == s, source, jnp.zeros_like(source))
                total = total + jnp.dot(picked, tiles[s, j], preferred_element_type=F32)
            spread = lax.dot_general(
                hot, total.astype(BF), (((0,), (0,)), ((), ())), preferred_element_type=F32
            ).astype(BF)
            for home, offset, size, start in pieces:
                out[home, offset : offset + size, at : at + tile] = spread[start : start + size]


def product(scal, x, gt, ut, code, owners, per_owner, pieces):
    rows = code.shape[1]
    per_slot = gt.shape[1]
    shape = (owners, rows // owners, x.shape[1])
    return pl.pallas_call(
        functools.partial(product_body, owners, per_owner, per_slot, pieces),
        grid_spec=pltpu.PrefetchScalarGridSpec(
            num_scalar_prefetch=1,
            grid=(1,),
            in_specs=[whole(x.shape), whole(gt.shape), whole(ut.shape), whole((1, rows))],
            out_specs=whole(shape),
        ),
        out_shape=jax.ShapeDtypeStruct(shape, BF),
        compiler_params=pltpu.CompilerParams(vmem_limit_bytes=VMEM),
        cost_estimate=cost(4e9, 4e6),
    )(scal, x, gt, ut, code)


def gate_up_body(x, wg, wu, send, keep):
    half = send.shape[1]
    for i, w in enumerate((wg, wu)):
        total = jnp.dot(x[...], w[...], preferred_element_type=F32)
        send[i] = total[:half].astype(send.dtype)
        keep[i] = total[half:]


def gate_up(x, wg, wu):
    rows, depth = x.shape
    width = wg.shape[1]
    block = min(1024, width)
    outs = pl.BlockSpec((2, rows // 2, block), lambda i: (0, 0, i))
    weights = pl.BlockSpec((depth, block), lambda i: (0, i))
    return pl.pallas_call(
        gate_up_body,
        grid=(width // block,),
        in_specs=[whole(x.shape), weights, weights],
        out_specs=[outs, outs],
        out_shape=[jax.ShapeDtypeStruct((2, rows // 2, width), F32)] * 2,
        compiler_params=pltpu.CompilerParams(vmem_limit_bytes=VMEM),
        cost_estimate=cost(4 * rows * depth * width, 4 * depth * width),
    )(x, wg, wu)


def activate_body(per_slot, start, each, keep, core, got, delta, where, out):
    tile = 256
    step = pl.program_id(0)
    across = out.shape[1] // tile
    at = [where[start : start + each, k : k + 1] - step * across for k in range(2 * per_slot)]
    adds = [
        delta[start : start + each, k * tile : (k + 1) * tile].astype(F32) for k in range(2 * per_slot)
    ]
    for b in range(across):
        cols = slice(b * tile, (b + 1) * tile)
        sums = []
        for kind in range(2):
            total = keep[kind, :, cols] + core[kind, :, cols] + got[kind, :, cols].astype(F32)
            for k in range(kind * per_slot, (kind + 1) * per_slot):
                total = total + jnp.where(at[k] == b, adds[k], 0.0)
            sums.append(total)
        gate, up = sums
        out[:, cols] = (gate / (1.0 + jnp.exp(-gate)) * up).astype(BF)


def activate(keep, core, got, delta, where, per_slot, start):
    each, width = got.shape[1:]
    last = keep.shape[1] // each - 1
    block = min(1024, width)
    own = pl.BlockSpec((2, each, block), lambda i: (0, last, i))
    return pl.pallas_call(
        functools.partial(activate_body, per_slot, start, each),
        grid=(width // block,),
        in_specs=[
            own,
            own,
            pl.BlockSpec((2, each, block), lambda i: (0, 0, i)),
            whole(delta.shape),
            whole(where.shape),
        ],
        out_specs=pl.BlockSpec((each, block), lambda i: (0, i)),
        out_shape=jax.ShapeDtypeStruct((each, width), BF),
        compiler_params=pltpu.CompilerParams(vmem_limit_bytes=VMEM),
        cost_estimate=cost(20 * each * width, 24 * each * width),
    )(keep, core, got, delta, where)


def down_body(width_tiles, here, count, start, scal, far, near, w, tiles, slot, out, hid):
    tile = 256
    me = scal[0]
    across = out.shape[1] // tile
    step = pl.program_id(0)
    half = far.shape[0]

    @pl.when(step == 0)
    def _():
        hid[:half] = far[...]
        hid[half:] = near[...]

    out[...] = jnp.dot(hid[...], w[...], preferred_element_type=F32)

    def one(i, carry):
        place = scal[1 + count + i]
        block = place % width_tiles - me * here - step * across

        @pl.when((block >= 0) & (block < across))
        def _():
            source = hid[:, pl.ds(pl.multiple_of((place // width_tiles) * tile, tile), tile)]
            hit = slot[start : start + 2 * half] == scal[1 + i]
            picked = jnp.where(hit, source, jnp.zeros_like(source))
            add = jnp.dot(picked, tiles[i], preferred_element_type=F32)
            cols = pl.ds(pl.multiple_of(block * tile, tile), tile)
            out[:, cols] = out[:, cols] + add

        return carry

    lax.fori_loop(0, count, one, 0)


def down(scal, far, near, w, tiles, slot, width_tiles, start):
    rows, depth = 2 * far.shape[0], far.shape[1]
    width = w.shape[1]
    block = min(512, width)
    count = tiles.shape[0]
    return pl.pallas_call(
        functools.partial(down_body, width_tiles, width // 256, count, start),
        grid_spec=pltpu.PrefetchScalarGridSpec(
            num_scalar_prefetch=1,
            grid=(width // block,),
            in_specs=[
                whole(far.shape),
                whole(near.shape),
                pl.BlockSpec((depth, block), lambda i, s: (0, i)),
                whole(tiles.shape),
                whole(slot.shape),
            ],
            out_specs=pl.BlockSpec((rows, block), lambda i, s: (0, i)),
            scratch_shapes=[pltpu.VMEM((rows, depth), BF)],
        ),
        out_shape=jax.ShapeDtypeStruct((rows, width), F32),
        compiler_params=pltpu.CompilerParams(vmem_limit_bytes=VMEM),
        cost_estimate=cost(3 * rows * depth * width, 3 * depth * width),
    )(scal, far, near, w, tiles, slot)


def shards(
    tokens,
    gate_weight,
    up_weight,
    down_weight,
    gate_tiles,
    up_tiles,
    down_tiles,
    gate_pattern,
    up_pattern,
    down_pattern,
    row_variant,
    variant_slot,
):
    owners = lax.axis_size("delta")
    shift = lax.axis_size("tensor")
    groups = lax.axis_size("groups")
    me = lax.axis_index("delta")
    here_t = lax.axis_index("tensor")
    my_core, my_y = me % 2, me // 2
    ys = owners // 2
    per_owner, per_slot = gate_pattern.shape
    slots = owners * per_owner
    rows, shard_width = tokens.shape
    width = gate_weight.shape[1]
    col_tiles = width // 256
    width_tiles = shard_width * owners // 256
    unit = rows // sum(CHUNKS)
    sizes = [unit * c for c in CHUNKS]

    def core_swap(x):
        return lax.ppermute(x, "delta", [(i, i ^ 1) for i in range(owners)])

    def y_move(x, k):
        return lax.ppermute(x, "delta", [(i, (i + 2 * k) % owners) for i in range(owners)])

    order_y = [(my_y + k) % ys for k in range(1, ys)] + [my_y]
    homes = jnp.stack([y * 2 + c for c in (1 - my_core, my_core) for y in order_y]).astype(jnp.int32)

    def reduce_homes(x, axis):
        half = owners // 2
        kept = x[half:] + core_swap(x[:half])
        total = kept[ys - 1]
        for k in range(1, ys):
            total = total + y_move(kept[k - 1], k)
        return total

    row_ids = []
    offset = 0
    for size in sizes:
        each = size // (owners * shift)
        ids = (
            jnp.arange(shift, dtype=jnp.int32)[None, :, None] * (rows // shift)
            + offset
            + homes[:, None, None] * each
            + jnp.arange(each, dtype=jnp.int32)[None, None, :]
        )
        row_ids.append(ids.reshape(-1))
        offset += owners * each
    row_of = jnp.concatenate(row_ids)

    hit = row_variant[:, None] == jnp.arange(variant_slot.shape[0], dtype=jnp.int32)[None, :]
    slot_rows = jnp.sum(jnp.where(hit, variant_slot[None, :], 0), axis=1)

    own = jnp.concatenate([gate_pattern, up_pattern, down_pattern], axis=1)
    seen = jnp.stack([own] + [lax.ppermute(own, "delta", [(i, (i - k) % owners) for i in range(owners)]) for k in range(1, owners)])
    back = (jnp.arange(owners, dtype=jnp.int32) - me) % owners
    by_owner = jnp.sum(
        jnp.where(
            (back[:, None] == jnp.arange(owners, dtype=jnp.int32)[None, :])[:, :, None, None], seen[None], 0
        ),
        axis=1,
    ).reshape(slots, 3 * per_slot)
    kinds = 2 * per_slot
    at_home = jnp.stack(
        [((d // 2) - my_y - 1) % ys + ys * jnp.where(d % 2 == my_core, 1, 0) for d in range(owners)]
    ).astype(jnp.int32)
    scal = jnp.concatenate([me.astype(jnp.int32)[None], at_home])
    blocks_in = (by_owner[:, :kinds] // col_tiles).astype(BF)
    table = jnp.pad(blocks_in, ((0, -slots % 128), (0, -kinds % 128)))

    if groups == 2 and per_owner % 2 == 0:
        part = per_owner // 2
        mine_g = lax.axis_index("groups")
        piece = lax.dynamic_slice_in_dim(down_tiles, mine_g * part, part, 0)
        gathered = jnp.stack([y_move(piece, -k) for k in range(1, ys)] + [piece])
        other = lax.ppermute(gathered, "groups", [(0, 1), (1, 0)])
        both = jnp.stack([gathered, other])
        firsts = [mine_g * part, (1 - mine_g) * part]
    else:
        part = per_owner
        both = jnp.stack([y_move(down_tiles, -k) for k in range(1, ys)] + [down_tiles])[None]
        firsts = [0]
    all_tiles = jnp.stack([core_swap(both), both]).reshape(-1, 256, 256)
    tile_slots = jnp.stack(
        [
            (y * 2 + c) * per_owner + first + s
            for c in (1 - my_core, my_core)
            for first in firsts
            for y in order_y
            for s in range(part)
        ]
    ).astype(jnp.int32)
    picked = tile_slots[:, None] == jnp.arange(slots, dtype=jnp.int32)[None, :]
    places = jnp.sum(jnp.where(picked[:, :, None], by_owner[None, :, kinds:], 0), axis=1).reshape(-1)
    down_scal = jnp.concatenate([me.astype(jnp.int32)[None], jnp.repeat(tile_slots, per_slot), places])

    def after(x, *earlier):
        return lax.optimization_barrier((x, *earlier))[0]

    def transform(i, x):
        send, keep = gate_up(x, gate_weight, up_weight)
        return keep, core_swap(send)

    def exchange(keep, core):
        each = keep.shape[1] // ys
        return [
            y_move(
                (keep[:, (k - 1) * each : k * each] + core[:, (k - 1) * each : k * each]).astype(BF), k
            )
            for k in range(1, ys)
        ]

    starts = [sum(sizes[:i]) for i in range(len(sizes))]
    inners = [s // owners for s in starts]
    xs = [jnp.take(tokens, ids, axis=0) for ids in row_ids]
    kept = [None] * len(sizes)
    cores = [None] * len(sizes)
    gots = [None] * len(sizes)

    kept[0], cores[0] = transform(0, xs[0])
    packed, code = pack(
        scal, after(tokens, kept[0]), slot_rows[None, :], slot_rows[:, None], table, owners, per_owner, kinds
    )
    gots[0] = exchange(kept[0], cores[0])
    features = reduce_homes(packed.reshape(owners, CAP, -1), 0)
    code_q = jnp.sum(
        jnp.where(row_of[:, None] == jnp.arange(rows, dtype=jnp.int32)[None, :], code, 0), axis=1
    )
    slot_q = code_q // CAP
    pieces = tuple(
        (home, inner, size // owners, start + home * (size // owners))
        for size, start, inner in zip(sizes, starts, inners)
        for home in range(owners)
    )
    slot_home = jnp.concatenate([slot_q[s + size - size // owners : s + size] for s, size in zip(starts, sizes)])
    hot_home = slot_home[:, None] == jnp.arange(slots, dtype=jnp.int32)[None, :]
    where = jnp.sum(
        jnp.where(hot_home[:, :, None], (by_owner[:, :kinds] % col_tiles)[None], 0), axis=1
    )
    ss_q = slot_q[:, None]

    for i in range(1, len(sizes)):
        kept[i], cores[i] = transform(i, after(xs[i], kept[i - 1], packed))
        if i == 1:
            spread = product(
                scal, after(features, kept[1]), gate_tiles, up_tiles, code_q[None, :], owners, per_owner, pieces
            )
            home_delta = reduce_homes(spread, 0)
        gots[i] = exchange(kept[i], cores[i])

    result = []
    for i, size in enumerate(sizes):
        keep = kept[i]
        got = gots[i][0]
        if ys > 2:
            got = sum(g.astype(F32) for g in gots[i])
        hid = activate(keep, cores[i], got, home_delta, where, per_slot, inners[i])
        chip = jnp.concatenate([y_move(hid, -k) for k in range(1, ys)] + [hid])
        out = down(down_scal, core_swap(chip), chip, down_weight, all_tiles, ss_q, width_tiles, starts[i])
        blocks = out.reshape(owners, shift, size // (owners * shift), shard_width).transpose(1, 0, 2, 3)
        total = lax.dynamic_index_in_dim(blocks, here_t, 0, keepdims=False)
        for k in range(1, shift):
            gone = lax.dynamic_index_in_dim(blocks, (here_t + k) % shift, 0, keepdims=False).astype(BF)
            total = total + lax.ppermute(
                gone, "tensor", [(i, (i + k) % shift) for i in range(shift)]
            ).astype(F32)
        result.append(total.astype(BF))

    placed = [jnp.take(r, at_home, axis=0).reshape(-1, shard_width) for r in result]
    return jnp.concatenate(placed, axis=0)


def solution(mesh):
    return jax.shard_map(
        shards,
        mesh=mesh,
        in_specs=(
            P("groups", "delta"),
            P("delta", "tensor"),
            P("delta", "tensor"),
            P("tensor", "delta"),
            P("delta", "tensor", None, None),
            P("delta", "tensor", None, None),
            P("delta", "tensor", None, None),
            P("delta", "tensor"),
            P("delta", "tensor"),
            P("delta", "tensor"),
            P("groups"),
            P("groups"),
        ),
        out_specs=P(("groups", "tensor"), "delta"),
        check_vma=False,
    )
```

```python
import functools

import jax
import jax.numpy as jnp
from jax import lax
from jax.experimental import pallas as pl
from jax.experimental.pallas import tpu as pltpu
from jax.sharding import PartitionSpec as P

CAP = 128
CHUNKS = (1, 2, 1)
SHORT = 120e9
VMEM = 56 * 1024 * 1024
BF = jnp.bfloat16
F32 = jnp.float32


def cost(flops, moved):
    return pl.CostEstimate(flops=int(flops), bytes_accessed=int(moved), transcendentals=0)


def whole(shape):
    zeros = (0,) * len(shape)
    return pl.BlockSpec(shape, lambda *_: zeros)


def pack_body(owners, per_owner, kinds, capacity, scal, x, sl, ss, table, out, code):
    tile = 256
    rows, held = x.shape
    here = held // tile
    owner_l = sl[...] // per_owner
    first = lax.broadcasted_iota(jnp.int32, (rows, rows), 0)
    second = lax.broadcasted_iota(jnp.int32, (rows, rows), 1)
    ahead = ((ss[...] // per_owner) == owner_l) & (first < second)
    pos = jnp.sum(jnp.where(ahead, 1, 0), axis=0, keepdims=True)
    code[...] = sl[...] * capacity + pos
    target = pos
    for o in range(owners):
        target = target + jnp.where(owner_l == o, scal[1 + o] * capacity, 0)
    hot = lax.broadcasted_iota(jnp.int32, (owners * capacity, rows), 0) == target
    hot = jnp.where(hot, 1.0, 0.0).astype(BF)
    lanes = lax.broadcasted_iota(jnp.int32, (rows, table.shape[0]), 1)
    slot_hot = jnp.where(ss[...] == lanes, 1.0, 0.0).astype(BF)
    block = jnp.dot(slot_hot, table[...], preferred_element_type=F32)
    block = block - (scal[0] * here).astype(F32)
    for j in range(kinds):
        at = block[:, j : j + 1]
        picked = jnp.zeros((rows, tile), BF)
        for b in range(here):
            picked = jnp.where(at == float(b), x[:, b * tile : (b + 1) * tile], picked)
        out[:, j * tile : (j + 1) * tile] = jnp.dot(hot, picked, preferred_element_type=F32).astype(BF)


def pack(scal, x, sl, ss, table, owners, per_owner, kinds):
    rows = x.shape[0]
    width = kinds * 256
    return pl.pallas_call(
        functools.partial(pack_body, owners, per_owner, kinds, CAP),
        grid_spec=pltpu.PrefetchScalarGridSpec(
            num_scalar_prefetch=1,
            grid=(1,),
            in_specs=[whole(x.shape), whole((1, rows)), whole((rows, 1)), whole(table.shape)],
            out_specs=[whole((owners * CAP, width)), whole((1, rows))],
        ),
        out_shape=[
            jax.ShapeDtypeStruct((owners * CAP, width), BF),
            jax.ShapeDtypeStruct((1, rows), jnp.int32),
        ],
        compiler_params=pltpu.CompilerParams(vmem_limit_bytes=VMEM),
        cost_estimate=cost(SHORT, 4e6),
    )(scal, x, sl, ss, table)


def product_body(owners, per_owner, per_slot, pieces, scal, x, gt, ut, code, out):
    tile = 256
    capacity = x.shape[0]
    rows = code.shape[1]
    slot_l = code[...] // capacity
    place = lax.broadcasted_iota(jnp.int32, (capacity, rows), 0) == code[...] % capacity
    mine = place & (slot_l // per_owner == scal[0])
    slot = jnp.sum(jnp.where(mine, slot_l % per_owner + 1, 0), axis=1, keepdims=True) - 1
    hot = jnp.where(mine, 1.0, 0.0).astype(BF)
    for kind, tiles in enumerate((gt, ut)):
        for j in range(per_slot):
            at = (kind * per_slot + j) * tile
            source = x[:, at : at + tile]
            total = jnp.zeros((capacity, tile), F32)
            for s in range(per_owner):
                picked = jnp.where(slot == s, source, jnp.zeros_like(source))
                total = total + jnp.dot(picked, tiles[s, j], preferred_element_type=F32)
            spread = lax.dot_general(
                hot, total.astype(BF), (((0,), (0,)), ((), ())), preferred_element_type=F32
            ).astype(BF)
            for home, offset, size, start in pieces:
                out[home, offset : offset + size, at : at + tile] = spread[start : start + size]


def product(scal, x, gt, ut, code, owners, per_owner, pieces):
    rows = code.shape[1]
    per_slot = gt.shape[1]
    shape = (owners, rows // owners, x.shape[1])
    return pl.pallas_call(
        functools.partial(product_body, owners, per_owner, per_slot, pieces),
        grid_spec=pltpu.PrefetchScalarGridSpec(
            num_scalar_prefetch=1,
            grid=(1,),
            in_specs=[whole(x.shape), whole(gt.shape), whole(ut.shape), whole((1, rows))],
            out_specs=whole(shape),
        ),
        out_shape=jax.ShapeDtypeStruct(shape, BF),
        compiler_params=pltpu.CompilerParams(vmem_limit_bytes=VMEM),
        cost_estimate=cost(SHORT, 4e6),
    )(scal, x, gt, ut, code)


def gate_up_body(pieces, scal, *refs):
    blocks, (wg, wu, send, keep, x) = refs[:pieces], refs[pieces:]
    half = send.shape[1]

    @pl.when(pl.program_id(0) == 0)
    def _():
        each = x.shape[0] // pieces
        for i, block in enumerate(blocks):
            x[i * each : (i + 1) * each] = block[...].reshape(each, x.shape[1])

    for i, w in enumerate((wg, wu)):
        total = jnp.dot(x[...], w[...], preferred_element_type=F32)
        send[i] = total[:half].astype(send.dtype)
        keep[i] = total[half:]


def gate_up(scal, tokens, wg, wu, owners, shift, start, size):
    rows, depth = tokens.shape
    width = wg.shape[1]
    block = min(1024, width)
    each = size // (owners * shift)
    first = start // (shift * each)
    view = tokens.reshape(shift, rows // (shift * each), each, depth)
    outs = pl.BlockSpec((2, size // 2, block), lambda i, s: (0, 0, i))
    weights = pl.BlockSpec((depth, block), lambda i, s: (0, i))
    piece = [
        pl.BlockSpec((shift, 1, each, depth), functools.partial(lambda h, i, s: (0, first + s[h], 0, 0), h))
        for h in range(owners)
    ]
    return pl.pallas_call(
        functools.partial(gate_up_body, owners),
        grid_spec=pltpu.PrefetchScalarGridSpec(
            num_scalar_prefetch=1,
            grid=(width // block,),
            in_specs=[*piece, weights, weights],
            out_specs=[outs, outs],
            scratch_shapes=[pltpu.VMEM((size, depth), BF)],
        ),
        out_shape=[jax.ShapeDtypeStruct((2, size // 2, width), F32)] * 2,
        compiler_params=pltpu.CompilerParams(vmem_limit_bytes=VMEM),
        cost_estimate=cost(4 * size * depth * width, 4 * depth * width),
    )(scal, *[view] * owners, wg, wu)


def activate_body(per_slot, start, each, parts, keep, core, *refs):
    gots, (delta, where, out) = refs[:parts], refs[parts:]
    tile = 256
    step = pl.program_id(0)
    across = out.shape[1] // tile
    at = [where[start : start + each, k : k + 1] - step * across for k in range(2 * per_slot)]
    adds = [
        delta[start : start + each, k * tile : (k + 1) * tile].astype(F32) for k in range(2 * per_slot)
    ]
    for b in range(across):
        cols = slice(b * tile, (b + 1) * tile)
        sums = []
        for kind in range(2):
            got = gots[0][kind, :, cols] if parts == 1 else gots[kind][0, :, cols]
            total = keep[kind, :, cols] + core[kind, :, cols] + got.astype(F32)
            for k in range(kind * per_slot, (kind + 1) * per_slot):
                total = total + jnp.where(at[k] == b, adds[k], 0.0)
            sums.append(total)
        gate, up = sums
        out[:, cols] = (gate / (1.0 + jnp.exp(-gate)) * up).astype(BF)


def activate(keep, core, gots, delta, where, per_slot, start):
    each, width = gots[0].shape[1:]
    last = keep.shape[1] // each - 1
    block = min(2048, width)
    own = pl.BlockSpec((2, each, block), lambda i: (0, last, i))
    taken = [pl.BlockSpec((g.shape[0], each, block), lambda i: (0, 0, i)) for g in gots]
    return pl.pallas_call(
        functools.partial(activate_body, per_slot, start, each, len(gots)),
        grid=(width // block,),
        in_specs=[own, own, *taken, whole(delta.shape), whole(where.shape)],
        out_specs=pl.BlockSpec((each, block), lambda i: (0, i)),
        out_shape=jax.ShapeDtypeStruct((each, width), BF),
        compiler_params=pltpu.CompilerParams(vmem_limit_bytes=VMEM),
        cost_estimate=cost(SHORT, 24 * each * width),
    )(keep, core, *gots, delta, where)


def down_body(width_tiles, here, count, start, scal, far, near, w, tiles, slot, out, hid):
    tile = 256
    me = scal[0]
    across = out.shape[1] // tile
    step = pl.program_id(0)
    half = far.shape[0]

    @pl.when(step == 0)
    def _():
        hid[:half] = far[...]
        hid[half:] = near[...]

    out[...] = jnp.dot(hid[...], w[...], preferred_element_type=F32)

    def one(i, carry):
        place = scal[1 + count + i]
        block = place % width_tiles - me * here - step * across

        @pl.when((block >= 0) & (block < across))
        def _():
            source = hid[:, pl.ds(pl.multiple_of((place // width_tiles) * tile, tile), tile)]
            hit = slot[start : start + 2 * half] == scal[1 + i]
            picked = jnp.where(hit, source, jnp.zeros_like(source))
            add = jnp.dot(picked, tiles[i], preferred_element_type=F32)
            cols = pl.ds(pl.multiple_of(block * tile, tile), tile)
            out[:, cols] = out[:, cols] + add

        return carry

    lax.fori_loop(0, count, one, 0)


def down(scal, far, near, w, tiles, slot, width_tiles, start):
    rows, depth = 2 * far.shape[0], far.shape[1]
    width = w.shape[1]
    block = min(512, width)
    count = tiles.shape[0]
    return pl.pallas_call(
        functools.partial(down_body, width_tiles, width // 256, count, start),
        grid_spec=pltpu.PrefetchScalarGridSpec(
            num_scalar_prefetch=1,
            grid=(width // block,),
            in_specs=[
                whole(far.shape),
                whole(near.shape),
                pl.BlockSpec((depth, block), lambda i, s: (0, i)),
                whole(tiles.shape),
                whole(slot.shape),
            ],
            out_specs=pl.BlockSpec((rows, block), lambda i, s: (0, i)),
            scratch_shapes=[pltpu.VMEM((rows, depth), BF)],
        ),
        out_shape=jax.ShapeDtypeStruct((rows, width), F32),
        compiler_params=pltpu.CompilerParams(vmem_limit_bytes=VMEM),
        cost_estimate=cost(3 * rows * depth * width, 3 * depth * width),
    )(scal, far, near, w, tiles, slot)


def shards(
    tokens,
    gate_weight,
    up_weight,
    down_weight,
    gate_tiles,
    up_tiles,
    down_tiles,
    gate_pattern,
    up_pattern,
    down_pattern,
    row_variant,
    variant_slot,
):
    owners = lax.axis_size("delta")
    shift = lax.axis_size("tensor")
    groups = lax.axis_size("groups")
    me = lax.axis_index("delta")
    here_t = lax.axis_index("tensor")
    my_core, my_y = me % 2, me // 2
    ys = owners // 2
    per_owner, per_slot = gate_pattern.shape
    slots = owners * per_owner
    rows, shard_width = tokens.shape
    width = gate_weight.shape[1]
    col_tiles = width // 256
    width_tiles = shard_width * owners // 256
    unit = rows // sum(CHUNKS)
    sizes = [unit * c for c in CHUNKS]

    def core_swap(x):
        return lax.ppermute(x, "delta", [(i, i ^ 1) for i in range(owners)])

    def y_move(x, k):
        return lax.ppermute(x, "delta", [(i, (i + 2 * k) % owners) for i in range(owners)])

    order_y = [(my_y + k) % ys for k in range(1, ys)] + [my_y]
    homes = jnp.stack([y * 2 + c for c in (1 - my_core, my_core) for y in order_y]).astype(jnp.int32)

    row_ids = []
    offset = 0
    for size in sizes:
        each = size // (owners * shift)
        ids = (
            jnp.arange(shift, dtype=jnp.int32)[None, :, None] * (rows // shift)
            + offset
            + homes[:, None, None] * each
            + jnp.arange(each, dtype=jnp.int32)[None, None, :]
        )
        row_ids.append(ids.reshape(-1))
        offset += owners * each
    row_of = jnp.concatenate(row_ids)

    hit = row_variant[:, None] == jnp.arange(variant_slot.shape[0], dtype=jnp.int32)[None, :]
    slot_rows = jnp.sum(jnp.where(hit, variant_slot[None, :], 0), axis=1)

    own = jnp.concatenate([gate_pattern, up_pattern, down_pattern], axis=1)
    seen = jnp.stack([own] + [lax.ppermute(own, "delta", [(i, (i - k) % owners) for i in range(owners)]) for k in range(1, owners)])
    back = (jnp.arange(owners, dtype=jnp.int32) - me) % owners
    by_owner = jnp.sum(
        jnp.where(
            (back[:, None] == jnp.arange(owners, dtype=jnp.int32)[None, :])[:, :, None, None], seen[None], 0
        ),
        axis=1,
    ).reshape(slots, 3 * per_slot)
    kinds = 2 * per_slot
    at_home = jnp.stack(
        [((d // 2) - my_y - 1) % ys + ys * jnp.where(d % 2 == my_core, 1, 0) for d in range(owners)]
    ).astype(jnp.int32)
    scal = jnp.concatenate([me.astype(jnp.int32)[None], at_home])
    blocks_in = (by_owner[:, :kinds] // col_tiles).astype(BF)
    table = jnp.pad(blocks_in, ((0, -slots % 128), (0, -kinds % 128)))

    if groups == 2 and per_owner % 2 == 0:
        part = per_owner // 2
        mine_g = lax.axis_index("groups")
        piece = lax.dynamic_slice_in_dim(down_tiles, mine_g * part, part, 0)
        gathered = jnp.stack([y_move(piece, -k) for k in range(1, ys)] + [piece])
        other = lax.ppermute(gathered, "groups", [(0, 1), (1, 0)])
        both = jnp.stack([gathered, other])
        firsts = [mine_g * part, (1 - mine_g) * part]
    else:
        part = per_owner
        gathered = jnp.stack([y_move(down_tiles, -k) for k in range(1, ys)] + [down_tiles])
        other = gathered
        both = gathered[None]
        firsts = [0]
    all_tiles = jnp.stack([core_swap(both), both]).reshape(-1, 256, 256)
    tile_slots = jnp.stack(
        [
            (y * 2 + c) * per_owner + first + s
            for c in (1 - my_core, my_core)
            for first in firsts
            for y in order_y
            for s in range(part)
        ]
    ).astype(jnp.int32)
    picked = tile_slots[:, None] == jnp.arange(slots, dtype=jnp.int32)[None, :]
    places = jnp.sum(jnp.where(picked[:, :, None], by_owner[None, :, kinds:], 0), axis=1).reshape(-1)
    down_scal = jnp.concatenate([me.astype(jnp.int32)[None], jnp.repeat(tile_slots, per_slot), places])

    def after(x, *earlier):
        return lax.optimization_barrier((x, *earlier))[0]

    starts = [sum(sizes[:i]) for i in range(len(sizes))]
    inners = [s // owners for s in starts]
    count = len(sizes)
    kept, cores, sends, gots = ([None] * count for _ in range(4))

    def multiply(i, *earlier):
        send, kept[i] = gate_up(
            after(homes, *earlier), tokens, gate_weight, up_weight, owners, shift, starts[i], sizes[i]
        )
        cores[i] = core_swap(send)

    def exchange(i):
        each = sizes[i] // owners
        parts = [slice(0, 2)] if CHUNKS[i] == 1 else [slice(0, 1), slice(1, 2)]
        sends[i], gots[i] = [], []
        for part in parts:
            got = None
            for k in range(1, ys):
                rows_k = slice((k - 1) * each, k * each)
                sends[i].append((kept[i][part, rows_k] + cores[i][part, rows_k]).astype(BF))
                moved = y_move(sends[i][-1], k)
                if ys > 2:
                    moved = moved.astype(F32)
                got = moved if got is None else got + moved
            gots[i].append(got)

    def halve(x):
        half = owners // 2
        return x[half:] + core_swap(x[:half])

    def finish(x, *earlier):
        total = after(x[ys - 1], *earlier)
        for k in range(1, ys):
            total = total + y_move(x[k - 1], k)
        return total

    multiply(0)
    packed, code = pack(
        after(scal, kept[0], gathered), tokens, slot_rows[None, :], slot_rows[:, None], table, owners, per_owner, kinds
    )
    exchange(0)
    packed = halve(packed.reshape(owners, CAP, -1))
    code_q = jnp.sum(
        jnp.where(row_of[:, None] == jnp.arange(rows, dtype=jnp.int32)[None, :], code, 0), axis=1
    )
    slot_q = code_q // CAP
    pieces = tuple(
        (home, inner, size // owners, start + home * (size // owners))
        for size, start, inner in zip(sizes, starts, inners)
        for home in range(owners)
    )
    slot_home = jnp.concatenate([slot_q[s + size - size // owners : s + size] for s, size in zip(starts, sizes)])
    hot_home = slot_home[:, None] == jnp.arange(slots, dtype=jnp.int32)[None, :]
    where = jnp.sum(
        jnp.where(hot_home[:, :, None], (by_owner[:, :kinds] % col_tiles)[None], 0), axis=1
    )
    ss_q = slot_q[:, None]

    for i in range(1, count):
        if i == 1:
            multiply(1, *sends[0], packed)
            features = finish(packed, kept[1])
            spread = product(
                after(scal, kept[1], *gots[0], other), features, gate_tiles, up_tiles, code_q[None, :], owners, per_owner, pieces
            )
            exchange(1)
            spread = halve(spread)
            held = (spread,)
        else:
            multiply(i, *sends[i - 1], *gots[i - 2], *held)
            held = ()
            exchange(i)
    home_delta = finish(spread, kept[2])

    def finish_hidden(i, *earlier):
        hid = activate(kept[i], cores[i], gots[i], home_delta, after(where, *earlier), per_slot, inners[i])
        return hid, jnp.concatenate([y_move(hid, -k) for k in range(1, ys)] + [hid])

    def finish_down(i, chip, *earlier):
        out = down(
            after(down_scal, *earlier), core_swap(chip), chip, down_weight, all_tiles, ss_q, width_tiles, starts[i]
        )
        blocks = out.reshape(owners, shift, sizes[i] // (owners * shift), shard_width).transpose(1, 0, 2, 3)
        total = lax.dynamic_index_in_dim(blocks, here_t, 0, keepdims=False)
        gone = [
            lax.dynamic_index_in_dim(blocks, (here_t + k) % shift, 0, keepdims=False).astype(BF)
            for k in range(1, shift)
        ]
        for k in range(1, shift):
            total = total + lax.ppermute(
                gone[k - 1], "tensor", [(i, (i + k) % shift) for i in range(shift)]
            ).astype(F32)
        return gone, total.astype(BF)

    chips, result = [], []
    hid, chip = finish_hidden(0, kept[count - 1], all_tiles, gots[1][0])
    chips.append(chip)
    for i in range(1, count):
        hid, chip = finish_hidden(i, hid, *sends[count - 1])
        chips.append(chip)
    gone = ()
    for i in range(count):
        gone, total = finish_down(i, chips[i], *gone)
        result.append(total)

    placed = [jnp.take(r, at_home, axis=0).reshape(-1, shard_width) for r in result]
    return jnp.concatenate(placed, axis=0)


def solution(mesh):
    return jax.shard_map(
        shards,
        mesh=mesh,
        in_specs=(
            P("groups", "delta"),
            P("delta", "tensor"),
            P("delta", "tensor"),
            P("tensor", "delta"),
            P("delta", "tensor", None, None),
            P("delta", "tensor", None, None),
            P("delta", "tensor", None, None),
            P("delta", "tensor"),
            P("delta", "tensor"),
            P("delta", "tensor"),
            P("groups"),
            P("groups"),
        ),
        out_specs=P(("groups", "tensor"), "delta"),
        check_vma=False,
    )
```

```python
import functools

import jax
import jax.numpy as jnp
from jax import lax
from jax.experimental import pallas as pl
from jax.experimental.pallas import tpu as pltpu
from jax.sharding import PartitionSpec as P

CAP = 128
CHUNKS = (2, 1, 1)
SHORT = 120e9
VMEM = 56 * 1024 * 1024
BF = jnp.bfloat16
F32 = jnp.float32


def cost(flops, moved):
    return pl.CostEstimate(flops=int(flops), bytes_accessed=int(moved), transcendentals=0)


def whole(shape):
    zeros = (0,) * len(shape)
    return pl.BlockSpec(shape, lambda *_: zeros)


def pack_body(owners, per_owner, kinds, stride, capacity, col_tiles, scal, x, sl, ss, out, code, table):
    tile = 256
    rows, held = x.shape
    here = held // tile
    me = scal[0]
    height = table.shape[0]
    at_row = lax.broadcasted_iota(jnp.int32, (height, 128), 0)
    at_lane = lax.broadcasted_iota(jnp.int32, (height, 128), 1)
    known = jnp.zeros((height, 128), jnp.int32)
    for s in range(owners * per_owner):
        back = (s // per_owner - me + owners) % owners
        for j in range(kinds):
            place = scal[1 + owners + (back * per_owner + s % per_owner) * stride + j]
            known = jnp.where((at_row == s) & (at_lane == j), place // col_tiles, known)
            known = jnp.where((at_row == s) & (at_lane == 64 + j), place % col_tiles, known)
    table[...] = known.astype(F32).astype(BF)
    owner_l = sl[...] // per_owner
    first = lax.broadcasted_iota(jnp.int32, (rows, rows), 0)
    second = lax.broadcasted_iota(jnp.int32, (rows, rows), 1)
    ahead = ((ss[...] // per_owner) == owner_l) & (first < second)
    pos = jnp.sum(jnp.where(ahead, 1, 0), axis=0, keepdims=True)
    code[...] = sl[...] * capacity + pos
    target = pos
    for o in range(owners):
        target = target + jnp.where(owner_l == o, scal[1 + o] * capacity, 0)
    hot = lax.broadcasted_iota(jnp.int32, (owners * capacity, rows), 0) == target
    hot = jnp.where(hot, 1.0, 0.0).astype(BF)
    lanes = lax.broadcasted_iota(jnp.int32, (rows, height), 1)
    slot_hot = jnp.where(ss[...] == lanes, 1.0, 0.0).astype(BF)
    block = jnp.dot(slot_hot, table[...], preferred_element_type=F32)
    block = block - (me * here).astype(F32)
    for j in range(kinds):
        at = block[:, j : j + 1]
        picked = jnp.zeros((rows, tile), BF)
        for b in range(here):
            picked = jnp.where(at == float(b), x[:, b * tile : (b + 1) * tile], picked)
        out[:, j * tile : (j + 1) * tile] = jnp.dot(hot, picked, preferred_element_type=F32).astype(BF)


def pack(scal, x, sl, ss, owners, per_owner, kinds, stride, col_tiles):
    rows = x.shape[0]
    width = kinds * 256
    height = -(-owners * per_owner // 128) * 128
    return pl.pallas_call(
        functools.partial(pack_body, owners, per_owner, kinds, stride, CAP, col_tiles),
        grid_spec=pltpu.PrefetchScalarGridSpec(
            num_scalar_prefetch=1,
            grid=(1,),
            in_specs=[whole(x.shape), whole((1, rows)), whole((rows, 1))],
            out_specs=[whole((owners * CAP, width)), whole((1, rows)), whole((height, 128))],
        ),
        out_shape=[
            jax.ShapeDtypeStruct((owners * CAP, width), BF),
            jax.ShapeDtypeStruct((1, rows), jnp.int32),
            jax.ShapeDtypeStruct((height, 128), BF),
        ],
        compiler_params=pltpu.CompilerParams(vmem_limit_bytes=VMEM),
        cost_estimate=cost(SHORT, 4e6),
    )(scal, x, sl, ss)


def product_body(owners, per_owner, per_slot, pieces, scal, x, gt, ut, code, out):
    tile = 256
    capacity = x.shape[0]
    rows = code.shape[1]
    slot_l = code[...] // capacity
    place = lax.broadcasted_iota(jnp.int32, (capacity, rows), 0) == code[...] % capacity
    mine = place & (slot_l // per_owner == scal[0])
    slot = jnp.sum(jnp.where(mine, slot_l % per_owner + 1, 0), axis=1, keepdims=True) - 1
    hot = jnp.where(mine, 1.0, 0.0).astype(BF)
    for kind, tiles in enumerate((gt, ut)):
        for j in range(per_slot):
            at = (kind * per_slot + j) * tile
            source = x[:, at : at + tile]
            total = jnp.zeros((capacity, tile), F32)
            for s in range(per_owner):
                picked = jnp.where(slot == s, source, jnp.zeros_like(source))
                total = total + jnp.dot(picked, tiles[s, j], preferred_element_type=F32)
            spread = lax.dot_general(
                hot, total.astype(BF), (((0,), (0,)), ((), ())), preferred_element_type=F32
            ).astype(BF)
            for home, offset, size, start in pieces:
                out[home, offset : offset + size, at : at + tile] = spread[start : start + size]


def product(scal, x, gt, ut, code, owners, per_owner, pieces):
    rows = code.shape[1]
    per_slot = gt.shape[1]
    shape = (owners, rows // owners, x.shape[1])
    return pl.pallas_call(
        functools.partial(product_body, owners, per_owner, per_slot, pieces),
        grid_spec=pltpu.PrefetchScalarGridSpec(
            num_scalar_prefetch=1,
            grid=(1,),
            in_specs=[whole(x.shape), whole(gt.shape), whole(ut.shape), whole((1, rows))],
            out_specs=whole(shape),
        ),
        out_shape=jax.ShapeDtypeStruct(shape, BF),
        compiler_params=pltpu.CompilerParams(vmem_limit_bytes=VMEM),
        cost_estimate=cost(SHORT, 4e6),
    )(scal, x, gt, ut, code)


def gate_up_body(pieces, scal, *refs):
    blocks, (wg, wu, send, keep, x) = refs[:pieces], refs[pieces:]
    half = send.shape[1]

    @pl.when(pl.program_id(0) == 0)
    def _():
        each = x.shape[0] // pieces
        for i, block in enumerate(blocks):
            x[i * each : (i + 1) * each] = block[...].reshape(each, x.shape[1])

    for i, w in enumerate((wg, wu)):
        total = jnp.dot(x[...], w[...], preferred_element_type=F32)
        send[i] = total[:half].astype(send.dtype)
        keep[i] = total[half:]


def gate_up(scal, tokens, wg, wu, owners, shift, start, size):
    rows, depth = tokens.shape
    width = wg.shape[1]
    block = min(1024, width)
    each = size // (owners * shift)
    first = start // (shift * each)
    view = tokens.reshape(shift, rows // (shift * each), each, depth)
    outs = pl.BlockSpec((2, size // 2, block), lambda i, s: (0, 0, i))
    weights = pl.BlockSpec((depth, block), lambda i, s: (0, i))
    piece = [
        pl.BlockSpec((shift, 1, each, depth), functools.partial(lambda h, i, s: (0, first + s[h], 0, 0), h))
        for h in range(owners)
    ]
    return pl.pallas_call(
        functools.partial(gate_up_body, owners),
        grid_spec=pltpu.PrefetchScalarGridSpec(
            num_scalar_prefetch=1,
            grid=(width // block,),
            in_specs=[*piece, weights, weights],
            out_specs=[outs, outs],
            scratch_shapes=[pltpu.VMEM((size, depth), BF)],
        ),
        out_shape=[jax.ShapeDtypeStruct((2, size // 2, width), F32)] * 2,
        compiler_params=pltpu.CompilerParams(vmem_limit_bytes=VMEM),
        cost_estimate=cost(4 * size * depth * width, 4 * depth * width),
    )(scal, *[view] * owners, wg, wu)


def activate_body(per_slot, start, each, row, parts, keep, core, *refs):
    gots, (delta, slot, table, out) = refs[:parts], refs[parts:]
    tile = 256
    step = pl.program_id(0)
    across = out.shape[1] // tile
    lanes = lax.broadcasted_iota(jnp.int32, (each, table.shape[0]), 1)
    hot = jnp.where(slot[row : row + each] == lanes, 1.0, 0.0).astype(BF)
    where = jnp.dot(hot, table[...], preferred_element_type=F32) - (step * across).astype(F32)
    at = [where[:, 64 + k : 65 + k] for k in range(2 * per_slot)]
    adds = [
        delta[start : start + each, k * tile : (k + 1) * tile].astype(F32) for k in range(2 * per_slot)
    ]
    for b in range(across):
        cols = slice(b * tile, (b + 1) * tile)
        sums = []
        for kind in range(2):
            got = gots[0][kind, :, cols] if parts == 1 else gots[kind][0, :, cols]
            total = keep[kind, :, cols] + core[kind, :, cols] + got.astype(F32)
            for k in range(kind * per_slot, (kind + 1) * per_slot):
                total = total + jnp.where(at[k] == float(b), adds[k], 0.0)
            sums.append(total)
        gate, up = sums
        out[:, cols] = (gate / (1.0 + jnp.exp(-gate)) * up).astype(BF)


def activate(keep, core, gots, delta, slot, table, per_slot, start, row, flops):
    each, width = gots[0].shape[1:]
    last = keep.shape[1] // each - 1
    block = min(2048, width)
    own = pl.BlockSpec((2, each, block), lambda i: (0, last, i))
    taken = [pl.BlockSpec((g.shape[0], each, block), lambda i: (0, 0, i)) for g in gots]
    return pl.pallas_call(
        functools.partial(activate_body, per_slot, start, each, row, len(gots)),
        grid=(width // block,),
        in_specs=[own, own, *taken, whole(delta.shape), whole(slot.shape), whole(table.shape)],
        out_specs=pl.BlockSpec((each, block), lambda i: (0, i)),
        out_shape=jax.ShapeDtypeStruct((each, width), BF),
        compiler_params=pltpu.CompilerParams(vmem_limit_bytes=VMEM),
        cost_estimate=cost(flops, 24 * each * width),
    )(keep, core, *gots, delta, slot, table)


def down_body(width_tiles, here, plan, owners, per_owner, per_slot, start, scal, far, near, w, *refs):
    tiles, (slot, out, hid, listed, number) = refs[: len(plan)], refs[len(plan) :]
    tile = 256
    across = out.shape[1] // tile
    step = pl.program_id(0)
    half = far.shape[0]
    stride = 3 * per_slot
    patterns = scal.shape[0] - owners * per_owner * stride

    @pl.when(step == 0)
    def _():
        hid[:half] = far[...]
        hid[half:] = near[...]
        me = scal[0]
        for r, (base, run) in enumerate(plan):
            for at in range(number.shape[1]):
                number[r, at] = 0

            def one(i, carry):
                local = i // per_slot
                which = scal[base + local // run] + local % run
                back = (which // per_owner - me + owners) % owners
                row = back * per_owner + which % per_owner
                place = scal[patterns + row * stride + 2 * per_slot + i % per_slot]
                block = place % width_tiles - me * here

                @pl.when((block >= 0) & (block < here))
                def _():
                    at = block // across
                    n = number[r, at]
                    listed[r * number.shape[1] + at, 4 * n] = i
                    listed[r * number.shape[1] + at, 4 * n + 1] = which
                    listed[r * number.shape[1] + at, 4 * n + 2] = place // width_tiles
                    listed[r * number.shape[1] + at, 4 * n + 3] = block % across
                    number[r, at] = n + 1

                return carry

            lax.fori_loop(0, tiles[r].shape[0], one, 0)

    out[...] = jnp.dot(hid[...], w[...], preferred_element_type=F32)
    for r in range(len(plan)):
        entry = r * number.shape[1] + step

        def add(n, carry):
            i = listed[entry, 4 * n]
            col = pl.multiple_of(listed[entry, 4 * n + 2] * tile, tile)
            source = hid[:, pl.ds(col, tile)]
            hit = slot[start : start + 2 * half] == listed[entry, 4 * n + 1]
            picked = jnp.where(hit, source, jnp.zeros_like(source))
            cols = pl.ds(pl.multiple_of(listed[entry, 4 * n + 3] * tile, tile), tile)
            out[:, cols] = out[:, cols] + jnp.dot(picked, tiles[r][i], preferred_element_type=F32)
            return carry

        lax.fori_loop(0, number[r, step], add, 0)


def down(scal, far, near, w, tiles, plan, slot, width_tiles, owners, per_owner, per_slot, start, flops):
    rows, depth = 2 * far.shape[0], far.shape[1]
    width = w.shape[1]
    block = min(512, width)
    steps = width // block
    most = max(t.shape[0] for t in tiles)
    return pl.pallas_call(
        functools.partial(down_body, width_tiles, width // 256, plan, owners, per_owner, per_slot, start),
        grid_spec=pltpu.PrefetchScalarGridSpec(
            num_scalar_prefetch=1,
            grid=(steps,),
            in_specs=[
                whole(far.shape),
                whole(near.shape),
                pl.BlockSpec((depth, block), lambda i, s: (0, i)),
                *[whole(t.shape) for t in tiles],
                whole(slot.shape),
            ],
            out_specs=pl.BlockSpec((rows, block), lambda i, s: (0, i)),
            scratch_shapes=[
                pltpu.VMEM((rows, depth), BF),
                pltpu.SMEM((len(tiles) * steps, 4 * most), jnp.int32),
                pltpu.SMEM((len(tiles), steps), jnp.int32),
            ],
        ),
        out_shape=jax.ShapeDtypeStruct((rows, width), F32),
        compiler_params=pltpu.CompilerParams(vmem_limit_bytes=VMEM),
        cost_estimate=cost(flops, 1e6),
    )(scal, far, near, w, *tiles, slot)


def shards(
    tokens,
    gate_weight,
    up_weight,
    down_weight,
    gate_tiles,
    up_tiles,
    down_tiles,
    gate_pattern,
    up_pattern,
    down_pattern,
    row_variant,
    variant_slot,
):
    owners = lax.axis_size("delta")
    shift = lax.axis_size("tensor")
    groups = lax.axis_size("groups")
    me = lax.axis_index("delta")
    here_t = lax.axis_index("tensor")
    my_core, my_y = me % 2, me // 2
    ys = owners // 2
    per_owner, per_slot = gate_pattern.shape
    slots = owners * per_owner
    rows, shard_width = tokens.shape
    width = gate_weight.shape[1]
    col_tiles = width // 256
    width_tiles = shard_width * owners // 256
    unit = rows // sum(CHUNKS)
    sizes = [unit * c for c in CHUNKS]

    def core_swap(x):
        return lax.ppermute(x, "delta", [(i, i ^ 1) for i in range(owners)])

    def y_move(x, k):
        return lax.ppermute(x, "delta", [(i, (i + 2 * k) % owners) for i in range(owners)])

    order_y = [(my_y + k) % ys for k in range(1, ys)] + [my_y]
    homes = jnp.stack([y * 2 + c for c in (1 - my_core, my_core) for y in order_y]).astype(jnp.int32)

    row_ids = []
    offset = 0
    for size in sizes:
        each = size // (owners * shift)
        ids = (
            jnp.arange(shift, dtype=jnp.int32)[None, :, None] * (rows // shift)
            + offset
            + homes[:, None, None] * each
            + jnp.arange(each, dtype=jnp.int32)[None, None, :]
        )
        row_ids.append(ids.reshape(-1))
        offset += owners * each
    row_of = jnp.concatenate(row_ids)

    hit = row_variant[:, None] == jnp.arange(variant_slot.shape[0], dtype=jnp.int32)[None, :]
    slot_rows = jnp.sum(jnp.where(hit, variant_slot[None, :], 0), axis=1)

    def after(x, *earlier):
        return lax.optimization_barrier((x, *earlier))[0]

    kinds = 2 * per_slot
    own = jnp.concatenate([gate_pattern, up_pattern, down_pattern], axis=1)
    seen = [own] + [
        lax.ppermute(own, "delta", [(i, (i - k) % owners) for i in range(owners)]) for k in range(1, owners)
    ]
    patterns = jnp.concatenate([s.reshape(-1) for s in seen])
    at_home = jnp.stack(
        [((d // 2) - my_y - 1) % ys + ys * jnp.where(d % 2 == my_core, 1, 0) for d in range(owners)]
    ).astype(jnp.int32)
    scal = jnp.concatenate([me.astype(jnp.int32)[None], at_home, patterns])

    flat_tiles = down_tiles.reshape(-1, 256, 256)
    if groups == 2 and per_owner % 2 == 0:
        part = per_owner // 2
        mine_g = lax.axis_index("groups")
        piece = lax.dynamic_slice_in_dim(flat_tiles, mine_g * part * per_slot, part * per_slot, 0)
        halves = [mine_g * part, (1 - mine_g) * part]
    else:
        part, piece, halves = per_owner, flat_tiles, [0]
    from_y = jnp.concatenate([y_move(piece, -k) for k in range(1, ys)])
    tiles = [from_y]
    if len(halves) == 2:
        tiles.append(lax.ppermute(from_y, "groups", [(0, 1), (1, 0)]))
    arrived = tuple(tiles)
    firsts, plan = [], []
    for core in (my_core, 1 - my_core):
        for first in halves:
            plan.append((1 + len(firsts), part))
            firsts.extend((y * 2 + core) * per_owner + first for y in order_y[:-1])
        plan.append((1 + len(firsts), per_owner))
        firsts.append((my_y * 2 + core) * per_owner)
    plan = tuple(plan)
    down_scal = jnp.concatenate([jnp.stack([me] + firsts).astype(jnp.int32), patterns])

    starts = [sum(sizes[:i]) for i in range(len(sizes))]
    inners = [s // owners for s in starts]
    count = len(sizes)
    kept, cores, sends, gots = ([None] * count for _ in range(4))

    def multiply(i, *earlier):
        send, kept[i] = gate_up(
            after(homes, *earlier), tokens, gate_weight, up_weight, owners, shift, starts[i], sizes[i]
        )
        cores[i] = core_swap(send)

    def exchange(i):
        each = sizes[i] // owners
        parts = [slice(0, 2)]
        sends[i], gots[i] = [], []
        for part in parts:
            got = None
            for k in range(1, ys):
                rows_k = slice((k - 1) * each, k * each)
                sends[i].append((kept[i][part, rows_k] + cores[i][part, rows_k]).astype(BF))
                moved = y_move(sends[i][-1], k)
                if ys > 2:
                    moved = moved.astype(F32)
                got = moved if got is None else got + moved
            gots[i].append(got)

    def halve(x):
        half = owners // 2
        return x[half:] + core_swap(x[:half])

    def finish(x, *earlier):
        total = after(x[ys - 1], *earlier)
        for k in range(1, ys):
            total = total + y_move(x[k - 1], k)
        return total

    multiply(0)
    packed, code, table = pack(
        after(scal, kept[0], from_y),
        tokens,
        slot_rows[None, :],
        slot_rows[:, None],
        owners,
        per_owner,
        kinds,
        3 * per_slot,
        col_tiles,
    )
    exchange(0)
    packed = halve(packed.reshape(owners, CAP, -1))
    code_q = jnp.sum(
        jnp.where(row_of[:, None] == jnp.arange(rows, dtype=jnp.int32)[None, :], code, 0), axis=1
    )
    slot_q = code_q // CAP
    pieces = tuple(
        (home, inner, size // owners, start + home * (size // owners))
        for size, start, inner in zip(sizes, starts, inners)
        for home in range(owners)
    )
    ss_q = slot_q[:, None]

    for i in range(1, count):
        if i == 1:
            multiply(1, *sends[0], packed)
            features = finish(packed, kept[1])
            spread = product(
                after(scal, kept[1], *gots[0], *arrived), features, gate_tiles, up_tiles, code_q[None, :], owners, per_owner, pieces
            )
            exchange(1)
            spread = halve(spread)
            held = (spread,)
        else:
            multiply(i, *sends[i - 1], *gots[i - 2], *held)
            held = ()
            exchange(i)
    home_delta = finish(spread, kept[2])

    near_tiles = [*tiles, flat_tiles]
    all_tiles = near_tiles + [core_swap(after(t, kept[1])) for t in near_tiles]

    def finish_hidden(i, *earlier):
        each = sizes[i] // owners
        hid = activate(
            kept[i],
            cores[i],
            gots[i],
            home_delta,
            ss_q,
            after(table, *earlier),
            per_slot,
            inners[i],
            starts[i] + sizes[i] - each,
            SHORT if i == 0 else 1e9,
        )
        return hid, [y_move(hid, -k) for k in range(1, ys)]

    def join(hid, moved, *earlier):
        return jnp.concatenate([after(m, *earlier) for m in moved] + [hid])

    def finish_down(i, chip, earlier, sent=()):
        out = down(
            after(down_scal, *earlier),
            core_swap(chip),
            chip,
            down_weight,
            all_tiles,
            plan,
            ss_q,
            width_tiles,
            owners,
            per_owner,
            per_slot,
            starts[i],
            SHORT if i == count - 2 else 1e9,
        )
        blocks = out.reshape(owners, shift, sizes[i] // (owners * shift), shard_width).transpose(1, 0, 2, 3)
        gone = blocks.astype(BF)
        came = lax.all_to_all(after(gone, *sent), "tensor", 0, 0)
        own = lax.dynamic_index_in_dim(blocks, here_t, 0, keepdims=False)
        total = own
        for t in range(shift):
            total = total + jnp.where(t == here_t, 0.0, came[t].astype(F32))
        return gone, total.astype(BF)

    result = []
    hid, moved = finish_hidden(0, kept[count - 1], gots[1][0])
    chip, out = None, ()
    for i in range(1, count):
        later, moved_later = finish_hidden(i, hid, *sends[count - 1], *out)
        if i == 1:
            chip = join(hid, moved, later)
        next_chip = join(later, moved_later)
        gone, total = finish_down(i - 1, chip, (later, *result[:-1]), result[-1:])
        hid, chip, out = later, next_chip, (gone, next_chip)
        result.append(total)
    gone, total = finish_down(count - 1, chip, (gone, *result[:-1]), result[-1:])
    result.append(total)

    placed = [jnp.take(r, at_home, axis=0).reshape(-1, shard_width) for r in result]
    return jnp.concatenate(placed, axis=0)


def solution(mesh):
    return jax.shard_map(
        shards,
        mesh=mesh,
        in_specs=(
            P("groups", "delta"),
            P("delta", "tensor"),
            P("delta", "tensor"),
            P("tensor", "delta"),
            P("delta", "tensor", None, None),
            P("delta", "tensor", None, None),
            P("delta", "tensor", None, None),
            P("delta", "tensor"),
            P("delta", "tensor"),
            P("delta", "tensor"),
            P("groups"),
            P("groups"),
        ),
        out_specs=P(("groups", "tensor"), "delta"),
        check_vma=False,
    )
```

```python
import functools

import jax
import jax.numpy as jnp
from jax import lax
from jax.experimental import pallas as pl
from jax.experimental.pallas import tpu as pltpu
from jax.sharding import PartitionSpec as P

CAP = 128
CHUNKS = (2, 2)
PARTS = 2
SHORT = 120e9
VMEM = 56 * 1024 * 1024
BF = jnp.bfloat16
F32 = jnp.float32


def cost(flops, moved):
    return pl.CostEstimate(flops=int(flops), bytes_accessed=int(moved), transcendentals=0)


def whole(shape):
    zeros = (0,) * len(shape)
    return pl.BlockSpec(shape, lambda *_: zeros)


def pack_body(owners, per_owner, kinds, stride, capacity, col_tiles, scal, x, sl, ss, out, code, table):
    tile = 256
    rows, held = x.shape
    here = held // tile
    me = scal[0]
    height = table.shape[0]
    at_row = lax.broadcasted_iota(jnp.int32, (height, 128), 0)
    at_lane = lax.broadcasted_iota(jnp.int32, (height, 128), 1)
    known = jnp.zeros((height, 128), jnp.int32)
    for s in range(owners * per_owner):
        back = (s // per_owner - me + owners) % owners
        for j in range(kinds):
            place = scal[1 + owners + (back * per_owner + s % per_owner) * stride + j]
            known = jnp.where((at_row == s) & (at_lane == j), place // col_tiles, known)
            known = jnp.where((at_row == s) & (at_lane == 64 + j), place % col_tiles, known)
    table[...] = known.astype(F32).astype(BF)
    owner_l = sl[...] // per_owner
    first = lax.broadcasted_iota(jnp.int32, (rows, rows), 0)
    second = lax.broadcasted_iota(jnp.int32, (rows, rows), 1)
    ahead = ((ss[...] // per_owner) == owner_l) & (first < second)
    pos = jnp.sum(jnp.where(ahead, 1, 0), axis=0, keepdims=True)
    code[...] = sl[...] * capacity + pos
    target = pos
    for o in range(owners):
        target = target + jnp.where(owner_l == o, scal[1 + o] * capacity, 0)
    hot = lax.broadcasted_iota(jnp.int32, (owners * capacity, rows), 0) == target
    hot = jnp.where(hot, 1.0, 0.0).astype(BF)
    lanes = lax.broadcasted_iota(jnp.int32, (rows, height), 1)
    slot_hot = jnp.where(ss[...] == lanes, 1.0, 0.0).astype(BF)
    block = jnp.dot(slot_hot, table[...], preferred_element_type=F32)
    block = block - (me * here).astype(F32)
    for j in range(kinds):
        at = block[:, j : j + 1]
        picked = jnp.zeros((rows, tile), BF)
        for b in range(here):
            picked = jnp.where(at == float(b), x[:, b * tile : (b + 1) * tile], picked)
        out[:, j * tile : (j + 1) * tile] = jnp.dot(hot, picked, preferred_element_type=F32).astype(BF)


def pack(scal, x, sl, ss, owners, per_owner, kinds, stride, col_tiles):
    rows = x.shape[0]
    width = kinds * 256
    height = -(-owners * per_owner // 128) * 128
    return pl.pallas_call(
        functools.partial(pack_body, owners, per_owner, kinds, stride, CAP, col_tiles),
        grid_spec=pltpu.PrefetchScalarGridSpec(
            num_scalar_prefetch=1,
            grid=(1,),
            in_specs=[whole(x.shape), whole((1, rows)), whole((rows, 1))],
            out_specs=[whole((owners * CAP, width)), whole((1, rows)), whole((height, 128))],
        ),
        out_shape=[
            jax.ShapeDtypeStruct((owners * CAP, width), BF),
            jax.ShapeDtypeStruct((1, rows), jnp.int32),
            jax.ShapeDtypeStruct((height, 128), BF),
        ],
        compiler_params=pltpu.CompilerParams(vmem_limit_bytes=VMEM),
        cost_estimate=cost(SHORT, 4e6),
    )(scal, x, sl, ss)


def product_body(owners, per_owner, per_slot, pieces, scal, x, gt, ut, code, out):
    tile = 256
    capacity = x.shape[0]
    rows = code.shape[1]
    slot_l = code[...] // capacity
    place = lax.broadcasted_iota(jnp.int32, (capacity, rows), 0) == code[...] % capacity
    mine = place & (slot_l // per_owner == scal[0])
    slot = jnp.sum(jnp.where(mine, slot_l % per_owner + 1, 0), axis=1, keepdims=True) - 1
    hot = jnp.where(mine, 1.0, 0.0).astype(BF)
    for kind, tiles in enumerate((gt, ut)):
        for j in range(per_slot):
            at = (kind * per_slot + j) * tile
            source = x[:, at : at + tile]
            total = jnp.zeros((capacity, tile), F32)
            for s in range(per_owner):
                picked = jnp.where(slot == s, source, jnp.zeros_like(source))
                total = total + jnp.dot(picked, tiles[s, j], preferred_element_type=F32)
            spread = lax.dot_general(
                hot, total.astype(BF), (((0,), (0,)), ((), ())), preferred_element_type=F32
            ).astype(BF)
            for home, offset, size, start in pieces:
                out[home, offset : offset + size, at : at + tile] = spread[start : start + size]


def product(scal, x, gt, ut, code, owners, per_owner, pieces):
    rows = code.shape[1]
    per_slot = gt.shape[1]
    shape = (owners, rows // owners, x.shape[1])
    return pl.pallas_call(
        functools.partial(product_body, owners, per_owner, per_slot, pieces),
        grid_spec=pltpu.PrefetchScalarGridSpec(
            num_scalar_prefetch=1,
            grid=(1,),
            in_specs=[whole(x.shape), whole(gt.shape), whole(ut.shape), whole((1, rows))],
            out_specs=whole(shape),
        ),
        out_shape=jax.ShapeDtypeStruct(shape, BF),
        compiler_params=pltpu.CompilerParams(vmem_limit_bytes=VMEM),
        cost_estimate=cost(SHORT, 4e6),
    )(scal, x, gt, ut, code)


def gate_up_body(pieces, scal, *refs):
    blocks, (wg, wu, send, keep, x) = refs[:pieces], refs[pieces:]
    half = send.shape[1]

    @pl.when(pl.program_id(0) == 0)
    def _():
        each = x.shape[0] // pieces
        for i, block in enumerate(blocks):
            x[i * each : (i + 1) * each] = block[...].reshape(each, x.shape[1])

    for i, w in enumerate((wg, wu)):
        total = jnp.dot(x[...], w[...], preferred_element_type=F32)
        send[i] = total[:half].astype(send.dtype)
        keep[i] = total[half:]


def gate_up(scal, tokens, wg, wu, owners, shift, start, size, part):
    rows, depth = tokens.shape
    width = wg.shape[1] // PARTS
    block = min(1024, width)
    skip = part * (width // block)
    each = size // (owners * shift)
    first = start // (shift * each)
    view = tokens.reshape(shift, rows // (shift * each), each, depth)
    outs = pl.BlockSpec((2, size // 2, block), lambda i, s: (0, 0, i))
    weights = pl.BlockSpec((depth, block), lambda i, s: (0, skip + i))
    piece = [
        pl.BlockSpec((shift, 1, each, depth), functools.partial(lambda h, i, s: (0, first + s[h], 0, 0), h))
        for h in range(owners)
    ]
    return pl.pallas_call(
        functools.partial(gate_up_body, owners),
        grid_spec=pltpu.PrefetchScalarGridSpec(
            num_scalar_prefetch=1,
            grid=(width // block,),
            in_specs=[*piece, weights, weights],
            out_specs=[outs, outs],
            scratch_shapes=[pltpu.VMEM((size, depth), BF)],
        ),
        out_shape=[jax.ShapeDtypeStruct((2, size // 2, width), F32)] * 2,
        compiler_params=pltpu.CompilerParams(vmem_limit_bytes=VMEM),
        cost_estimate=cost(4 * size * depth * width, 4 * depth * width),
    )(scal, *[view] * owners, wg, wu)


def activate_body(per_slot, start, each, row, parts, skip, keep, core, *refs):
    gots, (delta, slot, table, out) = refs[:parts], refs[parts:]
    tile = 256
    step = pl.program_id(0)
    across = out.shape[1] // tile
    lanes = lax.broadcasted_iota(jnp.int32, (each, table.shape[0]), 1)
    hot = jnp.where(slot[row : row + each] == lanes, 1.0, 0.0).astype(BF)
    where = jnp.dot(hot, table[...], preferred_element_type=F32) - (skip + step * across).astype(F32)
    at = [where[:, 64 + k : 65 + k] for k in range(2 * per_slot)]
    adds = [
        delta[start : start + each, k * tile : (k + 1) * tile].astype(F32) for k in range(2 * per_slot)
    ]
    for b in range(across):
        cols = slice(b * tile, (b + 1) * tile)
        sums = []
        for kind in range(2):
            got = gots[0][kind, :, cols] if parts == 1 else gots[kind][0, :, cols]
            total = keep[kind, :, cols] + core[kind, :, cols] + got.astype(F32)
            for k in range(kind * per_slot, (kind + 1) * per_slot):
                total = total + jnp.where(at[k] == float(b), adds[k], 0.0)
            sums.append(total)
        gate, up = sums
        out[:, cols] = (gate / (1.0 + jnp.exp(-gate)) * up).astype(BF)


def activate(keep, core, gots, delta, slot, table, per_slot, start, row, skip, flops):
    each, width = gots[0].shape[1:]
    last = keep.shape[1] // each - 1
    block = min(2048, width)
    own = pl.BlockSpec((2, each, block), lambda i: (0, last, i))
    taken = [pl.BlockSpec((g.shape[0], each, block), lambda i: (0, 0, i)) for g in gots]
    return pl.pallas_call(
        functools.partial(activate_body, per_slot, start, each, row, len(gots), skip),
        grid=(width // block,),
        in_specs=[own, own, *taken, whole(delta.shape), whole(slot.shape), whole(table.shape)],
        out_specs=pl.BlockSpec((each, block), lambda i: (0, i)),
        out_shape=jax.ShapeDtypeStruct((each, width), BF),
        compiler_params=pltpu.CompilerParams(vmem_limit_bytes=VMEM),
        cost_estimate=cost(flops, 24 * each * width),
    )(keep, core, *gots, delta, slot, table)


def down_body(width_tiles, here, plan, owners, per_owner, per_slot, start, scal, *refs):
    fars, nears, (w, *refs) = refs[:PARTS], refs[PARTS : 2 * PARTS], refs[2 * PARTS :]
    tiles, (slot, out, hid, listed, number) = refs[: len(plan)], refs[len(plan) :]
    tile = 256
    across = out.shape[1] // tile
    step = pl.program_id(0)
    half, wide = fars[0].shape
    stride = 3 * per_slot
    patterns = scal.shape[0] - owners * per_owner * stride

    @pl.when(step == 0)
    def _():
        for p in range(PARTS):
            hid[:half, p * wide : (p + 1) * wide] = fars[p][...]
            hid[half:, p * wide : (p + 1) * wide] = nears[p][...]
        me = scal[0]
        for r, (base, run) in enumerate(plan):
            for at in range(number.shape[1]):
                number[r, at] = 0

            def one(i, carry):
                local = i // per_slot
                which = scal[base + local // run] + local % run
                back = (which // per_owner - me + owners) % owners
                row = back * per_owner + which % per_owner
                place = scal[patterns + row * stride + 2 * per_slot + i % per_slot]
                block = place % width_tiles - me * here

                @pl.when((block >= 0) & (block < here))
                def _():
                    at = block // across
                    n = number[r, at]
                    listed[r * number.shape[1] + at, 4 * n] = i
                    listed[r * number.shape[1] + at, 4 * n + 1] = which
                    listed[r * number.shape[1] + at, 4 * n + 2] = place // width_tiles
                    listed[r * number.shape[1] + at, 4 * n + 3] = block % across
                    number[r, at] = n + 1

                return carry

            lax.fori_loop(0, tiles[r].shape[0], one, 0)

    out[...] = jnp.dot(hid[...], w[...], preferred_element_type=F32)
    for r in range(len(plan)):
        entry = r * number.shape[1] + step

        def add(n, carry):
            i = listed[entry, 4 * n]
            col = pl.multiple_of(listed[entry, 4 * n + 2] * tile, tile)
            source = hid[:, pl.ds(col, tile)]
            hit = slot[start : start + 2 * half] == listed[entry, 4 * n + 1]
            picked = jnp.where(hit, source, jnp.zeros_like(source))
            cols = pl.ds(pl.multiple_of(listed[entry, 4 * n + 3] * tile, tile), tile)
            out[:, cols] = out[:, cols] + jnp.dot(picked, tiles[r][i], preferred_element_type=F32)
            return carry

        lax.fori_loop(0, number[r, step], add, 0)


def down(scal, fars, nears, w, tiles, plan, slot, width_tiles, owners, per_owner, per_slot, start, flops):
    rows, depth = 2 * fars[0].shape[0], w.shape[0]
    width = w.shape[1]
    block = min(512, width)
    steps = width // block
    most = max(t.shape[0] for t in tiles)
    return pl.pallas_call(
        functools.partial(down_body, width_tiles, width // 256, plan, owners, per_owner, per_slot, start),
        grid_spec=pltpu.PrefetchScalarGridSpec(
            num_scalar_prefetch=1,
            grid=(steps,),
            in_specs=[
                *[whole(f.shape) for f in (*fars, *nears)],
                pl.BlockSpec((depth, block), lambda i, s: (0, i)),
                *[whole(t.shape) for t in tiles],
                whole(slot.shape),
            ],
            out_specs=pl.BlockSpec((rows, block), lambda i, s: (0, i)),
            scratch_shapes=[
                pltpu.VMEM((rows, depth), BF),
                pltpu.SMEM((len(tiles) * steps, 4 * most), jnp.int32),
                pltpu.SMEM((len(tiles), steps), jnp.int32),
            ],
        ),
        out_shape=jax.ShapeDtypeStruct((rows, width), F32),
        compiler_params=pltpu.CompilerParams(vmem_limit_bytes=VMEM),
        cost_estimate=cost(flops, 1e6),
    )(scal, *fars, *nears, w, *tiles, slot)


def shards(
    tokens,
    gate_weight,
    up_weight,
    down_weight,
    gate_tiles,
    up_tiles,
    down_tiles,
    gate_pattern,
    up_pattern,
    down_pattern,
    row_variant,
    variant_slot,
):
    owners = lax.axis_size("delta")
    shift = lax.axis_size("tensor")
    groups = lax.axis_size("groups")
    me = lax.axis_index("delta")
    here_t = lax.axis_index("tensor")
    my_core, my_y = me % 2, me // 2
    ys = owners // 2
    per_owner, per_slot = gate_pattern.shape
    slots = owners * per_owner
    rows, shard_width = tokens.shape
    width = gate_weight.shape[1]
    col_tiles = width // 256
    width_tiles = shard_width * owners // 256
    unit = rows // sum(CHUNKS)
    sizes = [unit * c for c in CHUNKS]

    def core_swap(x):
        return lax.ppermute(x, "delta", [(i, i ^ 1) for i in range(owners)])

    def y_move(x, k):
        return lax.ppermute(x, "delta", [(i, (i + 2 * k) % owners) for i in range(owners)])

    order_y = [(my_y + k) % ys for k in range(1, ys)] + [my_y]
    homes = jnp.stack([y * 2 + c for c in (1 - my_core, my_core) for y in order_y]).astype(jnp.int32)

    row_ids = []
    offset = 0
    for size in sizes:
        each = size // (owners * shift)
        ids = (
            jnp.arange(shift, dtype=jnp.int32)[None, :, None] * (rows // shift)
            + offset
            + homes[:, None, None] * each
            + jnp.arange(each, dtype=jnp.int32)[None, None, :]
        )
        row_ids.append(ids.reshape(-1))
        offset += owners * each
    row_of = jnp.concatenate(row_ids)

    hit = row_variant[:, None] == jnp.arange(variant_slot.shape[0], dtype=jnp.int32)[None, :]
    slot_rows = jnp.sum(jnp.where(hit, variant_slot[None, :], 0), axis=1)

    def after(x, *earlier):
        return lax.optimization_barrier((x, *earlier))[0]

    kinds = 2 * per_slot
    own = jnp.concatenate([gate_pattern, up_pattern, down_pattern], axis=1)
    seen = [own] + [
        lax.ppermute(own, "delta", [(i, (i - k) % owners) for i in range(owners)]) for k in range(1, owners)
    ]
    patterns = jnp.concatenate([s.reshape(-1) for s in seen])
    at_home = jnp.stack(
        [((d // 2) - my_y - 1) % ys + ys * jnp.where(d % 2 == my_core, 1, 0) for d in range(owners)]
    ).astype(jnp.int32)
    scal = jnp.concatenate([me.astype(jnp.int32)[None], at_home, patterns])

    flat_tiles = down_tiles.reshape(-1, 256, 256)
    if groups == 2 and per_owner % 2 == 0:
        part = per_owner // 2
        mine_g = lax.axis_index("groups")
        piece = lax.dynamic_slice_in_dim(flat_tiles, mine_g * part * per_slot, part * per_slot, 0)
        halves = [mine_g * part, (1 - mine_g) * part]
    else:
        part, piece, halves = per_owner, flat_tiles, [0]
    from_y = jnp.concatenate([y_move(piece, -k) for k in range(1, ys)])
    tiles = [from_y]
    if len(halves) == 2:
        tiles.append(lax.ppermute(from_y, "groups", [(0, 1), (1, 0)]))
    arrived = tuple(tiles)
    firsts, plan = [], []
    for core in (my_core, 1 - my_core):
        for first in halves:
            plan.append((1 + len(firsts), part))
            firsts.extend((y * 2 + core) * per_owner + first for y in order_y[:-1])
        plan.append((1 + len(firsts), per_owner))
        firsts.append((my_y * 2 + core) * per_owner)
    plan = tuple(plan)
    down_scal = jnp.concatenate([jnp.stack([me] + firsts).astype(jnp.int32), patterns])

    starts = [sum(sizes[:i]) for i in range(len(sizes))]
    inners = [s // owners for s in starts]
    kept, cores, sends, gots = {}, {}, {}, {}

    def multiply(u, *earlier):
        i, part = u
        send, kept[u] = gate_up(
            after(homes, *earlier), tokens, gate_weight, up_weight, owners, shift, starts[i], sizes[i], part
        )
        cores[u] = core_swap(send)

    def exchange(u, *earlier):
        each = sizes[u[0]] // owners
        sends[u], got = [], None
        own = after(kept[u], *earlier)
        for k in range(1, ys):
            rows_k = slice((k - 1) * each, k * each)
            sends[u].append((own[:, rows_k] + cores[u][:, rows_k]).astype(BF))
            moved = y_move(sends[u][-1], k)
            if ys > 2:
                moved = moved.astype(F32)
            got = moved if got is None else got + moved
        gots[u] = [got]

    def halve(x):
        half = owners // 2
        return x[half:] + core_swap(x[:half])

    def finish(x, *earlier):
        total = after(x[ys - 1], *earlier)
        for k in range(1, ys):
            total = total + y_move(x[k - 1], k)
        return total

    ahead, second, third, fourth = (0, 0), (0, 1), (1, 0), (1, 1)
    multiply(ahead)
    packed, code, table = pack(
        after(scal, kept[ahead], from_y),
        tokens,
        slot_rows[None, :],
        slot_rows[:, None],
        owners,
        per_owner,
        kinds,
        3 * per_slot,
        col_tiles,
    )
    exchange(ahead)
    packed = halve(packed.reshape(owners, CAP, -1))
    code_q = jnp.sum(
        jnp.where(row_of[:, None] == jnp.arange(rows, dtype=jnp.int32)[None, :], code, 0), axis=1
    )
    slot_q = code_q // CAP
    pieces = tuple(
        (home, inner, size // owners, start + home * (size // owners))
        for size, start, inner in zip(sizes, starts, inners)
        for home in range(owners)
    )
    ss_q = slot_q[:, None]

    multiply(second, *sends[ahead], packed)
    features = finish(packed, kept[second])
    spread = product(
        after(scal, kept[second], *gots[ahead], *arrived),
        features,
        gate_tiles,
        up_tiles,
        code_q[None, :],
        owners,
        per_owner,
        pieces,
    )
    exchange(second)
    spread = halve(spread)
    multiply(third, *sends[second], spread)
    home_delta = finish(spread, kept[third])

    near_tiles = [*tiles, flat_tiles]
    all_tiles = near_tiles + [core_swap(after(t, kept[second])) for t in near_tiles]

    def finish_hidden(u, flops, *earlier):
        i, part = u
        each = sizes[i] // owners
        hid = activate(
            kept[u],
            cores[u],
            gots[u],
            home_delta,
            ss_q,
            after(table, *earlier),
            per_slot,
            inners[i],
            starts[i] + sizes[i] - each,
            part * (col_tiles // PARTS),
            flops,
        )
        return hid, [y_move(hid, -k) for k in range(1, ys)]

    def join(hid, moved, *earlier):
        return jnp.concatenate([after(m, *earlier) for m in moved] + [hid])

    def finish_down(i, chips, earlier, sent=None):
        out = down(
            after(down_scal, *earlier),
            [core_swap(c) for c in chips],
            chips,
            down_weight,
            all_tiles,
            plan,
            ss_q,
            width_tiles,
            owners,
            per_owner,
            per_slot,
            starts[i],
            1e9,
        )
        blocks = out.reshape(owners, shift, sizes[i] // (owners * shift), shard_width).transpose(1, 0, 2, 3)
        total = lax.dynamic_index_in_dim(blocks, here_t, 0, keepdims=False)
        came = []
        for k in range(1, shift):
            gone = lax.dynamic_index_in_dim(blocks, (here_t + k) % shift, 0, keepdims=False).astype(BF)
            if sent is not None:
                gone = after(gone, sent[k - 1])
            came.append(lax.ppermute(gone, "tensor", [(j, (j + k) % shift) for j in range(shift)]))
            total = total + came[-1].astype(F32)
        return out, came, total.astype(BF)

    hid_a, moved_a = finish_hidden(ahead, SHORT, kept[third], *gots[second])
    exchange(third, hid_a)
    multiply(fourth, *sends[third], hid_a)
    hid_b, moved_b = finish_hidden(second, SHORT, kept[fourth], *gots[third], *moved_a)
    exchange(fourth, hid_b)
    hid_c, moved_c = finish_hidden(third, 1e9, hid_b, *sends[fourth])
    hid_d, moved_d = finish_hidden(fourth, 1e9, hid_c)
    first = [join(hid_a, moved_a, hid_b), join(hid_b, moved_b, hid_c)]
    last = [join(hid_c, moved_c, hid_d), join(hid_d, moved_d)]
    out, came, total = finish_down(0, first, (hid_d,))
    result = [total]
    out, came, total = finish_down(1, last, (out,), came)
    result.append(total)

    placed = [jnp.take(r, at_home, axis=0).reshape(-1, shard_width) for r in result]
    return jnp.concatenate(placed, axis=0)


def solution(mesh):
    return jax.shard_map(
        shards,
        mesh=mesh,
        in_specs=(
            P("groups", "delta"),
            P("delta", "tensor"),
            P("delta", "tensor"),
            P("tensor", "delta"),
            P("delta", "tensor", None, None),
            P("delta", "tensor", None, None),
            P("delta", "tensor", None, None),
            P("delta", "tensor"),
            P("delta", "tensor"),
            P("delta", "tensor"),
            P("groups"),
            P("groups"),
        ),
        out_specs=P(("groups", "tensor"), "delta"),
        check_vma=False,
    )
```

```python
import functools

import jax
import jax.numpy as jnp
from jax import lax
from jax.experimental import pallas as pl
from jax.experimental.pallas import tpu as pltpu
from jax.sharding import PartitionSpec as P

CAP = 128
CHUNKS = (2, 2)
PARTS = 2
SHORT = 120e9
VMEM = 56 * 1024 * 1024
BF = jnp.bfloat16
F32 = jnp.float32


def cost(flops, moved):
    return pl.CostEstimate(flops=int(flops), bytes_accessed=int(moved), transcendentals=0)


def whole(shape):
    zeros = (0,) * len(shape)
    return pl.BlockSpec(shape, lambda *_: zeros)


def pack_body(owners, per_owner, kinds, stride, capacity, col_tiles, scal, x, sl, ss, out, code, table):
    tile = 256
    rows, held = x.shape
    here = held // tile
    me = scal[0]
    height = table.shape[0]
    at_row = lax.broadcasted_iota(jnp.int32, (height, 128), 0)
    at_lane = lax.broadcasted_iota(jnp.int32, (height, 128), 1)
    known = jnp.zeros((height, 128), jnp.int32)
    for s in range(owners * per_owner):
        back = (s // per_owner - me + owners) % owners
        for j in range(kinds):
            place = scal[1 + owners + (back * per_owner + s % per_owner) * stride + j]
            known = jnp.where((at_row == s) & (at_lane == j), place // col_tiles, known)
            known = jnp.where((at_row == s) & (at_lane == 64 + j), place % col_tiles, known)
    table[...] = known.astype(F32).astype(BF)
    owner_l = sl[...] // per_owner
    first = lax.broadcasted_iota(jnp.int32, (rows, rows), 0)
    second = lax.broadcasted_iota(jnp.int32, (rows, rows), 1)
    ahead = ((ss[...] // per_owner) == owner_l) & (first < second)
    pos = jnp.sum(jnp.where(ahead, 1, 0), axis=0, keepdims=True)
    code[...] = sl[...] * capacity + pos
    target = pos
    for o in range(owners):
        target = target + jnp.where(owner_l == o, scal[1 + o] * capacity, 0)
    hot = lax.broadcasted_iota(jnp.int32, (owners * capacity, rows), 0) == target
    hot = jnp.where(hot, 1.0, 0.0).astype(BF)
    lanes = lax.broadcasted_iota(jnp.int32, (rows, height), 1)
    slot_hot = jnp.where(ss[...] == lanes, 1.0, 0.0).astype(BF)
    block = jnp.dot(slot_hot, table[...], preferred_element_type=F32)
    block = block - (me * here).astype(F32)
    for j in range(kinds):
        at = block[:, j : j + 1]
        picked = jnp.zeros((rows, tile), BF)
        for b in range(here):
            picked = jnp.where(at == float(b), x[:, b * tile : (b + 1) * tile], picked)
        out[:, j * tile : (j + 1) * tile] = jnp.dot(hot, picked, preferred_element_type=F32).astype(BF)


def pack(scal, x, sl, ss, owners, per_owner, kinds, stride, col_tiles):
    rows = x.shape[0]
    width = kinds * 256
    height = -(-owners * per_owner // 128) * 128
    return pl.pallas_call(
        functools.partial(pack_body, owners, per_owner, kinds, stride, CAP, col_tiles),
        grid_spec=pltpu.PrefetchScalarGridSpec(
            num_scalar_prefetch=1,
            grid=(1,),
            in_specs=[whole(x.shape), whole((1, rows)), whole((rows, 1))],
            out_specs=[whole((owners * CAP, width)), whole((1, rows)), whole((height, 128))],
        ),
        out_shape=[
            jax.ShapeDtypeStruct((owners * CAP, width), BF),
            jax.ShapeDtypeStruct((1, rows), jnp.int32),
            jax.ShapeDtypeStruct((height, 128), BF),
        ],
        compiler_params=pltpu.CompilerParams(vmem_limit_bytes=VMEM),
        cost_estimate=cost(SHORT, 4e6),
    )(scal, x, sl, ss)


def product_body(owners, per_owner, per_slot, pieces, scal, x, gt, ut, code, out):
    tile = 256
    capacity = x.shape[0]
    rows = code.shape[1]
    slot_l = code[...] // capacity
    place = lax.broadcasted_iota(jnp.int32, (capacity, rows), 0) == code[...] % capacity
    mine = place & (slot_l // per_owner == scal[0])
    slot = jnp.sum(jnp.where(mine, slot_l % per_owner + 1, 0), axis=1, keepdims=True) - 1
    hot = jnp.where(mine, 1.0, 0.0).astype(BF)
    for kind, tiles in enumerate((gt, ut)):
        for j in range(per_slot):
            at = (kind * per_slot + j) * tile
            source = x[:, at : at + tile]
            total = jnp.zeros((capacity, tile), F32)
            for s in range(per_owner):
                picked = jnp.where(slot == s, source, jnp.zeros_like(source))
                total = total + jnp.dot(picked, tiles[s, j], preferred_element_type=F32)
            spread = lax.dot_general(
                hot, total.astype(BF), (((0,), (0,)), ((), ())), preferred_element_type=F32
            ).astype(BF)
            for home, offset, size, start in pieces:
                out[home, offset : offset + size, at : at + tile] = spread[start : start + size]


def product(scal, x, gt, ut, code, owners, per_owner, pieces):
    rows = code.shape[1]
    per_slot = gt.shape[1]
    shape = (owners, rows // owners, x.shape[1])
    return pl.pallas_call(
        functools.partial(product_body, owners, per_owner, per_slot, pieces),
        grid_spec=pltpu.PrefetchScalarGridSpec(
            num_scalar_prefetch=1,
            grid=(1,),
            in_specs=[whole(x.shape), whole(gt.shape), whole(ut.shape), whole((1, rows))],
            out_specs=whole(shape),
        ),
        out_shape=jax.ShapeDtypeStruct(shape, BF),
        compiler_params=pltpu.CompilerParams(vmem_limit_bytes=VMEM),
        cost_estimate=cost(SHORT, 4e6),
    )(scal, x, gt, ut, code)


def gate_up_body(pieces, scal, *refs):
    blocks, (wg, wu, send, keep, x) = refs[:pieces], refs[pieces:]
    half = send.shape[1]

    @pl.when(pl.program_id(0) == 0)
    def _():
        each = x.shape[0] // pieces
        for i, block in enumerate(blocks):
            x[i * each : (i + 1) * each] = block[...].reshape(each, x.shape[1])

    for i, w in enumerate((wg, wu)):
        total = jnp.dot(x[...], w[...], preferred_element_type=F32)
        send[i] = total[:half].astype(send.dtype)
        keep[i] = total[half:]


def gate_up(scal, tokens, wg, wu, owners, shift, start, size, part):
    rows, depth = tokens.shape
    width = wg.shape[1] // PARTS
    block = min(1024, width)
    skip = part * (width // block)
    each = size // (owners * shift)
    first = start // (shift * each)
    view = tokens.reshape(shift, rows // (shift * each), each, depth)
    outs = pl.BlockSpec((2, size // 2, block), lambda i, s: (0, 0, i))
    weights = pl.BlockSpec((depth, block), lambda i, s: (0, skip + i))
    piece = [
        pl.BlockSpec((shift, 1, each, depth), functools.partial(lambda h, i, s: (0, first + s[h], 0, 0), h))
        for h in range(owners)
    ]
    return pl.pallas_call(
        functools.partial(gate_up_body, owners),
        grid_spec=pltpu.PrefetchScalarGridSpec(
            num_scalar_prefetch=1,
            grid=(width // block,),
            in_specs=[*piece, weights, weights],
            out_specs=[outs, outs],
            scratch_shapes=[pltpu.VMEM((size, depth), BF)],
        ),
        out_shape=[jax.ShapeDtypeStruct((2, size // 2, width), F32)] * 2,
        compiler_params=pltpu.CompilerParams(vmem_limit_bytes=VMEM),
        cost_estimate=cost(4 * size * depth * width, 4 * depth * width),
    )(scal, *[view] * owners, wg, wu)


def total_body(order, *refs):
    total = refs[0][...]
    for ref in refs[1:-1]:
        total = total + ref[...]
    refs[-1][...] = total


def total_of(order, parts):
    shape = parts[0].shape
    return pl.pallas_call(
        total_body,
        grid_spec=pltpu.PrefetchScalarGridSpec(
            num_scalar_prefetch=1,
            grid=(1,),
            in_specs=[whole(shape)] * len(parts),
            out_specs=whole(shape),
        ),
        out_shape=jax.ShapeDtypeStruct(shape, parts[0].dtype),
        compiler_params=pltpu.CompilerParams(vmem_limit_bytes=VMEM),
        cost_estimate=cost(SHORT, 1e6),
    )(order, *parts)


def activate_body(per_slot, start, each, row, parts, skip, keep, core, *refs):
    gots, (delta, slot, table, out) = refs[:parts], refs[parts:]
    tile = 256
    step = pl.program_id(0)
    across = out.shape[1] // tile
    lanes = lax.broadcasted_iota(jnp.int32, (each, table.shape[0]), 1)
    hot = jnp.where(slot[row : row + each] == lanes, 1.0, 0.0).astype(BF)
    where = jnp.dot(hot, table[...], preferred_element_type=F32) - (skip + step * across).astype(F32)
    at = [where[:, 64 + k : 65 + k] for k in range(2 * per_slot)]
    adds = [
        delta[start : start + each, k * tile : (k + 1) * tile].astype(F32) for k in range(2 * per_slot)
    ]
    for b in range(across):
        cols = slice(b * tile, (b + 1) * tile)
        sums = []
        for kind in range(2):
            got = gots[0][kind, :, cols] if parts == 1 else gots[kind][0, :, cols]
            total = keep[kind, :, cols] + core[kind, :, cols] + got.astype(F32)
            for k in range(kind * per_slot, (kind + 1) * per_slot):
                total = total + jnp.where(at[k] == float(b), adds[k], 0.0)
            sums.append(total)
        gate, up = sums
        out[:, cols] = (gate / (1.0 + jnp.exp(-gate)) * up).astype(BF)


def activate(keep, core, gots, delta, slot, table, per_slot, start, row, skip, flops):
    each, width = gots[0].shape[1:]
    last = keep.shape[1] // each - 1
    block = min(2048, width)
    own = pl.BlockSpec((2, each, block), lambda i: (0, last, i))
    taken = [pl.BlockSpec((g.shape[0], each, block), lambda i: (0, 0, i)) for g in gots]
    return pl.pallas_call(
        functools.partial(activate_body, per_slot, start, each, row, len(gots), skip),
        grid=(width // block,),
        in_specs=[own, own, *taken, whole(delta.shape), whole(slot.shape), whole(table.shape)],
        out_specs=pl.BlockSpec((each, block), lambda i: (0, i)),
        out_shape=jax.ShapeDtypeStruct((each, width), BF),
        compiler_params=pltpu.CompilerParams(vmem_limit_bytes=VMEM),
        cost_estimate=cost(flops, 24 * each * width),
    )(keep, core, *gots, delta, slot, table)


def down_body(width_tiles, here, plan, owners, per_owner, per_slot, start, scal, *refs):
    fars, nears, (w, *refs) = refs[:PARTS], refs[PARTS : 2 * PARTS], refs[2 * PARTS :]
    tiles, (slot, out, hid, listed, number) = refs[: len(plan)], refs[len(plan) :]
    tile = 256
    across = out.shape[1] // tile
    step = pl.program_id(0)
    half, wide = fars[0].shape
    stride = 3 * per_slot
    patterns = scal.shape[0] - owners * per_owner * stride

    @pl.when(step == 0)
    def _():
        for p in range(PARTS):
            hid[:half, p * wide : (p + 1) * wide] = fars[p][...]
            hid[half:, p * wide : (p + 1) * wide] = nears[p][...]
        me = scal[0]
        for r, (base, run) in enumerate(plan):
            for at in range(number.shape[1]):
                number[r, at] = 0

            def one(i, carry):
                local = i // per_slot
                which = scal[base + local // run] + local % run
                back = (which // per_owner - me + owners) % owners
                row = back * per_owner + which % per_owner
                place = scal[patterns + row * stride + 2 * per_slot + i % per_slot]
                block = place % width_tiles - me * here

                @pl.when((block >= 0) & (block < here))
                def _():
                    at = block // across
                    n = number[r, at]
                    listed[r * number.shape[1] + at, 4 * n] = i
                    listed[r * number.shape[1] + at, 4 * n + 1] = which
                    listed[r * number.shape[1] + at, 4 * n + 2] = place // width_tiles
                    listed[r * number.shape[1] + at, 4 * n + 3] = block % across
                    number[r, at] = n + 1

                return carry

            lax.fori_loop(0, tiles[r].shape[0], one, 0)

    out[...] = jnp.dot(hid[...], w[...], preferred_element_type=F32)
    for r in range(len(plan)):
        entry = r * number.shape[1] + step

        def add(n, carry):
            i = listed[entry, 4 * n]
            col = pl.multiple_of(listed[entry, 4 * n + 2] * tile, tile)
            source = hid[:, pl.ds(col, tile)]
            hit = slot[start : start + 2 * half] == listed[entry, 4 * n + 1]
            picked = jnp.where(hit, source, jnp.zeros_like(source))
            cols = pl.ds(pl.multiple_of(listed[entry, 4 * n + 3] * tile, tile), tile)
            out[:, cols] = out[:, cols] + jnp.dot(picked, tiles[r][i], preferred_element_type=F32)
            return carry

        lax.fori_loop(0, number[r, step], add, 0)


def down(scal, fars, nears, w, tiles, plan, slot, width_tiles, owners, per_owner, per_slot, start, flops):
    rows, depth = 2 * fars[0].shape[0], w.shape[0]
    width = w.shape[1]
    block = min(512, width)
    steps = width // block
    most = max(t.shape[0] for t in tiles)
    return pl.pallas_call(
        functools.partial(down_body, width_tiles, width // 256, plan, owners, per_owner, per_slot, start),
        grid_spec=pltpu.PrefetchScalarGridSpec(
            num_scalar_prefetch=1,
            grid=(steps,),
            in_specs=[
                *[whole(f.shape) for f in (*fars, *nears)],
                pl.BlockSpec((depth, block), lambda i, s: (0, i)),
                *[whole(t.shape) for t in tiles],
                whole(slot.shape),
            ],
            out_specs=pl.BlockSpec((rows, block), lambda i, s: (0, i)),
            scratch_shapes=[
                pltpu.VMEM((rows, depth), BF),
                pltpu.SMEM((len(tiles) * steps, 4 * most), jnp.int32),
                pltpu.SMEM((len(tiles), steps), jnp.int32),
            ],
        ),
        out_shape=jax.ShapeDtypeStruct((rows, width), F32),
        compiler_params=pltpu.CompilerParams(vmem_limit_bytes=VMEM),
        cost_estimate=cost(flops, 1e6),
    )(scal, *fars, *nears, w, *tiles, slot)


def shards(
    tokens,
    gate_weight,
    up_weight,
    down_weight,
    gate_tiles,
    up_tiles,
    down_tiles,
    gate_pattern,
    up_pattern,
    down_pattern,
    row_variant,
    variant_slot,
):
    owners = lax.axis_size("delta")
    shift = lax.axis_size("tensor")
    groups = lax.axis_size("groups")
    me = lax.axis_index("delta")
    here_t = lax.axis_index("tensor")
    my_core, my_y = me % 2, me // 2
    ys = owners // 2
    per_owner, per_slot = gate_pattern.shape
    slots = owners * per_owner
    rows, shard_width = tokens.shape
    width = gate_weight.shape[1]
    col_tiles = width // 256
    width_tiles = shard_width * owners // 256
    unit = rows // sum(CHUNKS)
    sizes = [unit * c for c in CHUNKS]

    def core_swap(x):
        return lax.ppermute(x, "delta", [(i, i ^ 1) for i in range(owners)])

    def y_move(x, k):
        return lax.ppermute(x, "delta", [(i, (i + 2 * k) % owners) for i in range(owners)])

    order_y = [(my_y + k) % ys for k in range(1, ys)] + [my_y]
    homes = jnp.stack([y * 2 + c for c in (1 - my_core, my_core) for y in order_y]).astype(jnp.int32)

    row_ids = []
    offset = 0
    for size in sizes:
        each = size // (owners * shift)
        ids = (
            jnp.arange(shift, dtype=jnp.int32)[None, :, None] * (rows // shift)
            + offset
            + homes[:, None, None] * each
            + jnp.arange(each, dtype=jnp.int32)[None, None, :]
        )
        row_ids.append(ids.reshape(-1))
        offset += owners * each
    row_of = jnp.concatenate(row_ids)

    hit = row_variant[:, None] == jnp.arange(variant_slot.shape[0], dtype=jnp.int32)[None, :]
    slot_rows = jnp.sum(jnp.where(hit, variant_slot[None, :], 0), axis=1)

    def after(x, *earlier):
        return lax.optimization_barrier((x, *earlier))[0]

    kinds = 2 * per_slot
    own = jnp.concatenate([gate_pattern, up_pattern, down_pattern], axis=1)
    seen = [own] + [
        lax.ppermute(own, "delta", [(i, (i - k) % owners) for i in range(owners)]) for k in range(1, owners)
    ]
    patterns = jnp.concatenate([s.reshape(-1) for s in seen])
    at_home = jnp.stack(
        [((d // 2) - my_y - 1) % ys + ys * jnp.where(d % 2 == my_core, 1, 0) for d in range(owners)]
    ).astype(jnp.int32)
    scal = jnp.concatenate([me.astype(jnp.int32)[None], at_home, patterns])

    flat_tiles = down_tiles.reshape(-1, 256, 256)
    if groups == 2 and per_owner % 2 == 0:
        part = per_owner // 2
        mine_g = lax.axis_index("groups")
        piece = lax.dynamic_slice_in_dim(flat_tiles, mine_g * part * per_slot, part * per_slot, 0)
        halves = [mine_g * part, (1 - mine_g) * part]
    else:
        part, piece, halves = per_owner, flat_tiles, [0]
    from_y = jnp.concatenate([y_move(piece, -k) for k in range(1, ys)])
    tiles = [from_y]
    if len(halves) == 2:
        tiles.append(lax.ppermute(from_y, "groups", [(0, 1), (1, 0)]))
    arrived = tuple(tiles)
    firsts, plan = [], []
    for core in (my_core, 1 - my_core):
        for first in halves:
            plan.append((1 + len(firsts), part))
            firsts.extend((y * 2 + core) * per_owner + first for y in order_y[:-1])
        plan.append((1 + len(firsts), per_owner))
        firsts.append((my_y * 2 + core) * per_owner)
    plan = tuple(plan)
    down_scal = jnp.concatenate([jnp.stack([me] + firsts).astype(jnp.int32), patterns])

    starts = [sum(sizes[:i]) for i in range(len(sizes))]
    inners = [s // owners for s in starts]
    kept, cores, sends, gots = {}, {}, {}, {}

    def multiply(u, *earlier):
        i, part = u
        send, kept[u] = gate_up(
            after(homes, *earlier), tokens, gate_weight, up_weight, owners, shift, starts[i], sizes[i], part
        )
        cores[u] = core_swap(send)

    def exchange(u, *earlier):
        each = sizes[u[0]] // owners
        sends[u], got = [], None
        own = after(kept[u], *earlier)
        for k in range(1, ys):
            rows_k = slice((k - 1) * each, k * each)
            sends[u].append((own[:, rows_k] + cores[u][:, rows_k]).astype(BF))
            moved = y_move(sends[u][-1], k)
            if ys > 2:
                moved = moved.astype(F32)
            got = moved if got is None else got + moved
        gots[u] = [got]

    def halve(x):
        half = owners // 2
        return x[half:] + core_swap(x[:half])

    def finish(x, *earlier):
        return total_of(after(homes, *earlier), [x[ys - 1]] + [y_move(x[k - 1], k) for k in range(1, ys)])

    ahead, second, third, fourth = (0, 0), (0, 1), (1, 0), (1, 1)
    multiply(ahead)
    packed, code, table = pack(
        after(scal, kept[ahead], from_y),
        tokens,
        slot_rows[None, :],
        slot_rows[:, None],
        owners,
        per_owner,
        kinds,
        3 * per_slot,
        col_tiles,
    )
    exchange(ahead)
    packed = halve(packed.reshape(owners, CAP, -1))
    code_q = jnp.sum(
        jnp.where(row_of[:, None] == jnp.arange(rows, dtype=jnp.int32)[None, :], code, 0), axis=1
    )
    slot_q = code_q // CAP
    pieces = tuple(
        (home, inner, size // owners, start + home * (size // owners))
        for size, start, inner in zip(sizes, starts, inners)
        for home in range(owners)
    )
    ss_q = slot_q[:, None]

    multiply(second, *sends[ahead], packed)
    features = finish(packed, kept[second], *gots[ahead])
    exchange(second, features)
    spread = product(
        after(scal, *sends[second], *arrived),
        features,
        gate_tiles,
        up_tiles,
        code_q[None, :],
        owners,
        per_owner,
        pieces,
    )
    spread = halve(spread)
    multiply(third, *sends[second], spread)
    home_delta = finish(spread, kept[third])
    exchange(third, home_delta)

    near_tiles = [*tiles, flat_tiles]
    all_tiles = near_tiles + [core_swap(after(t, kept[second])) for t in near_tiles]

    def finish_hidden(u, flops, *earlier):
        i, part = u
        each = sizes[i] // owners
        hid = activate(
            kept[u],
            cores[u],
            gots[u],
            home_delta,
            ss_q,
            after(table, *earlier),
            per_slot,
            inners[i],
            starts[i] + sizes[i] - each,
            part * (col_tiles // PARTS),
            flops,
        )
        return hid, [y_move(hid, -k) for k in range(1, ys)]

    def join(hid, moved, *earlier):
        return jnp.concatenate([after(m, *earlier) for m in moved] + [hid])

    def finish_down(i, chips, earlier, sent=None):
        out = down(
            after(down_scal, *earlier),
            [core_swap(c) for c in chips],
            chips,
            down_weight,
            all_tiles,
            plan,
            ss_q,
            width_tiles,
            owners,
            per_owner,
            per_slot,
            starts[i],
            1e9,
        )
        blocks = out.reshape(owners, shift, sizes[i] // (owners * shift), shard_width).transpose(1, 0, 2, 3)
        total = lax.dynamic_index_in_dim(blocks, here_t, 0, keepdims=False)
        came = []
        for k in range(1, shift):
            gone = lax.dynamic_index_in_dim(blocks, (here_t + k) % shift, 0, keepdims=False).astype(BF)
            if sent is not None:
                gone = after(gone, sent[k - 1])
            came.append(lax.ppermute(gone, "tensor", [(j, (j + k) % shift) for j in range(shift)]))
            total = total + came[-1].astype(F32)
        return out, came, total.astype(BF)

    hid_a, moved_a = finish_hidden(ahead, 1e9, *sends[third])
    multiply(fourth, *sends[third], hid_a, *gots[second])
    hid_b, moved_b = finish_hidden(second, SHORT, kept[fourth], *gots[third], *moved_a)
    hid_c, moved_c = finish_hidden(third, 1e9, hid_b)
    exchange(fourth, hid_c, *moved_b)
    first = [join(hid_a, moved_a, hid_b), join(hid_b, moved_b, hid_c)]
    out, came, total = finish_down(0, first, sends[fourth])
    result = [total]
    hid_d, moved_d = finish_hidden(fourth, 1e9, out)
    last = [join(hid_c, moved_c, hid_d), join(hid_d, moved_d)]
    out, came, total = finish_down(1, last, (out,), came)
    result.append(total)

    placed = [jnp.take(r, at_home, axis=0).reshape(-1, shard_width) for r in result]
    return jnp.concatenate(placed, axis=0)


def solution(mesh):
    return jax.shard_map(
        shards,
        mesh=mesh,
        in_specs=(
            P("groups", "delta"),
            P("delta", "tensor"),
            P("delta", "tensor"),
            P("tensor", "delta"),
            P("delta", "tensor", None, None),
            P("delta", "tensor", None, None),
            P("delta", "tensor", None, None),
            P("delta", "tensor"),
            P("delta", "tensor"),
            P("delta", "tensor"),
            P("groups"),
            P("groups"),
        ),
        out_specs=P(("groups", "tensor"), "delta"),
        check_vma=False,
    )
```

```python
import functools

import jax
import jax.numpy as jnp
from jax import lax
from jax.experimental import pallas as pl
from jax.experimental.pallas import tpu as pltpu
from jax.sharding import PartitionSpec as P

CAP = 128
CHUNKS = (3, 1)
PARTS = 2
SHORT = 120e9
VMEM = 56 * 1024 * 1024
BF = jnp.bfloat16
F32 = jnp.float32


def cost(flops, moved):
    return pl.CostEstimate(flops=int(flops), bytes_accessed=int(moved), transcendentals=0)


def whole(shape):
    zeros = (0,) * len(shape)
    return pl.BlockSpec(shape, lambda *_: zeros)


def pack_body(owners, per_owner, kinds, stride, capacity, col_tiles, scal, x, sl, ss, send, keep, code, table):
    tile = 256
    rows, held = x.shape
    here = held // tile
    me = scal[0]
    height = table.shape[0]
    at_row = lax.broadcasted_iota(jnp.int32, (height, 128), 0)
    at_lane = lax.broadcasted_iota(jnp.int32, (height, 128), 1)
    known = jnp.zeros((height, 128), jnp.int32)
    for s in range(owners * per_owner):
        back = (s // per_owner - me + owners) % owners
        for j in range(kinds):
            place = scal[1 + owners + (back * per_owner + s % per_owner) * stride + j]
            known = jnp.where((at_row == s) & (at_lane == j), place // col_tiles, known)
            known = jnp.where((at_row == s) & (at_lane == 64 + j), place % col_tiles, known)
    table[...] = known.astype(F32).astype(BF)
    owner_l = sl[...] // per_owner
    first = lax.broadcasted_iota(jnp.int32, (rows, rows), 0)
    second = lax.broadcasted_iota(jnp.int32, (rows, rows), 1)
    ahead = ((ss[...] // per_owner) == owner_l) & (first < second)
    pos = jnp.sum(jnp.where(ahead, 1, 0), axis=0, keepdims=True)
    code[...] = sl[...] * capacity + pos
    target = pos
    for o in range(owners):
        target = target + jnp.where(owner_l == o, scal[1 + o] * capacity, 0)
    hot = lax.broadcasted_iota(jnp.int32, (owners * capacity, rows), 0) == target
    hot = jnp.where(hot, 1.0, 0.0).astype(BF)
    lanes = lax.broadcasted_iota(jnp.int32, (rows, height), 1)
    slot_hot = jnp.where(ss[...] == lanes, 1.0, 0.0).astype(BF)
    block = jnp.dot(slot_hot, table[...], preferred_element_type=F32)
    block = block - (me * here).astype(F32)
    for j in range(kinds):
        at = block[:, j : j + 1]
        picked = jnp.zeros((rows, tile), BF)
        for b in range(here):
            picked = jnp.where(at == float(b), x[:, b * tile : (b + 1) * tile], picked)
        found = jnp.dot(hot, picked, preferred_element_type=F32).astype(BF)
        send[:, j * tile : (j + 1) * tile] = found[: send.shape[0]]
        keep[:, j * tile : (j + 1) * tile] = found[send.shape[0] :]


def pack(scal, x, sl, ss, owners, per_owner, kinds, stride, col_tiles):
    rows = x.shape[0]
    width = kinds * 256
    height = -(-owners * per_owner // 128) * 128
    return pl.pallas_call(
        functools.partial(pack_body, owners, per_owner, kinds, stride, CAP, col_tiles),
        grid_spec=pltpu.PrefetchScalarGridSpec(
            num_scalar_prefetch=1,
            grid=(1,),
            in_specs=[whole(x.shape), whole((1, rows)), whole((rows, 1))],
            out_specs=[*[whole((owners // 2 * CAP, width))] * 2, whole((1, rows)), whole((height, 128))],
        ),
        out_shape=[
            *[jax.ShapeDtypeStruct((owners // 2 * CAP, width), BF)] * 2,
            jax.ShapeDtypeStruct((1, rows), jnp.int32),
            jax.ShapeDtypeStruct((height, 128), BF),
        ],
        compiler_params=pltpu.CompilerParams(vmem_limit_bytes=VMEM),
        cost_estimate=cost(SHORT, 4e6),
    )(scal, x, sl, ss)


def product_body(owners, per_owner, per_slot, pieces, scal, x, gt, ut, code, send, keep):
    tile = 256
    capacity = x.shape[0]
    rows = code.shape[1]
    slot_l = code[...] // capacity
    place = lax.broadcasted_iota(jnp.int32, (capacity, rows), 0) == code[...] % capacity
    mine = place & (slot_l // per_owner == scal[0])
    slot = jnp.sum(jnp.where(mine, slot_l % per_owner + 1, 0), axis=1, keepdims=True) - 1
    hot = jnp.where(mine, 1.0, 0.0).astype(BF)
    for kind, tiles in enumerate((gt, ut)):
        for j in range(per_slot):
            at = (kind * per_slot + j) * tile
            source = x[:, at : at + tile]
            total = jnp.zeros((capacity, tile), F32)
            for s in range(per_owner):
                picked = jnp.where(slot == s, source, jnp.zeros_like(source))
                total = total + jnp.dot(picked, tiles[s, j], preferred_element_type=F32)
            spread = lax.dot_general(
                hot, total.astype(BF), (((0,), (0,)), ((), ())), preferred_element_type=F32
            ).astype(BF)
            for home, offset, size, start in pieces:
                out = send if home < owners // 2 else keep
                out[home % (owners // 2), offset : offset + size, at : at + tile] = spread[start : start + size]


def product(scal, x, gt, ut, code, owners, per_owner, pieces):
    rows = code.shape[1]
    per_slot = gt.shape[1]
    shape = (owners // 2, rows // owners, x.shape[1])
    return pl.pallas_call(
        functools.partial(product_body, owners, per_owner, per_slot, pieces),
        grid_spec=pltpu.PrefetchScalarGridSpec(
            num_scalar_prefetch=1,
            grid=(1,),
            in_specs=[whole(x.shape), whole(gt.shape), whole(ut.shape), whole((1, rows))],
            out_specs=[whole(shape)] * 2,
        ),
        out_shape=[jax.ShapeDtypeStruct(shape, BF)] * 2,
        compiler_params=pltpu.CompilerParams(vmem_limit_bytes=VMEM),
        cost_estimate=cost(SHORT, 4e6),
    )(scal, x, gt, ut, code)


def gate_up_body(pieces, scal, *refs):
    blocks, (wg, wu, send, keep, x) = refs[:pieces], refs[pieces:]
    half = send.shape[1]

    @pl.when(pl.program_id(0) == 0)
    def _():
        each = x.shape[0] // pieces
        for i, block in enumerate(blocks):
            x[i * each : (i + 1) * each] = block[...].reshape(each, x.shape[1])

    for i, w in enumerate((wg, wu)):
        total = jnp.dot(x[...], w[...], preferred_element_type=F32)
        send[i] = total[:half].astype(send.dtype)
        keep[i] = total[half:]


def gate_up(scal, tokens, wg, wu, owners, shift, start, size, part):
    rows, depth = tokens.shape
    width = wg.shape[1] // PARTS
    block = min(1024, width)
    skip = part * (width // block)
    each = size // (owners * shift)
    first = start // (shift * each)
    unit = rows // (sum(CHUNKS) * owners * shift)
    view = tokens.reshape(shift, rows // (shift * unit), unit, depth)
    outs = pl.BlockSpec((2, size // 2, block), lambda i, s: (0, 0, i))
    weights = pl.BlockSpec((depth, block), lambda i, s: (0, skip + i))
    piece = [
        pl.BlockSpec((shift, each // unit, unit, depth), functools.partial(lambda h, i, s: (0, first + s[h], 0, 0), h))
        for h in range(owners)
    ]
    return pl.pallas_call(
        functools.partial(gate_up_body, owners),
        grid_spec=pltpu.PrefetchScalarGridSpec(
            num_scalar_prefetch=1,
            grid=(width // block,),
            in_specs=[*piece, weights, weights],
            out_specs=[outs, outs],
            scratch_shapes=[pltpu.VMEM((size, depth), BF)],
        ),
        out_shape=[jax.ShapeDtypeStruct((2, size // 2, width), F32)] * 2,
        compiler_params=pltpu.CompilerParams(vmem_limit_bytes=VMEM),
        cost_estimate=cost(4 * size * depth * width, 4 * depth * width),
    )(scal, *[view] * owners, wg, wu)


def total_body(order, keep, core, *refs):
    total = keep[0] + core[0]
    for ref in refs[:-1]:
        total = total + ref[...]
    refs[-1][...] = total


def total_of(order, keep, core, came):
    shape = came[0].shape
    last = keep.shape[0] - 1
    own = pl.BlockSpec((1, *shape), lambda i, s: (last, 0, 0))
    return pl.pallas_call(
        total_body,
        grid_spec=pltpu.PrefetchScalarGridSpec(
            num_scalar_prefetch=1,
            grid=(1,),
            in_specs=[own, own, *[whole(shape)] * len(came)],
            out_specs=whole(shape),
        ),
        out_shape=jax.ShapeDtypeStruct(shape, BF),
        compiler_params=pltpu.CompilerParams(vmem_limit_bytes=VMEM),
        cost_estimate=cost(SHORT, 1e6),
    )(order, keep, core, *came)


def activate_body(per_slot, start, each, row, parts, skip, keep, core, *refs):
    gots, (delta, slot, table, out) = refs[:parts], refs[parts:]
    tile = 256
    step = pl.program_id(0)
    across = out.shape[1] // tile
    lanes = lax.broadcasted_iota(jnp.int32, (each, table.shape[0]), 1)
    hot = jnp.where(slot[row : row + each] == lanes, 1.0, 0.0).astype(BF)
    where = jnp.dot(hot, table[...], preferred_element_type=F32) - (skip + step * across).astype(F32)
    at = [where[:, 64 + k : 65 + k] for k in range(2 * per_slot)]
    adds = [
        delta[start : start + each, k * tile : (k + 1) * tile].astype(F32) for k in range(2 * per_slot)
    ]
    for b in range(across):
        cols = slice(b * tile, (b + 1) * tile)
        sums = []
        for kind in range(2):
            got = gots[0][kind, :, cols] if parts == 1 else gots[kind][0, :, cols]
            total = keep[kind, :, cols] + core[kind, :, cols] + got.astype(F32)
            for k in range(kind * per_slot, (kind + 1) * per_slot):
                total = total + jnp.where(at[k] == float(b), adds[k], 0.0)
            sums.append(total)
        gate, up = sums
        out[:, cols] = (gate / (1.0 + jnp.exp(-gate)) * up).astype(BF)


def activate(keep, core, gots, delta, slot, table, per_slot, start, row, skip, flops):
    each, width = gots[0].shape[1:]
    last = keep.shape[1] // each - 1
    block = min(2048, width)
    own = pl.BlockSpec((2, each, block), lambda i: (0, last, i))
    taken = [pl.BlockSpec((g.shape[0], each, block), lambda i: (0, 0, i)) for g in gots]
    return pl.pallas_call(
        functools.partial(activate_body, per_slot, start, each, row, len(gots), skip),
        grid=(width // block,),
        in_specs=[own, own, *taken, whole(delta.shape), whole(slot.shape), whole(table.shape)],
        out_specs=pl.BlockSpec((each, block), lambda i: (0, i)),
        out_shape=jax.ShapeDtypeStruct((each, width), BF),
        compiler_params=pltpu.CompilerParams(vmem_limit_bytes=VMEM),
        cost_estimate=cost(flops, 24 * each * width),
    )(keep, core, *gots, delta, slot, table)


def down_body(width_tiles, here, plan, owners, per_owner, per_slot, start, scal, *refs):
    fars, nears, (w, *refs) = refs[:PARTS], refs[PARTS : 2 * PARTS], refs[2 * PARTS :]
    tiles, (slot, out, hid, listed, number) = refs[: len(plan)], refs[len(plan) :]
    tile = 256
    across = out.shape[1] // tile
    step = pl.program_id(0)
    half, wide = fars[0].shape
    stride = 3 * per_slot
    patterns = scal.shape[0] - owners * per_owner * stride

    @pl.when(step == 0)
    def _():
        for p in range(PARTS):
            hid[:half, p * wide : (p + 1) * wide] = fars[p][...]
            hid[half:, p * wide : (p + 1) * wide] = nears[p][...]
        me = scal[0]
        for r, (base, run) in enumerate(plan):
            for at in range(number.shape[1]):
                number[r, at] = 0

            def one(i, carry):
                local = i // per_slot
                which = scal[base + local // run] + local % run
                back = (which // per_owner - me + owners) % owners
                row = back * per_owner + which % per_owner
                place = scal[patterns + row * stride + 2 * per_slot + i % per_slot]
                block = place % width_tiles - me * here

                @pl.when((block >= 0) & (block < here))
                def _():
                    at = block // across
                    n = number[r, at]
                    listed[r * number.shape[1] + at, 4 * n] = i
                    listed[r * number.shape[1] + at, 4 * n + 1] = which
                    listed[r * number.shape[1] + at, 4 * n + 2] = place // width_tiles
                    listed[r * number.shape[1] + at, 4 * n + 3] = block % across
                    number[r, at] = n + 1

                return carry

            lax.fori_loop(0, tiles[r].shape[0], one, 0)

    out[...] = jnp.dot(hid[...], w[...], preferred_element_type=F32)
    for r in range(len(plan)):
        entry = r * number.shape[1] + step

        def add(n, carry):
            i = listed[entry, 4 * n]
            col = pl.multiple_of(listed[entry, 4 * n + 2] * tile, tile)
            source = hid[:, pl.ds(col, tile)]
            hit = slot[start : start + 2 * half] == listed[entry, 4 * n + 1]
            picked = jnp.where(hit, source, jnp.zeros_like(source))
            cols = pl.ds(pl.multiple_of(listed[entry, 4 * n + 3] * tile, tile), tile)
            out[:, cols] = out[:, cols] + jnp.dot(picked, tiles[r][i], preferred_element_type=F32)
            return carry

        lax.fori_loop(0, number[r, step], add, 0)


def down(scal, fars, nears, w, tiles, plan, slot, width_tiles, owners, per_owner, per_slot, start, flops):
    rows, depth = 2 * fars[0].shape[0], w.shape[0]
    width = w.shape[1]
    block = min(512, width)
    steps = width // block
    most = max(t.shape[0] for t in tiles)
    return pl.pallas_call(
        functools.partial(down_body, width_tiles, width // 256, plan, owners, per_owner, per_slot, start),
        grid_spec=pltpu.PrefetchScalarGridSpec(
            num_scalar_prefetch=1,
            grid=(steps,),
            in_specs=[
                *[whole(f.shape) for f in (*fars, *nears)],
                pl.BlockSpec((depth, block), lambda i, s: (0, i)),
                *[whole(t.shape) for t in tiles],
                whole(slot.shape),
            ],
            out_specs=pl.BlockSpec((rows, block), lambda i, s: (0, i)),
            scratch_shapes=[
                pltpu.VMEM((rows, depth), BF),
                pltpu.SMEM((len(tiles) * steps, 4 * most), jnp.int32),
                pltpu.SMEM((len(tiles), steps), jnp.int32),
            ],
        ),
        out_shape=jax.ShapeDtypeStruct((rows, width), F32),
        compiler_params=pltpu.CompilerParams(vmem_limit_bytes=VMEM),
        cost_estimate=cost(flops, 1e6),
    )(scal, *fars, *nears, w, *tiles, slot)


def shards(
    tokens,
    gate_weight,
    up_weight,
    down_weight,
    gate_tiles,
    up_tiles,
    down_tiles,
    gate_pattern,
    up_pattern,
    down_pattern,
    row_variant,
    variant_slot,
):
    owners = lax.axis_size("delta")
    shift = lax.axis_size("tensor")
    groups = lax.axis_size("groups")
    me = lax.axis_index("delta")
    here_t = lax.axis_index("tensor")
    my_core, my_y = me % 2, me // 2
    ys = owners // 2
    per_owner, per_slot = gate_pattern.shape
    slots = owners * per_owner
    rows, shard_width = tokens.shape
    width = gate_weight.shape[1]
    col_tiles = width // 256
    width_tiles = shard_width * owners // 256
    unit = rows // sum(CHUNKS)
    sizes = [unit * c for c in CHUNKS]

    def core_swap(x):
        return lax.ppermute(x, "delta", [(i, i ^ 1) for i in range(owners)])

    def y_move(x, k):
        return lax.ppermute(x, "delta", [(i, (i + 2 * k) % owners) for i in range(owners)])

    order_y = [(my_y + k) % ys for k in range(1, ys)] + [my_y]
    homes = jnp.stack([y * 2 + c for c in (1 - my_core, my_core) for y in order_y]).astype(jnp.int32)

    row_ids = []
    offset = 0
    for size in sizes:
        each = size // (owners * shift)
        ids = (
            jnp.arange(shift, dtype=jnp.int32)[None, :, None] * (rows // shift)
            + offset
            + homes[:, None, None] * each
            + jnp.arange(each, dtype=jnp.int32)[None, None, :]
        )
        row_ids.append(ids.reshape(-1))
        offset += owners * each
    row_of = jnp.concatenate(row_ids)

    hit = row_variant[:, None] == jnp.arange(variant_slot.shape[0], dtype=jnp.int32)[None, :]
    slot_rows = jnp.sum(jnp.where(hit, variant_slot[None, :], 0), axis=1)

    def after(x, *earlier):
        return lax.optimization_barrier((x, *earlier))[0]

    kinds = 2 * per_slot
    own = jnp.concatenate([gate_pattern, up_pattern, down_pattern], axis=1)
    seen = [own] + [
        lax.ppermute(own, "delta", [(i, (i - k) % owners) for i in range(owners)]) for k in range(1, owners)
    ]
    patterns = jnp.concatenate([s.reshape(-1) for s in seen])
    at_home = jnp.stack(
        [((d // 2) - my_y - 1) % ys + ys * jnp.where(d % 2 == my_core, 1, 0) for d in range(owners)]
    ).astype(jnp.int32)
    scal = jnp.concatenate([me.astype(jnp.int32)[None], at_home, patterns])

    flat_tiles = down_tiles.reshape(-1, 256, 256)
    if groups == 2 and per_owner % 2 == 0:
        part = per_owner // 2
        mine_g = lax.axis_index("groups")
        piece = lax.dynamic_slice_in_dim(flat_tiles, mine_g * part * per_slot, part * per_slot, 0)
        halves = [mine_g * part, (1 - mine_g) * part]
    else:
        part, piece, halves = per_owner, flat_tiles, [0]
    from_y = jnp.concatenate([y_move(piece, -k) for k in range(1, ys)])
    tiles = [from_y]
    firsts, plan = [], []
    for core in (my_core, 1 - my_core):
        for first in halves:
            plan.append((1 + len(firsts), part))
            firsts.extend((y * 2 + core) * per_owner + first for y in order_y[:-1])
        plan.append((1 + len(firsts), per_owner))
        firsts.append((my_y * 2 + core) * per_owner)
    plan = tuple(plan)
    down_scal = jnp.concatenate([jnp.stack([me] + firsts).astype(jnp.int32), patterns])

    starts = [sum(sizes[:i]) for i in range(len(sizes))]
    inners = [s // owners for s in starts]
    kept, cores, sends, gots = {}, {}, {}, {}

    def multiply(u, *earlier):
        i, part = u
        send, kept[u] = gate_up(
            after(homes, *earlier), tokens, gate_weight, up_weight, owners, shift, starts[i], sizes[i], part
        )
        cores[u] = core_swap(send)

    def exchange(u, *earlier):
        each = sizes[u[0]] // owners
        sends[u], got = [], None
        own = after(kept[u], *earlier)
        for k in range(1, ys):
            rows_k = slice((k - 1) * each, k * each)
            sends[u].append((own[:, rows_k] + cores[u][:, rows_k]).astype(BF))
            moved = y_move(sends[u][-1], k)
            if ys > 2:
                moved = moved.astype(F32)
            got = moved if got is None else got + moved
        gots[u] = [got]

    def finish(keep, core, pieces, *earlier):
        return total_of(
            after(homes, *earlier), keep, core, [y_move(pieces[k - 1], k) for k in range(1, ys)]
        )

    ahead, second, third, fourth = (0, 0), (0, 1), (1, 0), (1, 1)
    multiply(ahead)
    send, keep, code, table = pack(
        after(scal, kept[ahead], from_y),
        tokens,
        slot_rows[None, :],
        slot_rows[:, None],
        owners,
        per_owner,
        kinds,
        3 * per_slot,
        col_tiles,
    )
    exchange(ahead)
    packed = keep.reshape(ys, CAP, -1)
    packed_core = core_swap(send.reshape(ys, CAP, -1))
    packed_sends = [packed[k - 1] + packed_core[k - 1] for k in range(1, ys)]
    multiply(second, *sends[ahead], *packed_sends)
    code = after(code, kept[second])
    if len(halves) == 2:
        tiles.append(lax.ppermute(after(from_y, kept[second]), "groups", [(0, 1), (1, 0)]))
    code_q = jnp.sum(
        jnp.where(row_of[:, None] == jnp.arange(rows, dtype=jnp.int32)[None, :], code, 0), axis=1
    )
    slot_q = code_q // CAP
    pieces = tuple(
        (home, inner, size // owners, start + home * (size // owners))
        for size, start, inner in zip(sizes, starts, inners)
        for home in range(owners)
    )
    ss_q = slot_q[:, None]

    features = finish(packed, packed_core, packed_sends, kept[second], *gots[ahead])
    exchange(second, features)
    send, spread = product(
        after(scal, *sends[second]),
        features,
        gate_tiles,
        up_tiles,
        code_q[None, :],
        owners,
        per_owner,
        pieces,
    )
    spread_core = core_swap(send)
    spread_sends = [spread[k - 1] + spread_core[k - 1] for k in range(1, ys)]
    multiply(third, *sends[second], *spread_sends)
    home_delta = finish(spread, spread_core, spread_sends, kept[third])
    exchange(third, home_delta)

    def finish_hidden(u, flops, *earlier):
        i, part = u
        each = sizes[i] // owners
        hid = activate(
            kept[u],
            cores[u],
            gots[u],
            home_delta,
            ss_q,
            after(table, *earlier),
            per_slot,
            inners[i],
            starts[i] + sizes[i] - each,
            part * (col_tiles // PARTS),
            flops,
        )
        return hid, [y_move(hid, -k) for k in range(1, ys)]

    def join(hid, moved, *earlier):
        return jnp.concatenate([after(m, *earlier) for m in moved] + [hid])

    def finish_down(i, chips, earlier, sent=None):
        out = down(
            after(down_scal, *earlier),
            [core_swap(c) for c in chips],
            chips,
            down_weight,
            all_tiles,
            plan,
            ss_q,
            width_tiles,
            owners,
            per_owner,
            per_slot,
            starts[i],
            1e9,
        )
        blocks = out.reshape(owners, shift, sizes[i] // (owners * shift), shard_width).transpose(1, 0, 2, 3)
        total = lax.dynamic_index_in_dim(blocks, here_t, 0, keepdims=False)
        came = []
        for k in range(1, shift):
            gone = lax.dynamic_index_in_dim(blocks, (here_t + k) % shift, 0, keepdims=False).astype(BF)
            if sent is not None:
                gone = after(gone, sent[k - 1])
            came.append(lax.ppermute(gone, "tensor", [(j, (j + k) % shift) for j in range(shift)]))
            total = total + came[-1].astype(F32)
        return out, came, total.astype(BF)

    hid_a, moved_a = finish_hidden(ahead, 1e9, *sends[third])
    near_tiles = [*tiles, flat_tiles]
    all_tiles = near_tiles + [core_swap(after(t, hid_a)) for t in near_tiles]
    multiply(fourth, *sends[third], hid_a, *gots[second])
    hid_b, moved_b = finish_hidden(second, SHORT, kept[fourth], *gots[third], *moved_a, *tiles[1:])
    hid_c, moved_c = finish_hidden(third, 1e9, hid_b)
    exchange(fourth, hid_c, *moved_b)
    first = [join(hid_a, moved_a, hid_b), join(hid_b, moved_b, hid_c)]
    out, came, total = finish_down(0, first, sends[fourth])
    result = [total]
    hid_d, moved_d = finish_hidden(fourth, 1e9, out)
    last = [join(hid_c, moved_c, hid_d), join(hid_d, moved_d)]
    out, came, total = finish_down(1, last, (out,), came)
    result.append(total)

    placed = [jnp.take(r, at_home, axis=0).reshape(-1, shard_width) for r in result]
    return jnp.concatenate(placed, axis=0)


def solution(mesh):
    return jax.shard_map(
        shards,
        mesh=mesh,
        in_specs=(
            P("groups", "delta"),
            P("delta", "tensor"),
            P("delta", "tensor"),
            P("tensor", "delta"),
            P("delta", "tensor", None, None),
            P("delta", "tensor", None, None),
            P("delta", "tensor", None, None),
            P("delta", "tensor"),
            P("delta", "tensor"),
            P("delta", "tensor"),
            P("groups"),
            P("groups"),
        ),
        out_specs=P(("groups", "tensor"), "delta"),
        check_vma=False,
    )
```

```python
import functools

import jax
import jax.numpy as jnp
from jax import lax
from jax.experimental import pallas as pl
from jax.experimental.pallas import tpu as pltpu
from jax.sharding import PartitionSpec as P

CAP = 128
CHUNKS = (2, 2)
PARTS = 2
SHORT = 120e9
VMEM = 56 * 1024 * 1024
BF = jnp.bfloat16
F32 = jnp.float32


def cost(flops, moved):
    return pl.CostEstimate(flops=int(flops), bytes_accessed=int(moved), transcendentals=0)


def whole(shape):
    zeros = (0,) * len(shape)
    return pl.BlockSpec(shape, lambda *_: zeros)


def pack_body(owners, per_owner, kinds, stride, capacity, col_tiles, scal, x, sl, ss, send, keep, code, table):
    tile = 256
    rows, held = x.shape
    here = held // tile
    me = scal[0]
    height = table.shape[0]
    at_row = lax.broadcasted_iota(jnp.int32, (height, 128), 0)
    at_lane = lax.broadcasted_iota(jnp.int32, (height, 128), 1)
    known = jnp.zeros((height, 128), jnp.int32)
    for s in range(owners * per_owner):
        back = (s // per_owner - me + owners) % owners
        for j in range(kinds):
            place = scal[1 + owners + (back * per_owner + s % per_owner) * stride + j]
            known = jnp.where((at_row == s) & (at_lane == j), place // col_tiles, known)
            known = jnp.where((at_row == s) & (at_lane == 64 + j), place % col_tiles, known)
    table[...] = known.astype(F32).astype(BF)
    owner_l = sl[...] // per_owner
    first = lax.broadcasted_iota(jnp.int32, (rows, rows), 0)
    second = lax.broadcasted_iota(jnp.int32, (rows, rows), 1)
    ahead = ((ss[...] // per_owner) == owner_l) & (first < second)
    pos = jnp.sum(jnp.where(ahead, 1, 0), axis=0, keepdims=True)
    code[...] = sl[...] * capacity + pos
    target = pos
    for o in range(owners):
        target = target + jnp.where(owner_l == o, scal[1 + o] * capacity, 0)
    hot = lax.broadcasted_iota(jnp.int32, (owners * capacity, rows), 0) == target
    hot = jnp.where(hot, 1.0, 0.0).astype(BF)
    lanes = lax.broadcasted_iota(jnp.int32, (rows, height), 1)
    slot_hot = jnp.where(ss[...] == lanes, 1.0, 0.0).astype(BF)
    block = jnp.dot(slot_hot, table[...], preferred_element_type=F32)
    block = block - (me * here).astype(F32)
    for j in range(kinds):
        at = block[:, j : j + 1]
        picked = jnp.zeros((rows, tile), BF)
        for b in range(here):
            picked = jnp.where(at == float(b), x[:, b * tile : (b + 1) * tile], picked)
        found = jnp.dot(hot, picked, preferred_element_type=F32).astype(BF)
        send[:, j * tile : (j + 1) * tile] = found[: send.shape[0]]
        keep[:, j * tile : (j + 1) * tile] = found[send.shape[0] :]


def pack(scal, x, sl, ss, owners, per_owner, kinds, stride, col_tiles):
    rows = x.shape[0]
    width = kinds * 256
    height = -(-owners * per_owner // 128) * 128
    return pl.pallas_call(
        functools.partial(pack_body, owners, per_owner, kinds, stride, CAP, col_tiles),
        grid_spec=pltpu.PrefetchScalarGridSpec(
            num_scalar_prefetch=1,
            grid=(1,),
            in_specs=[whole(x.shape), whole((1, rows)), whole((rows, 1))],
            out_specs=[*[whole((owners // 2 * CAP, width))] * 2, whole((1, rows)), whole((height, 128))],
        ),
        out_shape=[
            *[jax.ShapeDtypeStruct((owners // 2 * CAP, width), BF)] * 2,
            jax.ShapeDtypeStruct((1, rows), jnp.int32),
            jax.ShapeDtypeStruct((height, 128), BF),
        ],
        compiler_params=pltpu.CompilerParams(vmem_limit_bytes=VMEM),
        cost_estimate=cost(SHORT, 4e6),
    )(scal, x, sl, ss)


def product_body(owners, per_owner, per_slot, pieces, scal, x, gt, ut, code, send, keep):
    tile = 256
    capacity = x.shape[0]
    rows = code.shape[1]
    slot_l = code[...] // capacity
    place = lax.broadcasted_iota(jnp.int32, (capacity, rows), 0) == code[...] % capacity
    mine = place & (slot_l // per_owner == scal[0])
    slot = jnp.sum(jnp.where(mine, slot_l % per_owner + 1, 0), axis=1, keepdims=True) - 1
    hot = jnp.where(mine, 1.0, 0.0).astype(BF)
    for kind, tiles in enumerate((gt, ut)):
        for j in range(per_slot):
            at = (kind * per_slot + j) * tile
            source = x[:, at : at + tile]
            total = jnp.zeros((capacity, tile), F32)
            for s in range(per_owner):
                picked = jnp.where(slot == s, source, jnp.zeros_like(source))
                total = total + jnp.dot(picked, tiles[s, j], preferred_element_type=F32)
            spread = lax.dot_general(
                hot, total.astype(BF), (((0,), (0,)), ((), ())), preferred_element_type=F32
            ).astype(BF)
            for home, offset, size, start in pieces:
                out = send if home < owners // 2 else keep
                out[home % (owners // 2), offset : offset + size, at : at + tile] = spread[start : start + size]


def product(scal, x, gt, ut, code, owners, per_owner, pieces):
    rows = code.shape[1]
    per_slot = gt.shape[1]
    shape = (owners // 2, rows // owners, x.shape[1])
    return pl.pallas_call(
        functools.partial(product_body, owners, per_owner, per_slot, pieces),
        grid_spec=pltpu.PrefetchScalarGridSpec(
            num_scalar_prefetch=1,
            grid=(1,),
            in_specs=[whole(x.shape), whole(gt.shape), whole(ut.shape), whole((1, rows))],
            out_specs=[whole(shape)] * 2,
        ),
        out_shape=[jax.ShapeDtypeStruct(shape, BF)] * 2,
        compiler_params=pltpu.CompilerParams(vmem_limit_bytes=VMEM),
        cost_estimate=cost(SHORT, 4e6),
    )(scal, x, gt, ut, code)


def gate_up_body(pieces, scal, *refs):
    blocks, (wg, wu, send, keep, x) = refs[:pieces], refs[pieces:]
    half = send.shape[1]

    @pl.when(pl.program_id(0) == 0)
    def _():
        each = x.shape[0] // pieces
        for i, block in enumerate(blocks):
            x[i * each : (i + 1) * each] = block[...].reshape(each, x.shape[1])

    for i, w in enumerate((wg, wu)):
        total = jnp.dot(x[...], w[...], preferred_element_type=F32)
        send[i] = total[:half].astype(send.dtype)
        keep[i] = total[half:]


def gate_up(scal, tokens, wg, wu, owners, shift, start, size, part):
    rows, depth = tokens.shape
    width = wg.shape[1] // PARTS
    block = min(1024, width)
    skip = part * (width // block)
    each = size // (owners * shift)
    first = start // (shift * each)
    unit = rows // (sum(CHUNKS) * owners * shift)
    view = tokens.reshape(shift, rows // (shift * unit), unit, depth)
    outs = pl.BlockSpec((2, size // 2, block), lambda i, s: (0, 0, i))
    weights = pl.BlockSpec((depth, block), lambda i, s: (0, skip + i))
    piece = [
        pl.BlockSpec((shift, each // unit, unit, depth), functools.partial(lambda h, i, s: (0, first + s[h], 0, 0), h))
        for h in range(owners)
    ]
    return pl.pallas_call(
        functools.partial(gate_up_body, owners),
        grid_spec=pltpu.PrefetchScalarGridSpec(
            num_scalar_prefetch=1,
            grid=(width // block,),
            in_specs=[*piece, weights, weights],
            out_specs=[outs, outs],
            scratch_shapes=[pltpu.VMEM((size, depth), BF)],
        ),
        out_shape=[jax.ShapeDtypeStruct((2, size // 2, width), F32)] * 2,
        compiler_params=pltpu.CompilerParams(vmem_limit_bytes=VMEM),
        cost_estimate=cost(4 * size * depth * width, 4 * depth * width),
    )(scal, *[view] * owners, wg, wu)


def total_body(order, keep, core, *refs):
    total = keep[0] + core[0]
    for ref in refs[:-1]:
        total = total + ref[...]
    refs[-1][...] = total


def total_of(order, keep, core, came):
    shape = came[0].shape
    last = keep.shape[0] - 1
    own = pl.BlockSpec((1, *shape), lambda i, s: (last, 0, 0))
    return pl.pallas_call(
        total_body,
        grid_spec=pltpu.PrefetchScalarGridSpec(
            num_scalar_prefetch=1,
            grid=(1,),
            in_specs=[own, own, *[whole(shape)] * len(came)],
            out_specs=whole(shape),
        ),
        out_shape=jax.ShapeDtypeStruct(shape, BF),
        compiler_params=pltpu.CompilerParams(vmem_limit_bytes=VMEM),
        cost_estimate=cost(SHORT, 1e6),
    )(order, keep, core, *came)


def activate_body(per_slot, start, each, row, parts, skip, keep, core, *refs):
    gots, (delta, slot, table, out) = refs[:parts], refs[parts:]
    tile = 256
    step = pl.program_id(0)
    across = out.shape[1] // tile
    lanes = lax.broadcasted_iota(jnp.int32, (each, table.shape[0]), 1)
    hot = jnp.where(slot[row : row + each] == lanes, 1.0, 0.0).astype(BF)
    where = jnp.dot(hot, table[...], preferred_element_type=F32) - (skip + step * across).astype(F32)
    at = [where[:, 64 + k : 65 + k] for k in range(2 * per_slot)]
    adds = [
        delta[start : start + each, k * tile : (k + 1) * tile].astype(F32) for k in range(2 * per_slot)
    ]
    for b in range(across):
        cols = slice(b * tile, (b + 1) * tile)
        sums = []
        for kind in range(2):
            got = gots[0][kind, :, cols] if parts == 1 else gots[kind][0, :, cols]
            total = keep[kind, :, cols] + core[kind, :, cols] + got.astype(F32)
            for k in range(kind * per_slot, (kind + 1) * per_slot):
                total = total + jnp.where(at[k] == float(b), adds[k], 0.0)
            sums.append(total)
        gate, up = sums
        out[:, cols] = (gate / (1.0 + jnp.exp(-gate)) * up).astype(BF)


def activate(keep, core, gots, delta, slot, table, per_slot, start, row, skip, flops):
    each, width = gots[0].shape[1:]
    last = keep.shape[1] // each - 1
    block = min(2048, width)
    own = pl.BlockSpec((2, each, block), lambda i: (0, last, i))
    taken = [pl.BlockSpec((g.shape[0], each, block), lambda i: (0, 0, i)) for g in gots]
    return pl.pallas_call(
        functools.partial(activate_body, per_slot, start, each, row, len(gots), skip),
        grid=(width // block,),
        in_specs=[own, own, *taken, whole(delta.shape), whole(slot.shape), whole(table.shape)],
        out_specs=pl.BlockSpec((each, block), lambda i: (0, i)),
        out_shape=jax.ShapeDtypeStruct((each, width), BF),
        compiler_params=pltpu.CompilerParams(vmem_limit_bytes=VMEM),
        cost_estimate=cost(flops, 24 * each * width),
    )(keep, core, *gots, delta, slot, table)


def down_body(width_tiles, here, plan, owners, per_owner, per_slot, start, scal, *refs):
    fars, nears, (w, *refs) = refs[:PARTS], refs[PARTS : 2 * PARTS], refs[2 * PARTS :]
    tiles, (slot, out, hid, listed, number) = refs[: len(plan)], refs[len(plan) :]
    tile = 256
    across = out.shape[1] // tile
    step = pl.program_id(0)
    half, wide = fars[0].shape
    stride = 3 * per_slot
    patterns = scal.shape[0] - owners * per_owner * stride

    @pl.when(step == 0)
    def _():
        for p in range(PARTS):
            hid[:half, p * wide : (p + 1) * wide] = fars[p][...]
            hid[half:, p * wide : (p + 1) * wide] = nears[p][...]
        me = scal[0]
        for r, (base, run) in enumerate(plan):
            for at in range(number.shape[1]):
                number[r, at] = 0

            def one(i, carry):
                local = i // per_slot
                which = scal[base + local // run] + local % run
                back = (which // per_owner - me + owners) % owners
                row = back * per_owner + which % per_owner
                place = scal[patterns + row * stride + 2 * per_slot + i % per_slot]
                block = place % width_tiles - me * here

                @pl.when((block >= 0) & (block < here))
                def _():
                    at = block // across
                    n = number[r, at]
                    listed[r * number.shape[1] + at, 4 * n] = i
                    listed[r * number.shape[1] + at, 4 * n + 1] = which
                    listed[r * number.shape[1] + at, 4 * n + 2] = place // width_tiles
                    listed[r * number.shape[1] + at, 4 * n + 3] = block % across
                    number[r, at] = n + 1

                return carry

            lax.fori_loop(0, tiles[r].shape[0], one, 0)

    out[...] = jnp.dot(hid[...], w[...], preferred_element_type=F32)
    for r in range(len(plan)):
        entry = r * number.shape[1] + step

        def add(n, carry):
            i = listed[entry, 4 * n]
            col = pl.multiple_of(listed[entry, 4 * n + 2] * tile, tile)
            source = hid[:, pl.ds(col, tile)]
            hit = slot[start : start + 2 * half] == listed[entry, 4 * n + 1]
            picked = jnp.where(hit, source, jnp.zeros_like(source))
            cols = pl.ds(pl.multiple_of(listed[entry, 4 * n + 3] * tile, tile), tile)
            out[:, cols] = out[:, cols] + jnp.dot(picked, tiles[r][i], preferred_element_type=F32)
            return carry

        lax.fori_loop(0, number[r, step], add, 0)


def down(scal, fars, nears, w, tiles, plan, slot, width_tiles, owners, per_owner, per_slot, start, flops):
    rows, depth = 2 * fars[0].shape[0], w.shape[0]
    width = w.shape[1]
    block = min(512, width)
    steps = width // block
    most = max(t.shape[0] for t in tiles)
    return pl.pallas_call(
        functools.partial(down_body, width_tiles, width // 256, plan, owners, per_owner, per_slot, start),
        grid_spec=pltpu.PrefetchScalarGridSpec(
            num_scalar_prefetch=1,
            grid=(steps,),
            in_specs=[
                *[whole(f.shape) for f in (*fars, *nears)],
                pl.BlockSpec((depth, block), lambda i, s: (0, i)),
                *[whole(t.shape) for t in tiles],
                whole(slot.shape),
            ],
            out_specs=pl.BlockSpec((rows, block), lambda i, s: (0, i)),
            scratch_shapes=[
                pltpu.VMEM((rows, depth), BF),
                pltpu.SMEM((len(tiles) * steps, 4 * most), jnp.int32),
                pltpu.SMEM((len(tiles), steps), jnp.int32),
            ],
        ),
        out_shape=jax.ShapeDtypeStruct((rows, width), F32),
        compiler_params=pltpu.CompilerParams(vmem_limit_bytes=VMEM),
        cost_estimate=cost(flops, 1e6),
    )(scal, *fars, *nears, w, *tiles, slot)


def shards(
    tokens,
    gate_weight,
    up_weight,
    down_weight,
    gate_tiles,
    up_tiles,
    down_tiles,
    gate_pattern,
    up_pattern,
    down_pattern,
    row_variant,
    variant_slot,
):
    owners = lax.axis_size("delta")
    shift = lax.axis_size("tensor")
    groups = lax.axis_size("groups")
    me = lax.axis_index("delta")
    here_t = lax.axis_index("tensor")
    my_core, my_y = me % 2, me // 2
    ys = owners // 2
    per_owner, per_slot = gate_pattern.shape
    slots = owners * per_owner
    rows, shard_width = tokens.shape
    width = gate_weight.shape[1]
    col_tiles = width // 256
    width_tiles = shard_width * owners // 256
    unit = rows // sum(CHUNKS)
    sizes = [unit * c for c in CHUNKS]

    def core_swap(x):
        return lax.ppermute(x, "delta", [(i, i ^ 1) for i in range(owners)])

    def y_move(x, k):
        return lax.ppermute(x, "delta", [(i, (i + 2 * k) % owners) for i in range(owners)])

    order_y = [(my_y + k) % ys for k in range(1, ys)] + [my_y]
    homes = jnp.stack([y * 2 + c for c in (1 - my_core, my_core) for y in order_y]).astype(jnp.int32)

    row_ids = []
    offset = 0
    for size in sizes:
        each = size // (owners * shift)
        ids = (
            jnp.arange(shift, dtype=jnp.int32)[None, :, None] * (rows // shift)
            + offset
            + homes[:, None, None] * each
            + jnp.arange(each, dtype=jnp.int32)[None, None, :]
        )
        row_ids.append(ids.reshape(-1))
        offset += owners * each
    row_of = jnp.concatenate(row_ids)

    hit = row_variant[:, None] == jnp.arange(variant_slot.shape[0], dtype=jnp.int32)[None, :]
    slot_rows = jnp.sum(jnp.where(hit, variant_slot[None, :], 0), axis=1)

    def after(x, *earlier):
        return lax.optimization_barrier((x, *earlier))[0]

    kinds = 2 * per_slot
    own = jnp.concatenate([gate_pattern, up_pattern, down_pattern], axis=1)
    seen = [own] + [
        lax.ppermute(own, "delta", [(i, (i - k) % owners) for i in range(owners)]) for k in range(1, owners)
    ]
    patterns = jnp.concatenate([s.reshape(-1) for s in seen])
    at_home = jnp.stack(
        [((d // 2) - my_y - 1) % ys + ys * jnp.where(d % 2 == my_core, 1, 0) for d in range(owners)]
    ).astype(jnp.int32)
    scal = jnp.concatenate([me.astype(jnp.int32)[None], at_home, patterns])

    flat_tiles = down_tiles.reshape(-1, 256, 256)
    if groups == 2 and per_owner % 2 == 0:
        part = per_owner // 2
        mine_g = lax.axis_index("groups")
        piece = lax.dynamic_slice_in_dim(flat_tiles, mine_g * part * per_slot, part * per_slot, 0)
        halves = [mine_g * part, (1 - mine_g) * part]
    else:
        part, piece, halves = per_owner, flat_tiles, [0]
    from_y = jnp.concatenate([y_move(piece, -k) for k in range(1, ys)])
    tiles = [from_y]
    firsts, plan = [], []
    for core in (my_core, 1 - my_core):
        for first in halves:
            plan.append((1 + len(firsts), part))
            firsts.extend((y * 2 + core) * per_owner + first for y in order_y[:-1])
        plan.append((1 + len(firsts), per_owner))
        firsts.append((my_y * 2 + core) * per_owner)
    plan = tuple(plan)
    down_scal = jnp.concatenate([jnp.stack([me] + firsts).astype(jnp.int32), patterns])

    starts = [sum(sizes[:i]) for i in range(len(sizes))]
    inners = [s // owners for s in starts]
    kept, cores, sends, gots = {}, {}, {}, {}

    def multiply(u, *earlier):
        i, part = u
        send, kept[u] = gate_up(
            after(homes, *earlier), tokens, gate_weight, up_weight, owners, shift, starts[i], sizes[i], part
        )
        cores[u] = core_swap(send)

    def exchange(u, *earlier):
        each = sizes[u[0]] // owners
        sends[u], got = [], None
        own = after(kept[u], *earlier)
        for k in range(1, ys):
            rows_k = slice((k - 1) * each, k * each)
            sends[u].append((own[:, rows_k] + cores[u][:, rows_k]).astype(BF))
            moved = y_move(sends[u][-1], k)
            if ys > 2:
                moved = moved.astype(F32)
            got = moved if got is None else got + moved
        gots[u] = [got]

    def finish(keep, core, pieces, *earlier):
        return total_of(
            after(homes, *earlier), keep, core, [y_move(pieces[k - 1], k) for k in range(1, ys)]
        )

    ahead, second, third, fourth = (0, 0), (0, 1), (1, 0), (1, 1)
    multiply(ahead)
    send, keep, code, table = pack(
        after(scal, kept[ahead], from_y),
        tokens,
        slot_rows[None, :],
        slot_rows[:, None],
        owners,
        per_owner,
        kinds,
        3 * per_slot,
        col_tiles,
    )
    exchange(ahead)
    packed = keep.reshape(ys, CAP, -1)
    packed_core = core_swap(send.reshape(ys, CAP, -1))
    packed_sends = [packed[k - 1] + packed_core[k - 1] for k in range(1, ys)]
    multiply(second, *sends[ahead], *packed_sends)
    code = after(code, kept[second])
    if len(halves) == 2:
        tiles.append(lax.ppermute(after(from_y, kept[second]), "groups", [(0, 1), (1, 0)]))
    code_q = jnp.sum(
        jnp.where(row_of[:, None] == jnp.arange(rows, dtype=jnp.int32)[None, :], code, 0), axis=1
    )
    slot_q = code_q // CAP
    pieces = tuple(
        (home, inner, size // owners, start + home * (size // owners))
        for size, start, inner in zip(sizes, starts, inners)
        for home in range(owners)
    )
    ss_q = slot_q[:, None]

    features = finish(packed, packed_core, packed_sends, kept[second], *gots[ahead])
    exchange(second, features)
    send, spread = product(
        after(scal, *sends[second]),
        features,
        gate_tiles,
        up_tiles,
        code_q[None, :],
        owners,
        per_owner,
        pieces,
    )
    spread_core = core_swap(send)
    spread_sends = [spread[k - 1] + spread_core[k - 1] for k in range(1, ys)]
    multiply(third, *sends[second], *spread_sends)
    home_delta = finish(spread, spread_core, spread_sends, kept[third])
    exchange(third, home_delta)

    def finish_hidden(u, flops, *earlier):
        i, part = u
        each = sizes[i] // owners
        hid = activate(
            kept[u],
            cores[u],
            gots[u],
            home_delta,
            ss_q,
            after(table, *earlier),
            per_slot,
            inners[i],
            starts[i] + sizes[i] - each,
            part * (col_tiles // PARTS),
            flops,
        )
        return hid, [y_move(hid, -k) for k in range(1, ys)]

    def join(hid, moved, *earlier):
        return jnp.concatenate([after(m, *earlier) for m in moved] + [hid])

    def finish_down(i, chips, earlier, sent=None):
        out = down(
            after(down_scal, *earlier),
            [core_swap(c) for c in chips],
            chips,
            down_weight,
            all_tiles,
            plan,
            ss_q,
            width_tiles,
            owners,
            per_owner,
            per_slot,
            starts[i],
            1e9,
        )
        blocks = out.reshape(owners, shift, sizes[i] // (owners * shift), shard_width).transpose(1, 0, 2, 3)
        total = lax.dynamic_index_in_dim(blocks, here_t, 0, keepdims=False)
        came = []
        for k in range(1, shift):
            gone = lax.dynamic_index_in_dim(blocks, (here_t + k) % shift, 0, keepdims=False).astype(BF)
            if sent is not None:
                gone = after(gone, sent[k - 1])
            came.append(lax.ppermute(gone, "tensor", [(j, (j + k) % shift) for j in range(shift)]))
            total = total + came[-1].astype(F32)
        return out, came, total.astype(BF)

    hid_a, moved_a = finish_hidden(ahead, 1e9, *sends[third])
    near_tiles = [*tiles, flat_tiles]
    all_tiles = near_tiles + [core_swap(after(t, hid_a)) for t in near_tiles]
    multiply(fourth, *sends[third], hid_a, *gots[second])
    hid_b, moved_b = finish_hidden(second, SHORT, kept[fourth], *gots[third], *moved_a, *tiles[1:])
    hid_c, moved_c = finish_hidden(third, 1e9, hid_b)
    exchange(fourth, hid_c, *moved_b)
    first = [join(hid_a, moved_a, hid_b), join(hid_b, moved_b, hid_c)]
    out, came, total = finish_down(0, first, sends[fourth])
    result = [total]
    hid_d, moved_d = finish_hidden(fourth, 1e9, out)
    last = [join(hid_c, moved_c, hid_d), join(hid_d, moved_d)]
    out, came, total = finish_down(1, last, (out,), came)
    result.append(total)

    placed = [jnp.take(r, at_home, axis=0).reshape(-1, shard_width) for r in result]
    return jnp.concatenate(placed, axis=0)


def solution(mesh):
    return jax.shard_map(
        shards,
        mesh=mesh,
        in_specs=(
            P("groups", "delta"),
            P("delta", "tensor"),
            P("delta", "tensor"),
            P("tensor", "delta"),
            P("delta", "tensor", None, None),
            P("delta", "tensor", None, None),
            P("delta", "tensor", None, None),
            P("delta", "tensor"),
            P("delta", "tensor"),
            P("delta", "tensor"),
            P("groups"),
            P("groups"),
        ),
        out_specs=P(("groups", "tensor"), "delta"),
        check_vma=False,
    )
```

```python
import functools

import jax
import jax.numpy as jnp
from jax import lax
from jax.experimental import pallas as pl
from jax.experimental.pallas import tpu as pltpu
from jax.sharding import PartitionSpec as P

CAP = 128
CHUNKS = (2, 2)
PARTS = 2
SHORT = 120e9
VMEM = 56 * 1024 * 1024
BF = jnp.bfloat16
F32 = jnp.float32


def cost(flops, moved):
    return pl.CostEstimate(flops=int(flops), bytes_accessed=int(moved), transcendentals=0)


def whole(shape):
    zeros = (0,) * len(shape)
    return pl.BlockSpec(shape, lambda *_: zeros)


def pack_body(owners, per_owner, kinds, stride, capacity, col_tiles, scal, x, sl, ss, send, keep, code, table):
    tile = 256
    rows, held = x.shape
    here = held // tile
    me = scal[0]
    height = table.shape[0]
    at_row = lax.broadcasted_iota(jnp.int32, (height, 128), 0)
    at_lane = lax.broadcasted_iota(jnp.int32, (height, 128), 1)
    known = jnp.zeros((height, 128), jnp.int32)
    for s in range(owners * per_owner):
        back = (s // per_owner - me + owners) % owners
        for j in range(kinds):
            place = scal[1 + owners + (back * per_owner + s % per_owner) * stride + j]
            known = jnp.where((at_row == s) & (at_lane == j), place // col_tiles, known)
            known = jnp.where((at_row == s) & (at_lane == 64 + j), place % col_tiles, known)
    table[...] = known.astype(F32).astype(BF)
    owner_l = sl[...] // per_owner
    first = lax.broadcasted_iota(jnp.int32, (rows, rows), 0)
    second = lax.broadcasted_iota(jnp.int32, (rows, rows), 1)
    ahead = ((ss[...] // per_owner) == owner_l) & (first < second)
    pos = jnp.sum(jnp.where(ahead, 1, 0), axis=0, keepdims=True)
    code[...] = sl[...] * capacity + pos
    target = pos
    for o in range(owners):
        target = target + jnp.where(owner_l == o, scal[1 + o] * capacity, 0)
    hot = lax.broadcasted_iota(jnp.int32, (owners * capacity, rows), 0) == target
    hot = jnp.where(hot, 1.0, 0.0).astype(BF)
    lanes = lax.broadcasted_iota(jnp.int32, (rows, height), 1)
    slot_hot = jnp.where(ss[...] == lanes, 1.0, 0.0).astype(BF)
    block = jnp.dot(slot_hot, table[...], preferred_element_type=F32)
    block = block - (me * here).astype(F32)
    for j in range(kinds):
        at = block[:, j : j + 1]
        picked = jnp.zeros((rows, tile), BF)
        for b in range(here):
            picked = jnp.where(at == float(b), x[:, b * tile : (b + 1) * tile], picked)
        found = jnp.dot(hot, picked, preferred_element_type=F32).astype(BF)
        send[:, j * tile : (j + 1) * tile] = found[: send.shape[0]]
        keep[:, j * tile : (j + 1) * tile] = found[send.shape[0] :]


def pack(scal, x, sl, ss, owners, per_owner, kinds, stride, col_tiles):
    rows = x.shape[0]
    width = kinds * 256
    height = -(-owners * per_owner // 128) * 128
    return pl.pallas_call(
        functools.partial(pack_body, owners, per_owner, kinds, stride, CAP, col_tiles),
        grid_spec=pltpu.PrefetchScalarGridSpec(
            num_scalar_prefetch=1,
            grid=(1,),
            in_specs=[whole(x.shape), whole((1, rows)), whole((rows, 1))],
            out_specs=[*[whole((owners // 2 * CAP, width))] * 2, whole((1, rows)), whole((height, 128))],
        ),
        out_shape=[
            *[jax.ShapeDtypeStruct((owners // 2 * CAP, width), BF)] * 2,
            jax.ShapeDtypeStruct((1, rows), jnp.int32),
            jax.ShapeDtypeStruct((height, 128), BF),
        ],
        compiler_params=pltpu.CompilerParams(vmem_limit_bytes=VMEM),
        cost_estimate=cost(SHORT, 4e6),
    )(scal, x, sl, ss)


def product_body(owners, per_owner, per_slot, pieces, scal, x, gt, ut, code, send, keep):
    tile = 256
    capacity = x.shape[0]
    rows = code.shape[1]
    slot_l = code[...] // capacity
    place = lax.broadcasted_iota(jnp.int32, (capacity, rows), 0) == code[...] % capacity
    mine = place & (slot_l // per_owner == scal[0])
    slot = jnp.sum(jnp.where(mine, slot_l % per_owner + 1, 0), axis=1, keepdims=True) - 1
    hot = jnp.where(mine, 1.0, 0.0).astype(BF)
    for kind, tiles in enumerate((gt, ut)):
        for j in range(per_slot):
            at = (kind * per_slot + j) * tile
            source = x[:, at : at + tile]
            total = jnp.zeros((capacity, tile), F32)
            for s in range(per_owner):
                picked = jnp.where(slot == s, source, jnp.zeros_like(source))
                total = total + jnp.dot(picked, tiles[s, j], preferred_element_type=F32)
            spread = lax.dot_general(
                hot, total.astype(BF), (((0,), (0,)), ((), ())), preferred_element_type=F32
            ).astype(BF)
            for home, offset, size, start in pieces:
                out = send if home < owners // 2 else keep
                out[home % (owners // 2), offset : offset + size, at : at + tile] = spread[start : start + size]


def product(scal, x, gt, ut, code, owners, per_owner, pieces):
    rows = code.shape[1]
    per_slot = gt.shape[1]
    shape = (owners // 2, rows // owners, x.shape[1])
    return pl.pallas_call(
        functools.partial(product_body, owners, per_owner, per_slot, pieces),
        grid_spec=pltpu.PrefetchScalarGridSpec(
            num_scalar_prefetch=1,
            grid=(1,),
            in_specs=[whole(x.shape), whole(gt.shape), whole(ut.shape), whole((1, rows))],
            out_specs=[whole(shape)] * 2,
        ),
        out_shape=[jax.ShapeDtypeStruct(shape, BF)] * 2,
        compiler_params=pltpu.CompilerParams(vmem_limit_bytes=VMEM),
        cost_estimate=cost(SHORT, 4e6),
    )(scal, x, gt, ut, code)


def gate_up_body(pieces, scal, *refs):
    blocks, (wg, wu, send, keep, x) = refs[:pieces], refs[pieces:]
    half = send.shape[1]

    @pl.when(pl.program_id(0) == 0)
    def _():
        each = x.shape[0] // pieces
        for i, block in enumerate(blocks):
            x[i * each : (i + 1) * each] = block[...].reshape(each, x.shape[1])

    for i, w in enumerate((wg, wu)):
        total = jnp.dot(x[...], w[...], preferred_element_type=F32)
        send[i] = total[:half].astype(send.dtype)
        keep[i] = total[half:]


def gate_up(scal, tokens, wg, wu, owners, shift, start, size, part):
    rows, depth = tokens.shape
    width = wg.shape[1] // PARTS
    block = min(1024, width)
    skip = part * (width // block)
    each = size // (owners * shift)
    first = start // (shift * each)
    unit = rows // (sum(CHUNKS) * owners * shift)
    view = tokens.reshape(shift, rows // (shift * unit), unit, depth)
    outs = pl.BlockSpec((2, size // 2, block), lambda i, s: (0, 0, i))
    weights = pl.BlockSpec((depth, block), lambda i, s: (0, skip + i))
    piece = [
        pl.BlockSpec((shift, each // unit, unit, depth), functools.partial(lambda h, i, s: (0, first + s[h], 0, 0), h))
        for h in range(owners)
    ]
    return pl.pallas_call(
        functools.partial(gate_up_body, owners),
        grid_spec=pltpu.PrefetchScalarGridSpec(
            num_scalar_prefetch=1,
            grid=(width // block,),
            in_specs=[*piece, weights, weights],
            out_specs=[outs, outs],
            scratch_shapes=[pltpu.VMEM((size, depth), BF)],
        ),
        out_shape=[jax.ShapeDtypeStruct((2, size // 2, width), F32)] * 2,
        compiler_params=pltpu.CompilerParams(vmem_limit_bytes=VMEM),
        cost_estimate=cost(4 * size * depth * width, 4 * depth * width),
    )(scal, *[view] * owners, wg, wu)


def total_body(order, keep, core, *refs):
    total = keep[0] + core[0]
    for ref in refs[:-1]:
        total = total + ref[...]
    refs[-1][...] = total


def total_of(order, keep, core, came):
    shape = came[0].shape
    last = keep.shape[0] - 1
    own = pl.BlockSpec((1, *shape), lambda i, s: (last, 0, 0))
    return pl.pallas_call(
        total_body,
        grid_spec=pltpu.PrefetchScalarGridSpec(
            num_scalar_prefetch=1,
            grid=(1,),
            in_specs=[own, own, *[whole(shape)] * len(came)],
            out_specs=whole(shape),
        ),
        out_shape=jax.ShapeDtypeStruct(shape, BF),
        compiler_params=pltpu.CompilerParams(vmem_limit_bytes=VMEM),
        cost_estimate=cost(SHORT, 1e6),
    )(order, keep, core, *came)


def activate_body(per_slot, start, each, row, parts, skip, keep, core, *refs):
    gots, (delta, slot, table, out) = refs[:parts], refs[parts:]
    tile = 256
    step = pl.program_id(0)
    across = out.shape[1] // tile
    lanes = lax.broadcasted_iota(jnp.int32, (each, table.shape[0]), 1)
    hot = jnp.where(slot[row : row + each] == lanes, 1.0, 0.0).astype(BF)
    where = jnp.dot(hot, table[...], preferred_element_type=F32) - (skip + step * across).astype(F32)
    at = [where[:, 64 + k : 65 + k] for k in range(2 * per_slot)]
    adds = [
        delta[start : start + each, k * tile : (k + 1) * tile].astype(F32) for k in range(2 * per_slot)
    ]
    for b in range(across):
        cols = slice(b * tile, (b + 1) * tile)
        sums = []
        for kind in range(2):
            got = gots[0][kind, :, cols] if parts == 1 else gots[kind][0, :, cols]
            total = keep[kind, :, cols] + core[kind, :, cols] + got.astype(F32)
            for k in range(kind * per_slot, (kind + 1) * per_slot):
                total = total + jnp.where(at[k] == float(b), adds[k], 0.0)
            sums.append(total)
        gate, up = sums
        out[:, cols] = (gate / (1.0 + jnp.exp(-gate)) * up).astype(BF)


def activate(keep, core, gots, delta, slot, table, per_slot, start, row, skip, flops):
    each, width = gots[0].shape[1:]
    last = keep.shape[1] // each - 1
    block = min(2048, width)
    own = pl.BlockSpec((2, each, block), lambda i: (0, last, i))
    taken = [pl.BlockSpec((g.shape[0], each, block), lambda i: (0, 0, i)) for g in gots]
    return pl.pallas_call(
        functools.partial(activate_body, per_slot, start, each, row, len(gots), skip),
        grid=(width // block,),
        in_specs=[own, own, *taken, whole(delta.shape), whole(slot.shape), whole(table.shape)],
        out_specs=pl.BlockSpec((each, block), lambda i: (0, i)),
        out_shape=jax.ShapeDtypeStruct((each, width), BF),
        compiler_params=pltpu.CompilerParams(vmem_limit_bytes=VMEM),
        cost_estimate=cost(flops, 24 * each * width),
    )(keep, core, *gots, delta, slot, table)


def hits_body(width_tiles, here, across, plan, counts, owners, per_owner, per_slot, scal, listed):
    stride = 3 * per_slot
    patterns = scal.shape[0] - owners * per_owner * stride
    last = listed.shape[1] - 1
    steps = here // across
    me = scal[0]
    for r, (base, run) in enumerate(plan):
        for at in range(steps):
            listed[r * steps + at, last] = 0

        def one(i, carry):
            local = i // per_slot
            which = scal[base + local // run] + local % run
            back = (which // per_owner - me + owners) % owners
            row = back * per_owner + which % per_owner
            place = scal[patterns + row * stride + 2 * per_slot + i % per_slot]
            block = place % width_tiles - me * here

            @pl.when((block >= 0) & (block < here))
            def _():
                entry = r * steps + block // across
                n = listed[entry, last]
                listed[entry, 4 * n] = i
                listed[entry, 4 * n + 1] = which
                listed[entry, 4 * n + 2] = place // width_tiles
                listed[entry, 4 * n + 3] = block % across
                listed[entry, last] = n + 1

            return carry

        lax.fori_loop(0, counts[r], one, 0)


def hits(scal, width, width_tiles, plan, counts, owners, per_owner, per_slot):
    block = min(512, width)
    shape = (len(plan) * (width // block), 4 * max(counts) + 1)
    return pl.pallas_call(
        functools.partial(
            hits_body, width_tiles, width // 256, block // 256, plan, counts, owners, per_owner, per_slot
        ),
        in_specs=[pl.BlockSpec(memory_space=pltpu.SMEM)],
        out_specs=pl.BlockSpec(memory_space=pltpu.SMEM),
        out_shape=jax.ShapeDtypeStruct(shape, jnp.int32),
        cost_estimate=cost(1e6, 1e4),
    )(scal)


def down_body(arrays, steps, skip, start, listed, *refs):
    fars, nears, (w, *refs) = refs[:PARTS], refs[PARTS : 2 * PARTS], refs[2 * PARTS :]
    sources, (slot, out, hid, *refs) = refs[:arrays], refs[arrays:]
    tiles, arrived = refs[:arrays], refs[arrays]
    tile = 256
    step = pl.program_id(0)
    half, wide = fars[0].shape
    last = listed.shape[1] - 1
    copies = [pltpu.make_async_copy(sources[r], tiles[r], arrived.at[r]) for r in range(arrays)]

    @pl.when(step == 0)
    def _():
        for copy in copies:
            copy.start()
        for p in range(PARTS):
            hid[:half, p * wide : (p + 1) * wide] = fars[p][...]
            hid[half:, p * wide : (p + 1) * wide] = nears[p][...]

    out[...] = jnp.dot(hid[...], w[...], preferred_element_type=F32)

    @pl.when(step == 0)
    def _():
        for copy in copies:
            copy.wait()

    for r in range(arrays):
        entry = r * steps + skip + step

        def add(n, carry):
            i = listed[entry, 4 * n]
            col = pl.multiple_of(listed[entry, 4 * n + 2] * tile, tile)
            source = hid[:, pl.ds(col, tile)]
            hit = slot[start : start + 2 * half] == listed[entry, 4 * n + 1]
            picked = jnp.where(hit, source, jnp.zeros_like(source))
            cols = pl.ds(pl.multiple_of(listed[entry, 4 * n + 3] * tile, tile), tile)
            out[:, cols] = out[:, cols] + jnp.dot(picked, tiles[r][i], preferred_element_type=F32)
            return carry

        lax.fori_loop(0, listed[entry, last], add, 0)


def down(listed, fars, nears, w, tiles, slot, start, parts, part):
    rows, depth = 2 * fars[0].shape[0], w.shape[0]
    block = min(512, w.shape[1])
    steps = w.shape[1] // block
    here = steps // parts
    skip = part * here
    return pl.pallas_call(
        functools.partial(down_body, len(tiles), steps, skip, start),
        grid_spec=pltpu.PrefetchScalarGridSpec(
            num_scalar_prefetch=1,
            grid=(here,),
            in_specs=[
                *[whole(f.shape) for f in (*fars, *nears)],
                pl.BlockSpec((depth, block), lambda i, s: (0, skip + i)),
                *[pl.BlockSpec(memory_space=pl.ANY)] * len(tiles),
                whole(slot.shape),
            ],
            out_specs=pl.BlockSpec((rows, block), lambda i, s: (0, i)),
            scratch_shapes=[
                pltpu.VMEM((rows, depth), BF),
                *[pltpu.VMEM(t.shape, BF) for t in tiles],
                pltpu.SemaphoreType.DMA((len(tiles),)),
            ],
        ),
        out_shape=jax.ShapeDtypeStruct((rows, here * block), F32),
        compiler_params=pltpu.CompilerParams(vmem_limit_bytes=VMEM),
        cost_estimate=cost(1e9, 1e6),
    )(listed, *fars, *nears, w, *tiles, slot)


def shards(
    tokens,
    gate_weight,
    up_weight,
    down_weight,
    gate_tiles,
    up_tiles,
    down_tiles,
    gate_pattern,
    up_pattern,
    down_pattern,
    row_variant,
    variant_slot,
):
    owners = lax.axis_size("delta")
    shift = lax.axis_size("tensor")
    groups = lax.axis_size("groups")
    me = lax.axis_index("delta")
    here_t = lax.axis_index("tensor")
    my_core, my_y = me % 2, me // 2
    ys = owners // 2
    per_owner, per_slot = gate_pattern.shape
    slots = owners * per_owner
    rows, shard_width = tokens.shape
    width = gate_weight.shape[1]
    col_tiles = width // 256
    width_tiles = shard_width * owners // 256
    unit = rows // sum(CHUNKS)
    sizes = [unit * c for c in CHUNKS]

    def core_swap(x):
        return lax.ppermute(x, "delta", [(i, i ^ 1) for i in range(owners)])

    def y_move(x, k):
        return lax.ppermute(x, "delta", [(i, (i + 2 * k) % owners) for i in range(owners)])

    order_y = [(my_y + k) % ys for k in range(1, ys)] + [my_y]
    homes = jnp.stack([y * 2 + c for c in (1 - my_core, my_core) for y in order_y]).astype(jnp.int32)

    row_ids = []
    offset = 0
    for size in sizes:
        each = size // (owners * shift)
        ids = (
            jnp.arange(shift, dtype=jnp.int32)[None, :, None] * (rows // shift)
            + offset
            + homes[:, None, None] * each
            + jnp.arange(each, dtype=jnp.int32)[None, None, :]
        )
        row_ids.append(ids.reshape(-1))
        offset += owners * each
    row_of = jnp.concatenate(row_ids)

    hit = row_variant[:, None] == jnp.arange(variant_slot.shape[0], dtype=jnp.int32)[None, :]
    slot_rows = jnp.sum(jnp.where(hit, variant_slot[None, :], 0), axis=1)

    def after(x, *earlier):
        return lax.optimization_barrier((x, *earlier))[0]

    kinds = 2 * per_slot
    own = jnp.concatenate([gate_pattern, up_pattern, down_pattern], axis=1)
    seen = [own] + [
        lax.ppermute(own, "delta", [(i, (i - k) % owners) for i in range(owners)]) for k in range(1, owners)
    ]
    patterns = jnp.concatenate([s.reshape(-1) for s in seen])
    at_home = jnp.stack(
        [((d // 2) - my_y - 1) % ys + ys * jnp.where(d % 2 == my_core, 1, 0) for d in range(owners)]
    ).astype(jnp.int32)
    scal = jnp.concatenate([me.astype(jnp.int32)[None], at_home, patterns])

    flat_tiles = down_tiles.reshape(-1, 256, 256)
    if groups == 2 and per_owner % 2 == 0:
        part = per_owner // 2
        mine_g = lax.axis_index("groups")
        piece = lax.dynamic_slice_in_dim(flat_tiles, mine_g * part * per_slot, part * per_slot, 0)
        halves = [mine_g * part, (1 - mine_g) * part]
    else:
        part, piece, halves = per_owner, flat_tiles, [0]
    from_y = jnp.concatenate([y_move(piece, -k) for k in range(1, ys)])
    tiles = [from_y]
    firsts, plan = [], []
    for core in (my_core, 1 - my_core):
        for first in halves:
            plan.append((1 + len(firsts), part))
            firsts.extend((y * 2 + core) * per_owner + first for y in order_y[:-1])
        plan.append((1 + len(firsts), per_owner))
        firsts.append((my_y * 2 + core) * per_owner)
    plan = tuple(plan)
    down_scal = jnp.concatenate([jnp.stack([me] + firsts).astype(jnp.int32), patterns])

    starts = [sum(sizes[:i]) for i in range(len(sizes))]
    inners = [s // owners for s in starts]
    kept, cores, sends, gots = {}, {}, {}, {}

    def multiply(u, *earlier):
        i, part = u
        send, kept[u] = gate_up(
            after(homes, *earlier), tokens, gate_weight, up_weight, owners, shift, starts[i], sizes[i], part
        )
        cores[u] = core_swap(send)

    def exchange(u, *earlier):
        each = sizes[u[0]] // owners
        sends[u], got = [], None
        own = after(kept[u], *earlier)
        for k in range(1, ys):
            rows_k = slice((k - 1) * each, k * each)
            sends[u].append((own[:, rows_k] + cores[u][:, rows_k]).astype(BF))
            moved = y_move(sends[u][-1], k)
            if ys > 2:
                moved = moved.astype(F32)
            got = moved if got is None else got + moved
        gots[u] = [got]

    def finish(keep, core, pieces, *earlier):
        return total_of(
            after(homes, *earlier), keep, core, [y_move(pieces[k - 1], k) for k in range(1, ys)]
        )

    ahead, second, third, fourth = (0, 0), (0, 1), (1, 0), (1, 1)
    multiply(ahead)
    send, keep, code, table = pack(
        after(scal, kept[ahead], from_y),
        tokens,
        slot_rows[None, :],
        slot_rows[:, None],
        owners,
        per_owner,
        kinds,
        3 * per_slot,
        col_tiles,
    )
    exchange(ahead)
    packed = keep.reshape(ys, CAP, -1)
    packed_core = core_swap(send.reshape(ys, CAP, -1))
    packed_sends = [packed[k - 1] + packed_core[k - 1] for k in range(1, ys)]
    multiply(second, *sends[ahead], *packed_sends)
    code = after(code, kept[second])
    if len(halves) == 2:
        tiles.append(lax.ppermute(after(from_y, kept[second]), "groups", [(0, 1), (1, 0)]))
    code_q = jnp.sum(
        jnp.where(row_of[:, None] == jnp.arange(rows, dtype=jnp.int32)[None, :], code, 0), axis=1
    )
    slot_q = code_q // CAP
    pieces = tuple(
        (home, inner, size // owners, start + home * (size // owners))
        for size, start, inner in zip(sizes, starts, inners)
        for home in range(owners)
    )
    ss_q = slot_q[:, None]

    features = finish(packed, packed_core, packed_sends, kept[second], *gots[ahead])
    exchange(second, features)
    send, spread = product(
        after(scal, *sends[second]),
        features,
        gate_tiles,
        up_tiles,
        code_q[None, :],
        owners,
        per_owner,
        pieces,
    )
    spread_core = core_swap(send)
    spread_sends = [spread[k - 1] + spread_core[k - 1] for k in range(1, ys)]
    multiply(third, *sends[second], *spread_sends)
    home_delta = finish(spread, spread_core, spread_sends, kept[third])
    exchange(third, home_delta)

    def finish_hidden(u, flops, *earlier):
        i, part = u
        each = sizes[i] // owners
        hid = activate(
            kept[u],
            cores[u],
            gots[u],
            home_delta,
            ss_q,
            after(table, *earlier),
            per_slot,
            inners[i],
            starts[i] + sizes[i] - each,
            part * (col_tiles // PARTS),
            flops,
        )
        return hid, [y_move(hid, -k) for k in range(1, ys)]

    def join(hid, moved, *earlier):
        return jnp.concatenate([after(m, *earlier) for m in moved] + [hid])

    def multiply_down(i, chips, fars, parts, part, *earlier):
        return down(
            after(listed, *earlier), fars, chips, down_weight, all_tiles, ss_q, starts[i], parts, part
        )

    def finish_down(i, outs, sent=None):
        out = outs[0] if len(outs) == 1 else jnp.concatenate(outs, axis=1)
        blocks = out.reshape(owners, shift, sizes[i] // (owners * shift), shard_width).transpose(1, 0, 2, 3)
        total = lax.dynamic_index_in_dim(blocks, here_t, 0, keepdims=False)
        came = []
        for k in range(1, shift):
            gone = lax.dynamic_index_in_dim(blocks, (here_t + k) % shift, 0, keepdims=False).astype(BF)
            if sent is not None:
                gone = after(gone, sent[k - 1])
            came.append(lax.ppermute(gone, "tensor", [(j, (j + k) % shift) for j in range(shift)]))
            total = total + came[-1].astype(F32)
        return came, total.astype(BF)

    hid_a, moved_a = finish_hidden(ahead, 1e9, *sends[third])
    near_tiles = [*tiles, flat_tiles]
    all_tiles = near_tiles + [core_swap(after(t, hid_a)) for t in near_tiles]
    listed = hits(
        after(down_scal, kept[second]),
        shard_width,
        width_tiles,
        plan,
        [t.shape[0] for t in all_tiles],
        owners,
        per_owner,
        per_slot,
    )
    multiply(fourth, *sends[third], hid_a, *gots[second])
    hid_b, moved_b = finish_hidden(second, SHORT, kept[fourth], *gots[third], *moved_a, *tiles[1:])
    hid_c, moved_c = finish_hidden(third, 1e9, hid_b)
    exchange(fourth, hid_c, *moved_b)
    first = [join(hid_a, moved_a, hid_b), join(hid_b, moved_b, hid_c)]
    fars = [core_swap(c) for c in first]
    split = 2 if shard_width >= 1024 else 1
    outs = [multiply_down(0, first, fars, split, 0, *sends[fourth])]
    hid_d, moved_d = finish_hidden(fourth, 1e9, outs[0])
    if split == 2:
        outs.append(multiply_down(0, first, fars, split, 1, hid_d))
    came, total = finish_down(0, outs)
    result = [total]
    last = [join(hid_c, moved_c, hid_d), join(hid_d, moved_d, *outs[1:])]
    outs = [multiply_down(1, last, [core_swap(c) for c in last], 1, 0, *outs)]
    came, total = finish_down(1, outs, came)
    result.append(total)

    placed = [jnp.take(r, at_home, axis=0).reshape(-1, shard_width) for r in result]
    return jnp.concatenate(placed, axis=0)


def solution(mesh):
    return jax.shard_map(
        shards,
        mesh=mesh,
        in_specs=(
            P("groups", "delta"),
            P("delta", "tensor"),
            P("delta", "tensor"),
            P("tensor", "delta"),
            P("delta", "tensor", None, None),
            P("delta", "tensor", None, None),
            P("delta", "tensor", None, None),
            P("delta", "tensor"),
            P("delta", "tensor"),
            P("delta", "tensor"),
            P("groups"),
            P("groups"),
        ),
        out_specs=P(("groups", "tensor"), "delta"),
        check_vma=False,
    )
```

```python
import functools

import jax
import jax.numpy as jnp
from jax import lax
from jax.experimental import pallas as pl
from jax.experimental.pallas import tpu as pltpu
from jax.sharding import PartitionSpec as P

CAP = 128
CHUNKS = (2, 2)
PARTS = 2
SHORT = 120e9
VMEM = 56 * 1024 * 1024
BF = jnp.bfloat16
F32 = jnp.float32


def cost(flops, moved):
    return pl.CostEstimate(flops=int(flops), bytes_accessed=int(moved), transcendentals=0)


def whole(shape):
    zeros = (0,) * len(shape)
    return pl.BlockSpec(shape, lambda *_: zeros)


def pack_body(owners, per_owner, kinds, stride, capacity, col_tiles, scal, x, sl, ss, send, keep, code, table):
    tile = 256
    rows, held = x.shape
    here = held // tile
    me = scal[0]
    height = table.shape[0]
    at_row = lax.broadcasted_iota(jnp.int32, (height, 128), 0)
    at_lane = lax.broadcasted_iota(jnp.int32, (height, 128), 1)
    known = jnp.zeros((height, 128), jnp.int32)
    for s in range(owners * per_owner):
        back = (s // per_owner - me + owners) % owners
        for j in range(kinds):
            place = scal[1 + owners + (back * per_owner + s % per_owner) * stride + j]
            known = jnp.where((at_row == s) & (at_lane == j), place // col_tiles, known)
            known = jnp.where((at_row == s) & (at_lane == 64 + j), place % col_tiles, known)
    table[...] = known.astype(F32).astype(BF)
    owner_l = sl[...] // per_owner
    first = lax.broadcasted_iota(jnp.int32, (rows, rows), 0)
    second = lax.broadcasted_iota(jnp.int32, (rows, rows), 1)
    ahead = ((ss[...] // per_owner) == owner_l) & (first < second)
    pos = jnp.sum(jnp.where(ahead, 1, 0), axis=0, keepdims=True)
    code[...] = sl[...] * capacity + pos
    target = pos
    for o in range(owners):
        target = target + jnp.where(owner_l == o, scal[1 + o] * capacity, 0)
    hot = lax.broadcasted_iota(jnp.int32, (owners * capacity, rows), 0) == target
    hot = jnp.where(hot, 1.0, 0.0).astype(BF)
    lanes = lax.broadcasted_iota(jnp.int32, (rows, height), 1)
    slot_hot = jnp.where(ss[...] == lanes, 1.0, 0.0).astype(BF)
    block = jnp.dot(slot_hot, table[...], preferred_element_type=F32)
    block = block - (me * here).astype(F32)
    for j in range(kinds):
        at = block[:, j : j + 1]
        picked = jnp.zeros((rows, tile), BF)
        for b in range(here):
            picked = jnp.where(at == float(b), x[:, b * tile : (b + 1) * tile], picked)
        found = jnp.dot(hot, picked, preferred_element_type=F32).astype(BF)
        send[:, j * tile : (j + 1) * tile] = found[: send.shape[0]]
        keep[:, j * tile : (j + 1) * tile] = found[send.shape[0] :]


def pack(scal, x, sl, ss, owners, per_owner, kinds, stride, col_tiles):
    rows = x.shape[0]
    width = kinds * 256
    height = -(-owners * per_owner // 128) * 128
    return pl.pallas_call(
        functools.partial(pack_body, owners, per_owner, kinds, stride, CAP, col_tiles),
        grid_spec=pltpu.PrefetchScalarGridSpec(
            num_scalar_prefetch=1,
            grid=(1,),
            in_specs=[whole(x.shape), whole((1, rows)), whole((rows, 1))],
            out_specs=[*[whole((owners // 2 * CAP, width))] * 2, whole((1, rows)), whole((height, 128))],
        ),
        out_shape=[
            *[jax.ShapeDtypeStruct((owners // 2 * CAP, width), BF)] * 2,
            jax.ShapeDtypeStruct((1, rows), jnp.int32),
            jax.ShapeDtypeStruct((height, 128), BF),
        ],
        compiler_params=pltpu.CompilerParams(vmem_limit_bytes=VMEM),
        cost_estimate=cost(SHORT, 4e6),
    )(scal, x, sl, ss)


def product_body(owners, per_owner, per_slot, pieces, scal, x, gt, ut, code, send, keep):
    tile = 256
    capacity = x.shape[0]
    rows = code.shape[1]
    slot_l = code[...] // capacity
    place = lax.broadcasted_iota(jnp.int32, (capacity, rows), 0) == code[...] % capacity
    mine = place & (slot_l // per_owner == scal[0])
    slot = jnp.sum(jnp.where(mine, slot_l % per_owner + 1, 0), axis=1, keepdims=True) - 1
    hot = jnp.where(mine, 1.0, 0.0).astype(BF)
    for kind, tiles in enumerate((gt, ut)):
        for j in range(per_slot):
            at = (kind * per_slot + j) * tile
            source = x[:, at : at + tile]
            total = jnp.zeros((capacity, tile), F32)
            for s in range(per_owner):
                picked = jnp.where(slot == s, source, jnp.zeros_like(source))
                total = total + jnp.dot(picked, tiles[s, j], preferred_element_type=F32)
            spread = lax.dot_general(
                hot, total.astype(BF), (((0,), (0,)), ((), ())), preferred_element_type=F32
            ).astype(BF)
            for home, offset, size, start in pieces:
                out = send if home < owners // 2 else keep
                out[home % (owners // 2), offset : offset + size, at : at + tile] = spread[start : start + size]


def product(scal, x, gt, ut, code, owners, per_owner, pieces):
    rows = code.shape[1]
    per_slot = gt.shape[1]
    shape = (owners // 2, rows // owners, x.shape[1])
    return pl.pallas_call(
        functools.partial(product_body, owners, per_owner, per_slot, pieces),
        grid_spec=pltpu.PrefetchScalarGridSpec(
            num_scalar_prefetch=1,
            grid=(1,),
            in_specs=[whole(x.shape), whole(gt.shape), whole(ut.shape), whole((1, rows))],
            out_specs=[whole(shape)] * 2,
        ),
        out_shape=[jax.ShapeDtypeStruct(shape, BF)] * 2,
        compiler_params=pltpu.CompilerParams(vmem_limit_bytes=VMEM),
        cost_estimate=cost(SHORT, 4e6),
    )(scal, x, gt, ut, code)


def gate_up_body(pieces, scal, *refs):
    blocks, (wg, wu, send, keep, x) = refs[:pieces], refs[pieces:]
    half = send.shape[1]

    @pl.when(pl.program_id(0) == 0)
    def _():
        each = x.shape[0] // pieces
        for i, block in enumerate(blocks):
            x[i * each : (i + 1) * each] = block[...].reshape(each, x.shape[1])

    for i, w in enumerate((wg, wu)):
        total = jnp.dot(x[...], w[...], preferred_element_type=F32)
        send[i] = total[:half].astype(send.dtype)
        keep[i] = total[half:]


def gate_up(scal, tokens, wg, wu, owners, shift, start, size, part):
    rows, depth = tokens.shape
    width = wg.shape[1] // PARTS
    block = min(1024, width)
    skip = part * (width // block)
    each = size // (owners * shift)
    first = start // (shift * each)
    unit = rows // (sum(CHUNKS) * owners * shift)
    view = tokens.reshape(shift, rows // (shift * unit), unit, depth)
    outs = pl.BlockSpec((2, size // 2, block), lambda i, s: (0, 0, i))
    weights = pl.BlockSpec((depth, block), lambda i, s: (0, skip + i))
    piece = [
        pl.BlockSpec((shift, each // unit, unit, depth), functools.partial(lambda h, i, s: (0, first + s[h], 0, 0), h))
        for h in range(owners)
    ]
    return pl.pallas_call(
        functools.partial(gate_up_body, owners),
        grid_spec=pltpu.PrefetchScalarGridSpec(
            num_scalar_prefetch=1,
            grid=(width // block,),
            in_specs=[*piece, weights, weights],
            out_specs=[outs, outs],
            scratch_shapes=[pltpu.VMEM((size, depth), BF)],
        ),
        out_shape=[jax.ShapeDtypeStruct((2, size // 2, width), F32)] * 2,
        compiler_params=pltpu.CompilerParams(vmem_limit_bytes=VMEM),
        cost_estimate=cost(4 * size * depth * width, 4 * depth * width),
    )(scal, *[view] * owners, wg, wu)


def total_body(order, keep, core, *refs):
    total = keep[0] + core[0]
    for ref in refs[:-1]:
        total = total + ref[...]
    refs[-1][...] = total


def total_of(order, keep, core, came):
    shape = came[0].shape
    last = keep.shape[0] - 1
    own = pl.BlockSpec((1, *shape), lambda i, s: (last, 0, 0))
    return pl.pallas_call(
        total_body,
        grid_spec=pltpu.PrefetchScalarGridSpec(
            num_scalar_prefetch=1,
            grid=(1,),
            in_specs=[own, own, *[whole(shape)] * len(came)],
            out_specs=whole(shape),
        ),
        out_shape=jax.ShapeDtypeStruct(shape, BF),
        compiler_params=pltpu.CompilerParams(vmem_limit_bytes=VMEM),
        cost_estimate=cost(SHORT, 1e6),
    )(order, keep, core, *came)


def activate_body(per_slot, start, each, row, parts, skip, keep, core, *refs):
    gots, (delta, slot, table, out) = refs[:parts], refs[parts:]
    tile = 256
    step = pl.program_id(0)
    across = out.shape[1] // tile
    lanes = lax.broadcasted_iota(jnp.int32, (each, table.shape[0]), 1)
    hot = jnp.where(slot[row : row + each] == lanes, 1.0, 0.0).astype(BF)
    where = jnp.dot(hot, table[...], preferred_element_type=F32) - (skip + step * across).astype(F32)
    at = [where[:, 64 + k : 65 + k] for k in range(2 * per_slot)]
    adds = [
        delta[start : start + each, k * tile : (k + 1) * tile].astype(F32) for k in range(2 * per_slot)
    ]
    for b in range(across):
        cols = slice(b * tile, (b + 1) * tile)
        sums = []
        for kind in range(2):
            got = gots[0][kind, :, cols] if parts == 1 else gots[kind][0, :, cols]
            total = keep[kind, :, cols] + core[kind, :, cols] + got.astype(F32)
            for k in range(kind * per_slot, (kind + 1) * per_slot):
                total = total + jnp.where(at[k] == float(b), adds[k], 0.0)
            sums.append(total)
        gate, up = sums
        out[:, cols] = (gate / (1.0 + jnp.exp(-gate)) * up).astype(BF)


def activate(keep, core, gots, delta, slot, table, per_slot, start, row, skip, flops):
    each, width = gots[0].shape[1:]
    last = keep.shape[1] // each - 1
    block = min(2048, width)
    own = pl.BlockSpec((2, each, block), lambda i: (0, last, i))
    taken = [pl.BlockSpec((g.shape[0], each, block), lambda i: (0, 0, i)) for g in gots]
    return pl.pallas_call(
        functools.partial(activate_body, per_slot, start, each, row, len(gots), skip),
        grid=(width // block,),
        in_specs=[own, own, *taken, whole(delta.shape), whole(slot.shape), whole(table.shape)],
        out_specs=pl.BlockSpec((each, block), lambda i: (0, i)),
        out_shape=jax.ShapeDtypeStruct((each, width), BF),
        compiler_params=pltpu.CompilerParams(vmem_limit_bytes=VMEM),
        cost_estimate=cost(flops, 24 * each * width),
    )(keep, core, *gots, delta, slot, table)


def hits_body(width_tiles, here, across, plan, counts, owners, per_owner, per_slot, scal, listed):
    stride = 3 * per_slot
    patterns = scal.shape[0] - owners * per_owner * stride
    last = listed.shape[1] - 1
    steps = here // across
    me = scal[0]
    for r, (base, run) in enumerate(plan):
        for at in range(steps):
            listed[r * steps + at, last] = 0

        def one(i, carry):
            local = i // per_slot
            which = scal[base + local // run] + local % run
            back = (which // per_owner - me + owners) % owners
            row = back * per_owner + which % per_owner
            place = scal[patterns + row * stride + 2 * per_slot + i % per_slot]
            block = place % width_tiles - me * here

            @pl.when((block >= 0) & (block < here))
            def _():
                entry = r * steps + block // across
                n = listed[entry, last]
                listed[entry, 4 * n] = i
                listed[entry, 4 * n + 1] = which
                listed[entry, 4 * n + 2] = place // width_tiles
                listed[entry, 4 * n + 3] = block % across
                listed[entry, last] = n + 1

            return carry

        lax.fori_loop(0, counts[r], one, 0)


def hits(scal, width, width_tiles, plan, counts, owners, per_owner, per_slot):
    block = min(512, width)
    shape = (len(plan) * (width // block), 4 * max(counts) + 1)
    return pl.pallas_call(
        functools.partial(
            hits_body, width_tiles, width // 256, block // 256, plan, counts, owners, per_owner, per_slot
        ),
        in_specs=[pl.BlockSpec(memory_space=pltpu.SMEM)],
        out_specs=pl.BlockSpec(memory_space=pltpu.SMEM),
        out_shape=jax.ShapeDtypeStruct(shape, jnp.int32),
        cost_estimate=cost(1e6, 1e4),
    )(scal)


def down_body(arrays, steps, start, listed, *refs):
    fars, nears, (w, *refs) = refs[:PARTS], refs[PARTS : 2 * PARTS], refs[2 * PARTS :]
    sources, (slot, out, hid, *refs) = refs[:arrays], refs[arrays:]
    tiles, arrived = refs[:arrays], refs[arrays]
    tile = 256
    step = pl.program_id(0)
    half, wide = fars[0].shape
    last = listed.shape[1] - 1
    copies = [pltpu.make_async_copy(sources[r], tiles[r], arrived.at[r]) for r in range(arrays)]

    @pl.when(step == 0)
    def _():
        for copy in copies:
            copy.start()
        for p in range(PARTS):
            hid[:half, p * wide : (p + 1) * wide] = fars[p][...]
            hid[half:, p * wide : (p + 1) * wide] = nears[p][...]

    out[...] = jnp.dot(hid[...], w[...], preferred_element_type=F32)

    @pl.when(step == 0)
    def _():
        for copy in copies:
            copy.wait()

    for r in range(arrays):
        entry = r * steps + step

        def add(n, carry):
            i = listed[entry, 4 * n]
            col = pl.multiple_of(listed[entry, 4 * n + 2] * tile, tile)
            source = hid[:, pl.ds(col, tile)]
            hit = slot[start : start + 2 * half] == listed[entry, 4 * n + 1]
            picked = jnp.where(hit, source, jnp.zeros_like(source))
            cols = pl.ds(pl.multiple_of(listed[entry, 4 * n + 3] * tile, tile), tile)
            out[:, cols] = out[:, cols] + jnp.dot(picked, tiles[r][i], preferred_element_type=F32)
            return carry

        lax.fori_loop(0, listed[entry, last], add, 0)


def down(listed, fars, nears, w, tiles, slot, start):
    rows, depth = 2 * fars[0].shape[0], w.shape[0]
    block = min(512, w.shape[1])
    steps = w.shape[1] // block
    return pl.pallas_call(
        functools.partial(down_body, len(tiles), steps, start),
        grid_spec=pltpu.PrefetchScalarGridSpec(
            num_scalar_prefetch=1,
            grid=(steps,),
            in_specs=[
                *[whole(f.shape) for f in (*fars, *nears)],
                pl.BlockSpec((depth, block), lambda i, s: (0, i)),
                *[pl.BlockSpec(memory_space=pl.ANY)] * len(tiles),
                whole(slot.shape),
            ],
            out_specs=pl.BlockSpec((rows, block), lambda i, s: (0, i)),
            scratch_shapes=[
                pltpu.VMEM((rows, depth), BF),
                *[pltpu.VMEM(t.shape, BF) for t in tiles],
                pltpu.SemaphoreType.DMA((len(tiles),)),
            ],
        ),
        out_shape=jax.ShapeDtypeStruct((rows, w.shape[1]), F32),
        compiler_params=pltpu.CompilerParams(vmem_limit_bytes=VMEM),
        cost_estimate=cost(1e9, 1e6),
    )(listed, *fars, *nears, w, *tiles, slot)


def shards(
    tokens,
    gate_weight,
    up_weight,
    down_weight,
    gate_tiles,
    up_tiles,
    down_tiles,
    gate_pattern,
    up_pattern,
    down_pattern,
    row_variant,
    variant_slot,
):
    owners = lax.axis_size("delta")
    shift = lax.axis_size("tensor")
    groups = lax.axis_size("groups")
    me = lax.axis_index("delta")
    here_t = lax.axis_index("tensor")
    my_core, my_y = me % 2, me // 2
    ys = owners // 2
    per_owner, per_slot = gate_pattern.shape
    slots = owners * per_owner
    rows, shard_width = tokens.shape
    width = gate_weight.shape[1]
    col_tiles = width // 256
    width_tiles = shard_width * owners // 256
    unit = rows // sum(CHUNKS)
    sizes = [unit * c for c in CHUNKS]

    def core_swap(x):
        return lax.ppermute(x, "delta", [(i, i ^ 1) for i in range(owners)])

    def y_move(x, k):
        return lax.ppermute(x, "delta", [(i, (i + 2 * k) % owners) for i in range(owners)])

    order_y = [(my_y + k) % ys for k in range(1, ys)] + [my_y]
    homes = jnp.stack([y * 2 + c for c in (1 - my_core, my_core) for y in order_y]).astype(jnp.int32)

    row_ids = []
    offset = 0
    for size in sizes:
        each = size // (owners * shift)
        ids = (
            jnp.arange(shift, dtype=jnp.int32)[None, :, None] * (rows // shift)
            + offset
            + homes[:, None, None] * each
            + jnp.arange(each, dtype=jnp.int32)[None, None, :]
        )
        row_ids.append(ids.reshape(-1))
        offset += owners * each
    row_of = jnp.concatenate(row_ids)

    hit = row_variant[:, None] == jnp.arange(variant_slot.shape[0], dtype=jnp.int32)[None, :]
    slot_rows = jnp.sum(jnp.where(hit, variant_slot[None, :], 0), axis=1)

    def after(x, *earlier):
        return lax.optimization_barrier((x, *earlier))[0]

    kinds = 2 * per_slot
    own = jnp.concatenate([gate_pattern, up_pattern, down_pattern], axis=1)
    seen = [own] + [
        lax.ppermute(own, "delta", [(i, (i - k) % owners) for i in range(owners)]) for k in range(1, owners)
    ]
    patterns = jnp.concatenate([s.reshape(-1) for s in seen])
    at_home = jnp.stack(
        [((d // 2) - my_y - 1) % ys + ys * jnp.where(d % 2 == my_core, 1, 0) for d in range(owners)]
    ).astype(jnp.int32)
    scal = jnp.concatenate([me.astype(jnp.int32)[None], at_home, patterns])

    flat_tiles = down_tiles.reshape(-1, 256, 256)
    if groups == 2 and per_owner % 2 == 0:
        part = per_owner // 2
        mine_g = lax.axis_index("groups")
        piece = lax.dynamic_slice_in_dim(flat_tiles, mine_g * part * per_slot, part * per_slot, 0)
        halves = [mine_g * part, (1 - mine_g) * part]
    else:
        part, piece, halves = per_owner, flat_tiles, [0]
    from_y = jnp.concatenate([y_move(piece, -k) for k in range(1, ys)])
    tiles = [from_y]
    firsts, plan = [], []
    for core in (my_core, 1 - my_core):
        for first in halves:
            plan.append((1 + len(firsts), part))
            firsts.extend((y * 2 + core) * per_owner + first for y in order_y[:-1])
        plan.append((1 + len(firsts), per_owner))
        firsts.append((my_y * 2 + core) * per_owner)
    plan = tuple(plan)
    down_scal = jnp.concatenate([jnp.stack([me] + firsts).astype(jnp.int32), patterns])

    starts = [sum(sizes[:i]) for i in range(len(sizes))]
    inners = [s // owners for s in starts]
    kept, cores, sends, gots = {}, {}, {}, {}

    def multiply(u, *earlier):
        i, part = u
        send, kept[u] = gate_up(
            after(homes, *earlier), tokens, gate_weight, up_weight, owners, shift, starts[i], sizes[i], part
        )
        cores[u] = core_swap(send)

    def exchange(u, *earlier):
        each = sizes[u[0]] // owners
        sends[u], got = [], None
        own = after(kept[u], *earlier)
        for k in range(1, ys):
            rows_k = slice((k - 1) * each, k * each)
            sends[u].append((own[:, rows_k] + cores[u][:, rows_k]).astype(BF))
            moved = y_move(sends[u][-1], k)
            if ys > 2:
                moved = moved.astype(F32)
            got = moved if got is None else got + moved
        gots[u] = [got]

    def finish(keep, core, pieces, *earlier):
        return total_of(
            after(homes, *earlier), keep, core, [y_move(pieces[k - 1], k) for k in range(1, ys)]
        )

    ahead, second, third, fourth = (0, 0), (0, 1), (1, 0), (1, 1)
    multiply(ahead)
    send, keep, code, table = pack(
        after(scal, kept[ahead], from_y),
        tokens,
        slot_rows[None, :],
        slot_rows[:, None],
        owners,
        per_owner,
        kinds,
        3 * per_slot,
        col_tiles,
    )
    exchange(ahead)
    packed = keep.reshape(ys, CAP, -1)
    packed_core = core_swap(send.reshape(ys, CAP, -1))
    packed_sends = [packed[k - 1] + packed_core[k - 1] for k in range(1, ys)]
    multiply(second, *sends[ahead], *packed_sends)
    code = after(code, kept[second])
    if len(halves) == 2:
        tiles.append(lax.ppermute(after(from_y, kept[second]), "groups", [(0, 1), (1, 0)]))
    code_q = jnp.sum(
        jnp.where(row_of[:, None] == jnp.arange(rows, dtype=jnp.int32)[None, :], code, 0), axis=1
    )
    slot_q = code_q // CAP
    pieces = tuple(
        (home, inner, size // owners, start + home * (size // owners))
        for size, start, inner in zip(sizes, starts, inners)
        for home in range(owners)
    )
    ss_q = slot_q[:, None]

    counts = [t.shape[0] for t in [*tiles, flat_tiles]] * 2
    listed = hits(
        after(down_scal, kept[second]), shard_width, width_tiles, plan, counts, owners, per_owner, per_slot
    )
    features = finish(packed, packed_core, packed_sends, listed, *gots[ahead])
    exchange(second, features)
    send, spread = product(
        after(scal, *sends[second]),
        features,
        gate_tiles,
        up_tiles,
        code_q[None, :],
        owners,
        per_owner,
        pieces,
    )
    spread_core = core_swap(send)
    spread_sends = [spread[k - 1] + spread_core[k - 1] for k in range(1, ys)]
    multiply(third, *sends[second], *spread_sends)
    far_tiles = {0: core_swap(after(from_y, kept[second])), len(tiles): core_swap(after(flat_tiles, kept[second]))}
    home_delta = finish(spread, spread_core, spread_sends, kept[third], *tiles[1:], *far_tiles.values())
    if len(tiles) == 2:
        far_tiles[1] = core_swap(after(tiles[1], home_delta))
    all_tiles = [*tiles, flat_tiles] + [far_tiles[i] for i in range(len(far_tiles))]
    exchange(third, home_delta)

    def finish_hidden(u, flops, *earlier):
        i, part = u
        each = sizes[i] // owners
        hid = activate(
            kept[u],
            cores[u],
            gots[u],
            home_delta,
            ss_q,
            after(table, *earlier),
            per_slot,
            inners[i],
            starts[i] + sizes[i] - each,
            part * (col_tiles // PARTS),
            flops,
        )
        return hid, [y_move(hid, -k) for k in range(1, ys)]

    def join(hid, moved, *earlier):
        return jnp.concatenate([after(m, *earlier) for m in moved] + [hid])

    def multiply_down(i, chips, *earlier):
        fars = [core_swap(c) for c in chips]
        return down(after(listed, *earlier), fars, chips, down_weight, all_tiles, ss_q, starts[i])

    def finish_down(i, out, sent=None):
        blocks = out.reshape(owners, shift, sizes[i] // (owners * shift), shard_width).transpose(1, 0, 2, 3)
        total = lax.dynamic_index_in_dim(blocks, here_t, 0, keepdims=False)
        came = []
        for k in range(1, shift):
            gone = lax.dynamic_index_in_dim(blocks, (here_t + k) % shift, 0, keepdims=False).astype(BF)
            if sent is not None:
                gone = after(gone, sent[k - 1])
            came.append(lax.ppermute(gone, "tensor", [(j, (j + k) % shift) for j in range(shift)]))
            total = total + came[-1].astype(F32)
        return came, total.astype(BF)

    hid_a, moved_a = finish_hidden(ahead, 1e9, *sends[third])
    multiply(fourth, *sends[third], hid_a, *gots[second])
    hid_b, moved_b = finish_hidden(second, SHORT, kept[fourth], *gots[third], *moved_a, *all_tiles)
    exchange(fourth, hid_b)
    hid_c, moved_c = finish_hidden(third, 1e9, hid_b, *sends[fourth])
    hid_d, moved_d = finish_hidden(fourth, 1e9, hid_c)
    first = [join(hid_a, moved_a, hid_b), join(hid_b, moved_b, *sends[fourth])]
    out = multiply_down(0, first, hid_d)
    came, total = finish_down(0, out)
    result = [total]
    last = [join(hid_c, moved_c, out), join(hid_d, moved_d, out)]
    out = multiply_down(1, last, out)
    came, total = finish_down(1, out, came)
    result.append(total)

    placed = [jnp.take(r, at_home, axis=0).reshape(-1, shard_width) for r in result]
    return jnp.concatenate(placed, axis=0)


def solution(mesh):
    return jax.shard_map(
        shards,
        mesh=mesh,
        in_specs=(
            P("groups", "delta"),
            P("delta", "tensor"),
            P("delta", "tensor"),
            P("tensor", "delta"),
            P("delta", "tensor", None, None),
            P("delta", "tensor", None, None),
            P("delta", "tensor", None, None),
            P("delta", "tensor"),
            P("delta", "tensor"),
            P("delta", "tensor"),
            P("groups"),
            P("groups"),
        ),
        out_specs=P(("groups", "tensor"), "delta"),
        check_vma=False,
    )
```

```python
import functools

import jax
import jax.numpy as jnp
from jax import lax
from jax.experimental import pallas as pl
from jax.experimental.pallas import tpu as pltpu
from jax.sharding import PartitionSpec as P

CAP = 128
CHUNKS = (2, 2)
PARTS = 2
SHORT = 120e9
VMEM = 56 * 1024 * 1024
BF = jnp.bfloat16
F32 = jnp.float32


def cost(flops, moved):
    return pl.CostEstimate(flops=int(flops), bytes_accessed=int(moved), transcendentals=0)


def whole(shape):
    zeros = (0,) * len(shape)
    return pl.BlockSpec(shape, lambda *_: zeros)


def pack_body(owners, per_owner, kinds, stride, capacity, col_tiles, scal, x, sl, ss, send, keep, code, table):
    tile = 256
    rows, held = x.shape
    here = held // tile
    me = scal[0]
    height = table.shape[0]
    at_row = lax.broadcasted_iota(jnp.int32, (height, 128), 0)
    at_lane = lax.broadcasted_iota(jnp.int32, (height, 128), 1)
    known = jnp.zeros((height, 128), jnp.int32)
    for s in range(owners * per_owner):
        back = (s // per_owner - me + owners) % owners
        for j in range(kinds):
            place = scal[1 + owners + (back * per_owner + s % per_owner) * stride + j]
            known = jnp.where((at_row == s) & (at_lane == j), place // col_tiles, known)
            known = jnp.where((at_row == s) & (at_lane == 64 + j), place % col_tiles, known)
    table[...] = known.astype(F32).astype(BF)
    owner_l = sl[...] // per_owner
    first = lax.broadcasted_iota(jnp.int32, (rows, rows), 0)
    second = lax.broadcasted_iota(jnp.int32, (rows, rows), 1)
    ahead = ((ss[...] // per_owner) == owner_l) & (first < second)
    pos = jnp.sum(jnp.where(ahead, 1, 0), axis=0, keepdims=True)
    code[...] = sl[...] * capacity + pos
    target = pos
    for o in range(owners):
        target = target + jnp.where(owner_l == o, scal[1 + o] * capacity, 0)
    hot = lax.broadcasted_iota(jnp.int32, (owners * capacity, rows), 0) == target
    hot = jnp.where(hot, 1.0, 0.0).astype(BF)
    lanes = lax.broadcasted_iota(jnp.int32, (rows, height), 1)
    slot_hot = jnp.where(ss[...] == lanes, 1.0, 0.0).astype(BF)
    block = jnp.dot(slot_hot, table[...], preferred_element_type=F32)
    block = block - (me * here).astype(F32)
    for j in range(kinds):
        at = block[:, j : j + 1]
        picked = jnp.zeros((rows, tile), BF)
        for b in range(here):
            picked = jnp.where(at == float(b), x[:, b * tile : (b + 1) * tile], picked)
        found = jnp.dot(hot, picked, preferred_element_type=F32).astype(BF)
        send[:, j * tile : (j + 1) * tile] = found[: send.shape[0]]
        keep[:, j * tile : (j + 1) * tile] = found[send.shape[0] :]


def pack(scal, x, sl, ss, owners, per_owner, kinds, stride, col_tiles):
    rows = x.shape[0]
    width = kinds * 256
    height = -(-owners * per_owner // 128) * 128
    return pl.pallas_call(
        functools.partial(pack_body, owners, per_owner, kinds, stride, CAP, col_tiles),
        grid_spec=pltpu.PrefetchScalarGridSpec(
            num_scalar_prefetch=1,
            grid=(1,),
            in_specs=[whole(x.shape), whole((1, rows)), whole((rows, 1))],
            out_specs=[*[whole((owners // 2 * CAP, width))] * 2, whole((1, rows)), whole((height, 128))],
        ),
        out_shape=[
            *[jax.ShapeDtypeStruct((owners // 2 * CAP, width), BF)] * 2,
            jax.ShapeDtypeStruct((1, rows), jnp.int32),
            jax.ShapeDtypeStruct((height, 128), BF),
        ],
        compiler_params=pltpu.CompilerParams(vmem_limit_bytes=VMEM),
        cost_estimate=cost(SHORT, 4e6),
    )(scal, x, sl, ss)


def product_body(owners, per_owner, per_slot, pieces, scal, x, gt, ut, code, send, keep):
    tile = 256
    capacity = x.shape[0]
    rows = code.shape[1]
    slot_l = code[...] // capacity
    place = lax.broadcasted_iota(jnp.int32, (capacity, rows), 0) == code[...] % capacity
    mine = place & (slot_l // per_owner == scal[0])
    slot = jnp.sum(jnp.where(mine, slot_l % per_owner + 1, 0), axis=1, keepdims=True) - 1
    hot = jnp.where(mine, 1.0, 0.0).astype(BF)
    for kind, tiles in enumerate((gt, ut)):
        for j in range(per_slot):
            at = (kind * per_slot + j) * tile
            source = x[:, at : at + tile]
            total = jnp.zeros((capacity, tile), F32)
            for s in range(per_owner):
                picked = jnp.where(slot == s, source, jnp.zeros_like(source))
                total = total + jnp.dot(picked, tiles[s, j], preferred_element_type=F32)
            spread = lax.dot_general(
                hot, total.astype(BF), (((0,), (0,)), ((), ())), preferred_element_type=F32
            ).astype(BF)
            for home, offset, size, start in pieces:
                out = send if home < owners // 2 else keep
                out[home % (owners // 2), offset : offset + size, at : at + tile] = spread[start : start + size]


def product(scal, x, gt, ut, code, owners, per_owner, pieces):
    rows = code.shape[1]
    per_slot = gt.shape[1]
    shape = (owners // 2, rows // owners, x.shape[1])
    return pl.pallas_call(
        functools.partial(product_body, owners, per_owner, per_slot, pieces),
        grid_spec=pltpu.PrefetchScalarGridSpec(
            num_scalar_prefetch=1,
            grid=(1,),
            in_specs=[whole(x.shape), whole(gt.shape), whole(ut.shape), whole((1, rows))],
            out_specs=[whole(shape)] * 2,
        ),
        out_shape=[jax.ShapeDtypeStruct(shape, BF)] * 2,
        compiler_params=pltpu.CompilerParams(vmem_limit_bytes=VMEM),
        cost_estimate=cost(SHORT, 4e6),
    )(scal, x, gt, ut, code)


def gate_up_body(pieces, scal, *refs):
    blocks, (wg, wu, send, keep, x) = refs[:pieces], refs[pieces:]
    half = send.shape[1]

    @pl.when(pl.program_id(0) == 0)
    def _():
        each = x.shape[0] // pieces
        for i, block in enumerate(blocks):
            x[i * each : (i + 1) * each] = block[...].reshape(each, x.shape[1])

    for i, w in enumerate((wg, wu)):
        total = jnp.dot(x[...], w[...], preferred_element_type=F32)
        send[i] = total[:half].astype(send.dtype)
        keep[i] = total[half:]


def gate_up(scal, tokens, wg, wu, owners, shift, start, size, part):
    rows, depth = tokens.shape
    width = wg.shape[1] // PARTS
    block = min(1024, width)
    skip = part * (width // block)
    each = size // (owners * shift)
    first = start // (shift * each)
    unit = rows // (sum(CHUNKS) * owners * shift)
    view = tokens.reshape(shift, rows // (shift * unit), unit, depth)
    outs = pl.BlockSpec((2, size // 2, block), lambda i, s: (0, 0, i))
    weights = pl.BlockSpec((depth, block), lambda i, s: (0, skip + i))
    piece = [
        pl.BlockSpec((shift, each // unit, unit, depth), functools.partial(lambda h, i, s: (0, first + s[h], 0, 0), h))
        for h in range(owners)
    ]
    return pl.pallas_call(
        functools.partial(gate_up_body, owners),
        grid_spec=pltpu.PrefetchScalarGridSpec(
            num_scalar_prefetch=1,
            grid=(width // block,),
            in_specs=[*piece, weights, weights],
            out_specs=[outs, outs],
            scratch_shapes=[pltpu.VMEM((size, depth), BF)],
        ),
        out_shape=[jax.ShapeDtypeStruct((2, size // 2, width), F32)] * 2,
        compiler_params=pltpu.CompilerParams(vmem_limit_bytes=VMEM),
        cost_estimate=cost(4 * size * depth * width, 4 * depth * width),
    )(scal, *[view] * owners, wg, wu)


def total_body(order, keep, core, *refs):
    total = keep[0] + core[0]
    for ref in refs[:-1]:
        total = total + ref[...]
    refs[-1][...] = total


def total_of(order, keep, core, came):
    shape = came[0].shape
    last = keep.shape[0] - 1
    own = pl.BlockSpec((1, *shape), lambda i, s: (last, 0, 0))
    return pl.pallas_call(
        total_body,
        grid_spec=pltpu.PrefetchScalarGridSpec(
            num_scalar_prefetch=1,
            grid=(1,),
            in_specs=[own, own, *[whole(shape)] * len(came)],
            out_specs=whole(shape),
        ),
        out_shape=jax.ShapeDtypeStruct(shape, BF),
        compiler_params=pltpu.CompilerParams(vmem_limit_bytes=VMEM),
        cost_estimate=cost(SHORT, 1e6),
    )(order, keep, core, *came)


def activate_body(per_slot, start, each, row, parts, skip, keep, core, *refs):
    gots, (delta, slot, table, out) = refs[:parts], refs[parts:]
    tile = 256
    step = pl.program_id(0)
    across = out.shape[1] // tile
    lanes = lax.broadcasted_iota(jnp.int32, (each, table.shape[0]), 1)
    hot = jnp.where(slot[row : row + each] == lanes, 1.0, 0.0).astype(BF)
    where = jnp.dot(hot, table[...], preferred_element_type=F32) - (skip + step * across).astype(F32)
    at = [where[:, 64 + k : 65 + k] for k in range(2 * per_slot)]
    adds = [
        delta[start : start + each, k * tile : (k + 1) * tile].astype(F32) for k in range(2 * per_slot)
    ]
    for b in range(across):
        cols = slice(b * tile, (b + 1) * tile)
        sums = []
        for kind in range(2):
            got = gots[0][kind, :, cols] if parts == 1 else gots[kind][0, :, cols]
            total = keep[kind, :, cols] + core[kind, :, cols] + got.astype(F32)
            for k in range(kind * per_slot, (kind + 1) * per_slot):
                total = total + jnp.where(at[k] == float(b), adds[k], 0.0)
            sums.append(total)
        gate, up = sums
        out[:, cols] = (gate / (1.0 + jnp.exp(-gate)) * up).astype(BF)


def activate(keep, core, gots, delta, slot, table, per_slot, start, row, skip, flops):
    each, width = gots[0].shape[1:]
    last = keep.shape[1] // each - 1
    block = min(2048, width)
    own = pl.BlockSpec((2, each, block), lambda i: (0, last, i))
    taken = [pl.BlockSpec((g.shape[0], each, block), lambda i: (0, 0, i)) for g in gots]
    return pl.pallas_call(
        functools.partial(activate_body, per_slot, start, each, row, len(gots), skip),
        grid=(width // block,),
        in_specs=[own, own, *taken, whole(delta.shape), whole(slot.shape), whole(table.shape)],
        out_specs=pl.BlockSpec((each, block), lambda i: (0, i)),
        out_shape=jax.ShapeDtypeStruct((each, width), BF),
        compiler_params=pltpu.CompilerParams(vmem_limit_bytes=VMEM),
        cost_estimate=cost(flops, 24 * each * width),
    )(keep, core, *gots, delta, slot, table)


def hits_body(width_tiles, here, across, plan, counts, owners, per_owner, per_slot, scal, listed):
    stride = 3 * per_slot
    patterns = scal.shape[0] - owners * per_owner * stride
    last = listed.shape[1] - 1
    steps = here // across
    me = scal[0]
    for r, (base, run) in enumerate(plan):
        for at in range(steps):
            listed[r * steps + at, last] = 0

        def one(i, carry):
            local = i // per_slot
            which = scal[base + local // run] + local % run
            back = (which // per_owner - me + owners) % owners
            row = back * per_owner + which % per_owner
            place = scal[patterns + row * stride + 2 * per_slot + i % per_slot]
            block = place % width_tiles - me * here

            @pl.when((block >= 0) & (block < here))
            def _():
                entry = r * steps + block // across
                n = listed[entry, last]
                listed[entry, 4 * n] = i
                listed[entry, 4 * n + 1] = which
                listed[entry, 4 * n + 2] = place // width_tiles
                listed[entry, 4 * n + 3] = block % across
                listed[entry, last] = n + 1

            return carry

        lax.fori_loop(0, counts[r], one, 0)


def hits(scal, width, width_tiles, plan, counts, owners, per_owner, per_slot):
    block = min(512, width)
    shape = (len(plan) * (width // block), 4 * max(counts) + 1)
    return pl.pallas_call(
        functools.partial(
            hits_body, width_tiles, width // 256, block // 256, plan, counts, owners, per_owner, per_slot
        ),
        in_specs=[pl.BlockSpec(memory_space=pltpu.SMEM)],
        out_specs=pl.BlockSpec(memory_space=pltpu.SMEM),
        out_shape=jax.ShapeDtypeStruct(shape, jnp.int32),
        cost_estimate=cost(1e6, 1e4),
    )(scal)


def copy_body(x, out):
    out[...] = x[...]


def copied(x):
    return pl.pallas_call(
        copy_body, out_shape=jax.ShapeDtypeStruct(x.shape, x.dtype), cost_estimate=cost(SHORT, 1e3)
    )(x)


def down_body(arrays, steps, start, listed, *refs):
    fars, nears, (w, *refs) = refs[:PARTS], refs[PARTS : 2 * PARTS], refs[2 * PARTS :]
    sources, (slot, out, hid, *refs) = refs[:arrays], refs[arrays:]
    tiles, arrived = refs[:arrays], refs[arrays]
    tile = 256
    step = pl.program_id(0)
    half, wide = fars[0].shape
    last = listed.shape[1] - 1
    copies = [pltpu.make_async_copy(sources[r], tiles[r], arrived.at[r]) for r in range(arrays)]

    @pl.when(step == 0)
    def _():
        for copy in copies:
            copy.start()
        for p in range(PARTS):
            hid[:half, p * wide : (p + 1) * wide] = fars[p][...]
            hid[half:, p * wide : (p + 1) * wide] = nears[p][...]

    out[...] = jnp.dot(hid[...], w[...], preferred_element_type=F32)

    @pl.when(step == 0)
    def _():
        for copy in copies:
            copy.wait()

    for r in range(arrays):
        entry = r * steps + step

        def add(n, carry):
            i = listed[entry, 4 * n]
            col = pl.multiple_of(listed[entry, 4 * n + 2] * tile, tile)
            source = hid[:, pl.ds(col, tile)]
            hit = slot[start : start + 2 * half] == listed[entry, 4 * n + 1]
            picked = jnp.where(hit, source, jnp.zeros_like(source))
            cols = pl.ds(pl.multiple_of(listed[entry, 4 * n + 3] * tile, tile), tile)
            out[:, cols] = out[:, cols] + jnp.dot(picked, tiles[r][i], preferred_element_type=F32)
            return carry

        lax.fori_loop(0, listed[entry, last], add, 0)


def down(listed, fars, nears, w, tiles, slot, start):
    rows, depth = 2 * fars[0].shape[0], w.shape[0]
    block = min(512, w.shape[1])
    steps = w.shape[1] // block
    return pl.pallas_call(
        functools.partial(down_body, len(tiles), steps, start),
        grid_spec=pltpu.PrefetchScalarGridSpec(
            num_scalar_prefetch=1,
            grid=(steps,),
            in_specs=[
                *[whole(f.shape) for f in (*fars, *nears)],
                pl.BlockSpec((depth, block), lambda i, s: (0, i)),
                *[pl.BlockSpec(memory_space=pl.ANY)] * len(tiles),
                whole(slot.shape),
            ],
            out_specs=pl.BlockSpec((rows, block), lambda i, s: (0, i)),
            scratch_shapes=[
                pltpu.VMEM((rows, depth), BF),
                *[pltpu.VMEM(t.shape, BF) for t in tiles],
                pltpu.SemaphoreType.DMA((len(tiles),)),
            ],
        ),
        out_shape=jax.ShapeDtypeStruct((rows, w.shape[1]), F32),
        compiler_params=pltpu.CompilerParams(vmem_limit_bytes=VMEM),
        cost_estimate=cost(1e9, 1e6),
    )(listed, *fars, *nears, w, *tiles, slot)


def shards(
    tokens,
    gate_weight,
    up_weight,
    down_weight,
    gate_tiles,
    up_tiles,
    down_tiles,
    gate_pattern,
    up_pattern,
    down_pattern,
    row_variant,
    variant_slot,
):
    owners = lax.axis_size("delta")
    shift = lax.axis_size("tensor")
    groups = lax.axis_size("groups")
    me = lax.axis_index("delta")
    here_t = lax.axis_index("tensor")
    my_core, my_y = me % 2, me // 2
    ys = owners // 2
    per_owner, per_slot = gate_pattern.shape
    slots = owners * per_owner
    rows, shard_width = tokens.shape
    width = gate_weight.shape[1]
    col_tiles = width // 256
    width_tiles = shard_width * owners // 256
    unit = rows // sum(CHUNKS)
    sizes = [unit * c for c in CHUNKS]

    def core_swap(x):
        return lax.ppermute(x, "delta", [(i, i ^ 1) for i in range(owners)])

    def y_move(x, k):
        return lax.ppermute(x, "delta", [(i, (i + 2 * k) % owners) for i in range(owners)])

    order_y = [(my_y + k) % ys for k in range(1, ys)] + [my_y]
    homes = jnp.stack([y * 2 + c for c in (1 - my_core, my_core) for y in order_y]).astype(jnp.int32)

    row_ids = []
    offset = 0
    for size in sizes:
        each = size // (owners * shift)
        ids = (
            jnp.arange(shift, dtype=jnp.int32)[None, :, None] * (rows // shift)
            + offset
            + homes[:, None, None] * each
            + jnp.arange(each, dtype=jnp.int32)[None, None, :]
        )
        row_ids.append(ids.reshape(-1))
        offset += owners * each
    row_of = jnp.concatenate(row_ids)

    hit = row_variant[:, None] == jnp.arange(variant_slot.shape[0], dtype=jnp.int32)[None, :]
    slot_rows = jnp.sum(jnp.where(hit, variant_slot[None, :], 0), axis=1)

    def after(x, *earlier):
        return lax.optimization_barrier((x, *earlier))[0]

    kinds = 2 * per_slot
    own = jnp.concatenate([gate_pattern, up_pattern, down_pattern], axis=1)
    seen = [own] + [
        lax.ppermute(own, "delta", [(i, (i - k) % owners) for i in range(owners)]) for k in range(1, owners)
    ]
    patterns = jnp.concatenate([s.reshape(-1) for s in seen])
    at_home = jnp.stack(
        [((d // 2) - my_y - 1) % ys + ys * jnp.where(d % 2 == my_core, 1, 0) for d in range(owners)]
    ).astype(jnp.int32)
    scal = jnp.concatenate([me.astype(jnp.int32)[None], at_home, patterns])

    flat_tiles = down_tiles.reshape(-1, 256, 256)
    if groups == 2 and per_owner % 2 == 0:
        part = per_owner // 2
        mine_g = lax.axis_index("groups")
        piece = lax.dynamic_slice_in_dim(flat_tiles, mine_g * part * per_slot, part * per_slot, 0)
        halves = [mine_g * part, (1 - mine_g) * part]
    else:
        part, piece, halves = per_owner, flat_tiles, [0]
    from_y = jnp.concatenate([y_move(piece, -k) for k in range(1, ys)])
    tiles = [from_y]
    firsts, plan = [], []
    for core in (my_core, 1 - my_core):
        for first in halves:
            plan.append((1 + len(firsts), part))
            firsts.extend((y * 2 + core) * per_owner + first for y in order_y[:-1])
        plan.append((1 + len(firsts), per_owner))
        firsts.append((my_y * 2 + core) * per_owner)
    plan = tuple(plan)
    down_scal = jnp.concatenate([jnp.stack([me] + firsts).astype(jnp.int32), patterns])

    starts = [sum(sizes[:i]) for i in range(len(sizes))]
    inners = [s // owners for s in starts]
    kept, cores, sends, gots = {}, {}, {}, {}

    def multiply(u, *earlier):
        i, part = u
        send, kept[u] = gate_up(
            after(homes, *earlier), tokens, gate_weight, up_weight, owners, shift, starts[i], sizes[i], part
        )
        cores[u] = core_swap(send)

    def exchange(u, *earlier):
        each = sizes[u[0]] // owners
        sends[u], got = [], None
        own = after(kept[u], *earlier)
        for k in range(1, ys):
            rows_k = slice((k - 1) * each, k * each)
            sends[u].append((own[:, rows_k] + cores[u][:, rows_k]).astype(BF))
            moved = y_move(sends[u][-1], k)
            if ys > 2:
                moved = moved.astype(F32)
            got = moved if got is None else got + moved
        gots[u] = [got]

    def finish(keep, core, pieces, *earlier):
        return total_of(
            after(homes, *earlier), keep, core, [y_move(pieces[k - 1], k) for k in range(1, ys)]
        )

    ahead, second, third, fourth = (0, 0), (0, 1), (1, 0), (1, 1)
    multiply(ahead)
    send, keep, code, table = pack(
        after(scal, kept[ahead], from_y),
        tokens,
        slot_rows[None, :],
        slot_rows[:, None],
        owners,
        per_owner,
        kinds,
        3 * per_slot,
        col_tiles,
    )
    exchange(ahead)
    packed = keep.reshape(ys, CAP, -1)
    packed_core = core_swap(send.reshape(ys, CAP, -1))
    packed_sends = [packed[k - 1] + packed_core[k - 1] for k in range(1, ys)]
    multiply(second, *sends[ahead], *packed_sends)
    code = after(code, kept[second])
    if len(halves) == 2:
        tiles.append(lax.ppermute(after(from_y, kept[second]), "groups", [(0, 1), (1, 0)]))
    code_q = jnp.sum(
        jnp.where(row_of[:, None] == jnp.arange(rows, dtype=jnp.int32)[None, :], code, 0), axis=1
    )
    slot_q = code_q // CAP
    pieces = tuple(
        (home, inner, size // owners, start + home * (size // owners))
        for size, start, inner in zip(sizes, starts, inners)
        for home in range(owners)
    )
    ss_q = slot_q[:, None]

    counts = [t.shape[0] for t in [*tiles, flat_tiles]] * 2
    listed = hits(
        after(down_scal, kept[second]), shard_width, width_tiles, plan, counts, owners, per_owner, per_slot
    )
    features = finish(packed, packed_core, packed_sends, listed, *gots[ahead])
    exchange(second, features)
    send, spread = product(
        after(scal, *sends[second]),
        features,
        gate_tiles,
        up_tiles,
        code_q[None, :],
        owners,
        per_owner,
        pieces,
    )
    spread_core = core_swap(send)
    spread_sends = [spread[k - 1] + spread_core[k - 1] for k in range(1, ys)]
    multiply(third, *sends[second], *spread_sends)
    far_tiles = {0: core_swap(after(from_y, kept[second])), len(tiles): core_swap(after(flat_tiles, kept[second]))}
    home_delta = finish(spread, spread_core, spread_sends, kept[third], *tiles[1:], *far_tiles.values())
    if len(tiles) == 2:
        far_tiles[1] = core_swap(after(tiles[1], home_delta))
    all_tiles = [*tiles, flat_tiles] + [far_tiles[i] for i in range(len(far_tiles))]
    exchange(third, home_delta)

    def finish_hidden(u, flops, *earlier):
        i, part = u
        each = sizes[i] // owners
        hid = activate(
            kept[u],
            cores[u],
            gots[u],
            home_delta,
            ss_q,
            after(table, *earlier),
            per_slot,
            inners[i],
            starts[i] + sizes[i] - each,
            part * (col_tiles // PARTS),
            flops,
        )
        return hid, [y_move(hid, -k) for k in range(1, ys)]

    def join(hid, moved, *earlier):
        return jnp.concatenate([after(m, *earlier) for m in moved] + [hid])

    def multiply_down(i, chips, listed, *earlier):
        fars = [core_swap(c) for c in chips]
        return down(after(listed, *earlier), fars, chips, down_weight, all_tiles, ss_q, starts[i])

    def finish_down(i, out, sent=None):
        blocks = out.reshape(owners, shift, sizes[i] // (owners * shift), shard_width).transpose(1, 0, 2, 3)
        total = lax.dynamic_index_in_dim(blocks, here_t, 0, keepdims=False)
        came = []
        for k in range(1, shift):
            gone = lax.dynamic_index_in_dim(blocks, (here_t + k) % shift, 0, keepdims=False).astype(BF)
            if sent is not None:
                gone = after(gone, sent[k - 1])
            came.append(lax.ppermute(gone, "tensor", [(j, (j + k) % shift) for j in range(shift)]))
            total = total + came[-1].astype(F32)
        return came, total.astype(BF)

    hid_a, moved_a = finish_hidden(ahead, 1e9, *sends[third])
    multiply(fourth, *sends[third], hid_a, *gots[second])
    hid_b, moved_b = finish_hidden(second, SHORT, kept[fourth], *gots[third], *moved_a, *all_tiles)
    exchange(fourth, hid_b)
    hid_c, moved_c = finish_hidden(third, 1e9, hid_b, *sends[fourth])
    first = [join(hid_a, moved_a, hid_b), join(hid_b, moved_b, *sends[fourth])]
    out = multiply_down(0, first, listed, hid_c)
    came, total = finish_down(0, out)
    result = [total]
    hid_d, moved_d = finish_hidden(fourth, 1e9, out)
    beside = copied(after(listed, hid_d))
    last = [join(hid_c, moved_c, out), join(hid_d, moved_d, beside)]
    beside = copied(after(beside, last[1]))
    out = multiply_down(1, last, beside, out)
    came, total = finish_down(1, out, came)
    result.append(total)

    placed = [jnp.take(r, at_home, axis=0).reshape(-1, shard_width) for r in result]
    return jnp.concatenate(placed, axis=0)


def solution(mesh):
    return jax.shard_map(
        shards,
        mesh=mesh,
        in_specs=(
            P("groups", "delta"),
            P("delta", "tensor"),
            P("delta", "tensor"),
            P("tensor", "delta"),
            P("delta", "tensor", None, None),
            P("delta", "tensor", None, None),
            P("delta", "tensor", None, None),
            P("delta", "tensor"),
            P("delta", "tensor"),
            P("delta", "tensor"),
            P("groups"),
            P("groups"),
        ),
        out_specs=P(("groups", "tensor"), "delta"),
        check_vma=False,
    )
```
